256 devices in a mesh: ctx: 32 (over y, z_hi, core), ch: 8 (over z_lo, x).
Axes of the slice: x: 4, y: 4, z: 8 (z_hi: 4, z_lo: 2; z = z_hi * 2 + z_lo), core: 2. Of those that a mesh axis runs over, the one named last changes fastest.
Arguments:
- tokens: bfloat16 [8192, 4096], P('ctx', 'ch'), may hold values from -6 to 6
- w_in: bfloat16 [4096, 3, 4096], P('ctx', None, 'ch'), may hold values from -0.09375 to 0.09375
- taps: float32 [3, 3, 4096], P(None, None, 'ch'), may hold values from -2 to 2
- modes_gain: float32 [16, 4096], P(None, 'ch'), may hold values from -1.5 to 1.5
- decay: float32 [16, 4096], P(None, 'ch'), may hold values from 0.3 to 300
- skip: float32 [4096], P('ch'), may hold values from -4 to 4
Outputs:
- mixed: bfloat16 [8192, 4096], P('ctx', 'ch')
The draws below stay inside these ranges and needn't reach their ends.
All inputs are finite; a program needn't handle non-finite values.
Results may differ from the reference program's by a relative error of at most 0.0075.
Values may be sent and summed in bfloat16 or wider, within the bound.
No kernel may reach another device: no remote copies, remote signals or barrier semaphores. Data moves between devices by JAX's collectives and lax.ppermute only.
A program may use at most 64 MiB of HBM per device.

```python
import math
import jax
import jax.numpy as jnp

D = 4096
MODES = 16
SEQ = 8192


def level_of(key, extent, shards, smallest, high):
    level, own = 1.0, jax.random.fold_in(key, 6)
    for axis_at, parts in shards:
        heights = jnp.exp(jax.random.uniform(jax.random.fold_in(own, axis_at), (parts,), jnp.float32, smallest / len(shards), high / len(shards)))
        level = level * jnp.repeat(heights, extent[axis_at] // parts).reshape([-1 if axis == axis_at else 1 for axis in range(len(extent))])
    return level


def normal_values(rng, shape, scale, limit, pieces=(), kind=jnp.bfloat16):
    array = scale * jax.random.normal(rng, shape, jnp.float32)
    if pieces:
        array = array * level_of(rng, shape, pieces, -0.22, 0.18)
    return jnp.clip(array, -limit, limit).astype(kind)


def setup_inputs(seed: int = 0) -> dict:
    splits = jax.random.split(jax.random.key(seed), 7)
    return {
        "tokens": normal_values(splits[0], (SEQ, D), 1.0, 6.0, ((0, 32), (1, 8))),
        "w_in": normal_values(splits[1], (D, 3, D), D ** -0.5, 0.09375, ((0, 32), (2, 8))),
        "taps": normal_values(splits[2], (3, 3, D), 0.6, 2.0, ((2, 8),), jnp.float32),
        "modes_gain": normal_values(splits[3], (MODES, D), MODES ** -0.5, 1.5, ((1, 8),), jnp.float32),
        "decay": jnp.clip(jnp.exp(math.log(300.0) - 6.9077552 * jax.random.uniform(splits[4], (MODES, D), jnp.float32) ** level_of(splits[4], (MODES, D), ((1, 8),), -0.2, 0.2)), 0.3, 300.0),
        "skip": normal_values(splits[5], (D,), 1.0, 4.0, ((0, 8),), jnp.float32),
    }


def reference(tokens, w_in, taps, modes_gain, decay, skip):
    length, width = tokens.shape
    flat = w_in.reshape(width, 3 * width)
    projected = jnp.dot(tokens, flat, preferred_element_type=jnp.float32).astype(jnp.bfloat16)
    projected = projected.reshape(length, 3, width)
    extended = jnp.concatenate([jnp.zeros((2, 3, width), jnp.bfloat16), projected], 0).astype(jnp.float32)
    features = taps[0] * extended[2:] + taps[1] * extended[1:-1] + taps[2] * extended[:-2]
    gate_out = features[:, 0]
    product = features[:, 1] * features[:, 2]
    moments = jnp.arange(length, dtype=jnp.int32).astype(jnp.float32)[:, None]
    filt = jnp.zeros((length, width), jnp.float32)
    for index in range(decay.shape[0]):
        rate = decay[index] / length
        filt = filt + modes_gain[index] * jnp.sqrt(2.0 * rate) * jnp.exp(-rate * moments)
    total = 2 * length
    spectrum = jnp.fft.rfft(product, n=total, axis=0) * jnp.fft.rfft(filt, n=total, axis=0)
    conv = jnp.fft.irfft(spectrum, n=total, axis=0)[:length]
    return (gate_out * (conv + skip * product)).astype(jnp.bfloat16)
```

```python
import functools

import jax
import jax.numpy as jnp
from jax import lax
from jax.experimental import pallas as pl
from jax.experimental.pallas import tpu as pltpu
from jax.sharding import Mesh
from jax.sharding import PartitionSpec as P

AXES = ("y", "h", "c", "l", "x")
CTX = ("y", "h", "c")
CH = ("l", "x")
F32 = jnp.float32
BF16 = jnp.bfloat16
HALO = 16
SUB = 8


def shifted(array, axis, step):
    n = lax.axis_size(axis)
    return lax.ppermute(array, axis, [(i, (i + step) % n) for i in range(n)])


def ring(piece, axis):
    half = piece.shape[0] // 2
    behind = shifted(piece, axis, 1)
    ahead = shifted(piece, axis, -1)
    first = shifted(behind[:half], axis, 1)
    second = shifted(ahead[half:], axis, -1)
    return behind, ahead, first, second


def project_kernel(sizes, *refs):
    rows, depth, width, modes, seq = sizes
    pos, tok, *pieces = refs[:22]
    taps, decay = refs[22:24]
    gate, product, inside, state = refs[24:28]
    tokv, wv, acc, tok_sem, w_sem = refs[28:]
    y, h, c = pos[1], pos[2], pos[3]
    k = depth // 16
    half = k // 2
    top = rows + HALO

    copies = []
    for ch in range(8):
        lanes = pl.ds(ch * (depth // 8), depth // 8)
        for core in range(2):
            skip = HALO * core
            at = (core * 8 + ch) * top
            copies.append(
                pltpu.make_async_copy(
                    tok.at[pl.ds(at + skip, top - skip), :],
                    tokv.at[pl.ds(core * top, top - skip), lanes],
                    tok_sem.at[core * 8 + ch],
                )
            )
    groups = [[], [], [], []]
    for kind, dh in enumerate((0, 1, -1, 2)):
        hs = lax.rem(h - dh + 4, 4)
        for number, (dy, skip, n, group) in enumerate(
            ((0, 0, k, 0), (1, 0, k, 1), (-1, 0, k, 2), (2, 0, half, 3), (2, half, half, 3))
        ):
            ys = lax.rem(y - dy + 4, 4)
            at = pl.multiple_of((ys * 4 + hs) * k + skip, half)
            copy = pltpu.make_async_copy(
                pieces[kind * 5 + number], wv.at[pl.ds(at, n), :], w_sem.at[kind * 5 + number]
            )
            groups[group].append(copy)
    for copy in groups[0] + copies + groups[1] + groups[2] + groups[3]:
        copy.start()
    for copy in copies:
        copy.wait()
    for group, dy in enumerate((0, 1, -1, 2)):
        for copy in groups[group]:
            copy.wait()
        at = pl.multiple_of(lax.rem(y - dy + 4, 4) * (4 * k), 4 * k)

        @pl.loop(0, 3)
        def _(j):
            cols = pl.ds(pl.multiple_of(j * width, width), width)
            part = jnp.dot(
                tokv[:, pl.ds(at, 4 * k)], wv[pl.ds(at, 4 * k), cols], preferred_element_type=F32
            )
            for lh in range(width // 128):
                at_lane = j * (width // 128) + lh
                new = part[:, lh * 128 : lh * 128 + 128]
                if group == 0:
                    acc[at_lane] = new
                elif group < 3:
                    acc[at_lane] += new
                else:
                    acc[at_lane] = (acc[at_lane] + new).astype(BF16).astype(F32)

    steps = 2 * rows // SUB
    for lh in range(width // 128):
        mine = pl.ds(pl.multiple_of(c * width + lh * 128, 128), 128)
        lanes = pl.ds(lh * 128, 128)
        weights = [[taps[lag, j : j + 1, mine] for j in range(3)] for lag in range(3)]
        rates = [jnp.broadcast_to(decay[m : m + 1, mine] / seq, (SUB, 128)) for m in range(modes)]
        factors = [jnp.exp(-rate) for rate in rates]

        def read(start):
            return [
                acc[j * (width // 128) + lh, pl.ds(start, SUB, stride=steps), :]
                for j in range(3)
            ]

        def step(t, carry):
            before, last, states = carry
            now = read(HALO + t)
            f = [
                weights[0][j] * now[j] + weights[1][j] * last[j] + weights[2][j] * before[j]
                for j in range(3)
            ]
            p = f[1] * f[2]
            gate[t, :, lanes] = f[0]
            product[t, :, lanes] = p
            return last, now, [a * s + p for a, s in zip(factors, states)]

        zero = jnp.zeros((SUB, 128), F32)
        carry = (read(HALO - 2), read(HALO - 1), [zero] * modes)
        states = lax.fori_loop(0, steps, step, carry, unroll=4)[2]
        line = lax.broadcasted_iota(jnp.int32, (SUB, 128), 0)

        def later(value, by):
            return jnp.where(line >= by, pltpu.roll(value, by, 0), 0.0)

        for m in range(modes):
            s = states[m]
            for by in (1, 2, 4):
                s = s + jnp.exp(-float(steps * by) * rates[m]) * later(s, by)
            inside[m, :, lanes] = later(s, 1)
            state[m : m + 1, lanes] = s[SUB - 1 :]


def local_kernel(sizes, pos, product, gain, decay, skip, local):
    rows, depth, width, modes, seq = sizes
    c = pos[3]
    steps = 2 * rows // SUB
    for lh in range(width // 128):
        mine = pl.ds(pl.multiple_of(c * width + lh * 128, 128), 128)
        lanes = pl.ds(lh * 128, 128)
        rates = [jnp.broadcast_to(decay[m : m + 1, mine] / seq, (SUB, 128)) for m in range(modes)]
        factors = [jnp.exp(-rate) for rate in rates]
        heights = [gain[m : m + 1, mine] * jnp.sqrt(2.0 * rates[m]) for m in range(modes)]
        direct = jnp.broadcast_to(skip[:, mine], (SUB, 128))

        def step(t, states):
            p = product[t, :, lanes]
            states = [a * s + p for a, s in zip(factors, states)]
            parts = [w * s for w, s in zip(heights, states)]
            while len(parts) > 1:
                parts = [a + b for a, b in zip(parts[::2], parts[1::2])]
            local[t, :, lanes] = parts[0] + direct * p
            return states

        lax.fori_loop(0, steps, step, [jnp.zeros((SUB, 128), F32)] * modes, unroll=4)


def finish_kernel(sizes, pos, gate, local, inside, states, gain, decay, out, start, whole):
    rows, depth, width, modes, seq = sizes
    rank, c = pos[0], pos[3]
    steps = 2 * rows // SUB
    length = 2 * rows
    for lh in range(width // 128):
        mine = pl.ds(pl.multiple_of(c * width + lh * 128, 128), 128)
        lanes = pl.ds(lh * 128, 128)
        over = jnp.exp(-float(length) * (decay[:, mine] / seq))
        entering = jnp.zeros((modes, 128), F32)
        for r in range(16):
            entering = jnp.where(r < rank, over * entering + states[r, :, lanes], entering)
        start[:, lanes] = entering
        line = lax.broadcasted_iota(jnp.int32, (SUB, 128), 0).astype(F32) * float(steps)
        factors, waves = [], []
        for m in range(modes):
            rate = jnp.broadcast_to(decay[m : m + 1, mine] / seq, (SUB, 128))
            factors.append(jnp.exp(-rate))
            height = gain[m : m + 1, mine] * jnp.sqrt(2.0 * rate)
            waves.append(height * (inside[m, :, lanes] + jnp.exp(-rate * line) * start[m : m + 1, lanes]))

        def step(t, waves):
            waves = [a * z for a, z in zip(factors, waves)]
            parts = waves
            while len(parts) > 1:
                parts = [a + b for a, b in zip(parts[::2], parts[1::2])]
            whole[lh, pl.ds(t, SUB, stride=steps), :] = gate[t, :, lanes] * (local[t, :, lanes] + parts[0])
            return waves

        lax.fori_loop(0, steps, step, waves, unroll=4)
        for part in range(2):
            out[part, :, lanes] = whole[lh, part * rows : part * rows + rows, :].astype(BF16)


def body(tokens, w_in, taps, modes_gain, decay, skip):
    rows = tokens.shape[0]
    group = w_in.shape[2]
    width = group // 2
    k = w_in.shape[0]
    modes = decay.shape[0]
    depth = tokens.shape[1] * 8
    seq = rows * 32
    sizes = (rows, depth, width, modes, seq)
    y, h, c = (lax.axis_index(a) for a in CTX)
    pos = jnp.stack([y * 4 + h, y, h, c]).astype(jnp.int32)

    with jax.named_scope("token_gather"):
        tail = lax.ppermute(tokens[rows - HALO :], CTX, [(i, i + 1) for i in range(1, 31, 2)])
        tok = lax.all_gather(jnp.concatenate([tail, tokens], 0), ("c", *CH), axis=0, tiled=True)

    with jax.named_scope("weight_gather"):
        halves = w_in.reshape(k, 3, 2, width).transpose(2, 0, 1, 3).reshape(2, k, 3 * width)
        own = lax.all_to_all(halves, "c", 0, 0, tiled=True).reshape(2 * k, 3 * width)
        behind, ahead, first, second = ring(own, "h")
        opposite = jnp.concatenate([first, second], 0)
        pieces = []
        for piece in (own, behind, ahead, opposite):
            pieces += [piece, *ring(piece, "y")]

    vmem = pl.BlockSpec(memory_space=pltpu.VMEM)
    smem = pl.BlockSpec(memory_space=pltpu.SMEM)
    anywhere = pl.BlockSpec(memory_space=pl.ANY)
    block = (2 * rows // SUB, SUB, width)
    full = jax.ShapeDtypeStruct(block, F32)
    params = pltpu.CompilerParams(vmem_limit_bytes=40 * 2**20)
    gate, product, inside, state = pl.pallas_call(
        functools.partial(project_kernel, sizes),
        out_shape=(
            full,
            full,
            jax.ShapeDtypeStruct((modes, SUB, width), F32),
            jax.ShapeDtypeStruct((modes, width), F32),
        ),
        in_specs=[smem] + [anywhere] * 21 + [vmem] * 2,
        out_specs=(vmem,) * 4,
        scratch_shapes=[
            pltpu.VMEM((2 * rows + HALO, depth), BF16),
            pltpu.VMEM((depth, 3 * width), BF16),
            pltpu.VMEM((3 * width // 128, 2 * rows + HALO, 128), F32),
            pltpu.SemaphoreType.DMA((16,)),
            pltpu.SemaphoreType.DMA((20,)),
        ],
        compiler_params=params,
        name="project",
    )(pos, tok, *pieces, taps, decay)

    with jax.named_scope("state_exchange"):
        states = lax.all_to_all(
            jnp.broadcast_to(state, (16, *state.shape)), ("y", "h"), 0, 0, tiled=True
        )
    local = pl.pallas_call(
        functools.partial(local_kernel, sizes),
        out_shape=full,
        in_specs=[smem] + [vmem] * 4,
        out_specs=vmem,
        compiler_params=params,
        cost_estimate=pl.CostEstimate(flops=20_000_000, bytes_accessed=1_000_000, transcendentals=0),
        name="local",
    )(pos, product, modes_gain, decay, skip.reshape(1, group))
    out = pl.pallas_call(
        functools.partial(finish_kernel, sizes),
        out_shape=jax.ShapeDtypeStruct((2, rows, width), BF16),
        in_specs=[smem] + [vmem] * 6,
        out_specs=vmem,
        scratch_shapes=[pltpu.VMEM((modes, width), F32), pltpu.VMEM((width // 128, 2 * rows, 128), F32)],
        compiler_params=params,
        name="finish",
    )(pos, gate, local, inside, states, modes_gain, decay)
    with jax.named_scope("result_swap"):
        both = lax.all_to_all(out, "c", 0, 0, tiled=True)
        return both.transpose(1, 0, 2).reshape(rows, group)


def solution(mesh):
    split = Mesh(mesh.devices.reshape(4, 4, 2, 2, 4), AXES)
    return jax.shard_map(
        body,
        mesh=split,
        in_specs=(
            P(CTX, CH),
            P(CTX, None, CH),
            P(None, None, CH),
            P(None, CH),
            P(None, CH),
            P(CH),
        ),
        out_specs=P(CTX, CH),
        check_vma=False,
    )
```

```python
import functools

import jax
import jax.numpy as jnp
from jax import lax
from jax.experimental import pallas as pl
from jax.experimental.pallas import tpu as pltpu
from jax.sharding import Mesh
from jax.sharding import PartitionSpec as P

AXES = ("y", "h", "c", "l", "x")
CTX = ("y", "h", "c")
CH = ("l", "x")
F32 = jnp.float32
BF16 = jnp.bfloat16
HALO = 16
SUB = 8


def shifted(array, axis, step):
    n = lax.axis_size(axis)
    return lax.ppermute(array, axis, [(i, (i + step) % n) for i in range(n)])


def both_ways(piece, axis):
    return shifted(piece, axis, 1), shifted(piece, axis, -1)


def onward(behind, ahead, axis):
    half = behind.shape[0] // 2
    return shifted(behind[:half], axis, 1), shifted(ahead[half:], axis, -1)


def place(sizes, pos, dy, dh):
    rows, depth, width, modes, seq = sizes
    k = depth // 16
    ys, hs = lax.rem(pos[1] - dy + 4, 4), lax.rem(pos[2] - dh + 4, 4)
    return pl.multiple_of((ys * 4 + hs) * k, k)


def project_kernel(sizes, *refs):
    rows, depth, width, modes, seq = sizes
    pos, tok, halo, *pieces = refs[:16]
    acc, tokv, wv, tok_sem, w_sem = refs[16:]
    k = depth // 16
    half = k // 2
    top = rows + HALO

    copies = []
    for ch in range(8):
        lanes = pl.ds(ch * (depth // 8), depth // 8)
        copies.append((halo.at[pl.ds(ch * HALO, HALO), :], tokv.at[pl.ds(0, HALO), lanes]))
        for core in range(2):
            at = (core * 8 + ch) * rows
            copies.append(
                (tok.at[pl.ds(at, rows), :], tokv.at[pl.ds(HALO + core * rows, rows), lanes])
            )
    copies = [pltpu.make_async_copy(a, b, tok_sem.at[i]) for i, (a, b) in enumerate(copies)]
    lie = {}
    parts = iter(pieces)
    for dy in (0, 1, -1):
        for run in (((0, 0, k),), ((1, 0, k), (-1, 0, k)), ((2, 0, k),)):
            piece, at = next(parts), 0
            for dh, skip, n in run:
                lie.setdefault(dy, []).append((piece, at, dh, skip, n))
                at += n
    for run in (((0, 0, half),), ((0, half, half),), ((1, 0, k),), ((-1, 0, k),)):
        for dh, skip, n in run:
            lie.setdefault(2, []).append((next(parts), 0, dh, skip, n))
    groups, number = {}, 0
    for dy, list_ in lie.items():
        for piece, at, dh, skip, n in list_:
            to = pl.multiple_of(place(sizes, pos, dy, dh) + skip, half)
            copy = pltpu.make_async_copy(
                piece.at[pl.ds(at, n), :], wv.at[pl.ds(to, n), :], w_sem.at[number]
            )
            groups.setdefault(dy, []).append(copy)
            number += 1
    for copy in groups[0] + copies + groups[1] + groups[-1] + groups[2]:
        copy.start()
    for copy in copies:
        copy.wait()

    def add(at, n, first=False):
        @pl.loop(0, 3)
        def _(j):
            cols = pl.ds(pl.multiple_of(j * width, width), width)
            part = jnp.dot(tokv[:, pl.ds(at, n)], wv[pl.ds(at, n), cols], preferred_element_type=F32)
            for lh in range(width // 128):
                chunk = j * (width // 128) + lh
                new = part[:, lh * 128 : lh * 128 + 128]
                if first:
                    acc[chunk] = new
                else:
                    acc[chunk] += new

    for dy in (0, 1, -1):
        for copy in groups[dy]:
            copy.wait()
        at = pl.multiple_of(lax.rem(pos[1] - dy + 4, 4) * (4 * k), 4 * k)
        add(at, 4 * k, dy == 0)
    for copy in groups[2]:
        copy.wait()
    for dh in (0, 1, -1):
        add(place(sizes, pos, 2, dh), k)


def state_kernel(sizes, *refs):
    rows, depth, width, modes, seq = sizes
    pos, tok, halo, first, second, sums, taps, decay = refs[:8]
    gate, product, inside, state = refs[8:12]
    tokv, wv, acc, sem = refs[12:]
    c = pos[3]
    k = depth // 16
    half = k // 2
    at = place(sizes, pos, 2, 2)
    ch = lax.div(at, depth // 8)
    lanes = pl.ds(pl.multiple_of(lax.rem(at, depth // 8), k), k)
    copies = [
        (halo.at[pl.ds(pl.multiple_of(ch * HALO, HALO), HALO), lanes], tokv.at[pl.ds(0, HALO), :]),
        (first, wv.at[pl.ds(0, half), :]),
        (second, wv.at[pl.ds(half, half), :]),
    ]
    for core in range(2):
        from_ = pl.multiple_of((core * 8 + ch) * rows, rows)
        copies.append(
            (tok.at[pl.ds(from_, rows), lanes], tokv.at[pl.ds(HALO + core * rows, rows), :])
        )
    copies = [pltpu.make_async_copy(a, b, sem.at[i]) for i, (a, b) in enumerate(copies)]
    for copy in copies:
        copy.start()
    for copy in copies:
        copy.wait()

    @pl.loop(0, 3)
    def _(j):
        cols = pl.ds(pl.multiple_of(j * width, width), width)
        part = jnp.dot(tokv[...], wv[:, cols], preferred_element_type=F32)
        for lh in range(width // 128):
            chunk = j * (width // 128) + lh
            new = part[:, lh * 128 : lh * 128 + 128]
            acc[chunk] = (sums[chunk] + new).astype(BF16).astype(F32)

    steps = 2 * rows // SUB
    for lh in range(width // 128):
        mine = pl.ds(pl.multiple_of(c * width + lh * 128, 128), 128)
        lanes = pl.ds(lh * 128, 128)
        weights = [[taps[lag, j : j + 1, mine] for j in range(3)] for lag in range(3)]
        rates = [jnp.broadcast_to(decay[m : m + 1, mine] / seq, (SUB, 128)) for m in range(modes)]
        factors = [jnp.exp(-rate) for rate in rates]

        def read(start):
            return [
                acc[j * (width // 128) + lh, pl.ds(start, SUB, stride=steps), :]
                for j in range(3)
            ]

        def step(t, carry):
            before, last, states = carry
            now = read(HALO + t)
            f = [
                weights[0][j] * now[j] + weights[1][j] * last[j] + weights[2][j] * before[j]
                for j in range(3)
            ]
            p = f[1] * f[2]
            gate[t, :, lanes] = f[0]
            product[t, :, lanes] = p
            return last, now, [a * s + p for a, s in zip(factors, states)]

        zero = jnp.zeros((SUB, 128), F32)
        carry = (read(HALO - 2), read(HALO - 1), [zero] * modes)
        states = lax.fori_loop(0, steps, step, carry, unroll=4)[2]
        line = lax.broadcasted_iota(jnp.int32, (SUB, 128), 0)

        def later(value, by):
            return jnp.where(line >= by, pltpu.roll(value, by, 0), 0.0)

        for m in range(modes):
            s = states[m]
            for by in (1, 2, 4):
                s = s + jnp.exp(-float(steps * by) * rates[m]) * later(s, by)
            inside[m, :, lanes] = later(s, 1)
            state[m : m + 1, lanes] = s[SUB - 1 :]


def local_kernel(sizes, pos, product, gain, decay, skip, local):
    rows, depth, width, modes, seq = sizes
    c = pos[3]
    steps = 2 * rows // SUB
    for lh in range(width // 128):
        mine = pl.ds(pl.multiple_of(c * width + lh * 128, 128), 128)
        lanes = pl.ds(lh * 128, 128)
        rates = [jnp.broadcast_to(decay[m : m + 1, mine] / seq, (SUB, 128)) for m in range(modes)]
        factors = [jnp.exp(-rate) for rate in rates]
        heights = [gain[m : m + 1, mine] * jnp.sqrt(2.0 * rates[m]) for m in range(modes)]
        direct = jnp.broadcast_to(skip[:, mine], (SUB, 128))

        def step(t, states):
            p = product[t, :, lanes]
            states = [a * s + p for a, s in zip(factors, states)]
            parts = [w * s for w, s in zip(heights, states)]
            while len(parts) > 1:
                parts = [a + b for a, b in zip(parts[::2], parts[1::2])]
            local[t, :, lanes] = parts[0] + direct * p
            return states

        lax.fori_loop(0, steps, step, [jnp.zeros((SUB, 128), F32)] * modes, unroll=4)


def finish_kernel(sizes, pos, gate, local, inside, states, gain, decay, out, start, whole):
    rows, depth, width, modes, seq = sizes
    rank, c = pos[0], pos[3]
    steps = 2 * rows // SUB
    length = 2 * rows
    for lh in range(width // 128):
        mine = pl.ds(pl.multiple_of(c * width + lh * 128, 128), 128)
        lanes = pl.ds(lh * 128, 128)
        over = jnp.exp(-float(length) * (decay[:, mine] / seq))
        entering = jnp.zeros((modes, 128), F32)
        for r in range(16):
            entering = jnp.where(r < rank, over * entering + states[r, :, lanes], entering)
        start[:, lanes] = entering
        line = lax.broadcasted_iota(jnp.int32, (SUB, 128), 0).astype(F32) * float(steps)
        factors, waves = [], []
        for m in range(modes):
            rate = jnp.broadcast_to(decay[m : m + 1, mine] / seq, (SUB, 128))
            factors.append(jnp.exp(-rate))
            height = gain[m : m + 1, mine] * jnp.sqrt(2.0 * rate)
            waves.append(height * (inside[m, :, lanes] + jnp.exp(-rate * line) * start[m : m + 1, lanes]))

        def step(t, waves):
            waves = [a * z for a, z in zip(factors, waves)]
            parts = waves
            while len(parts) > 1:
                parts = [a + b for a, b in zip(parts[::2], parts[1::2])]
            whole[lh, pl.ds(t, SUB, stride=steps), :] = gate[t, :, lanes] * (local[t, :, lanes] + parts[0])
            return waves

        lax.fori_loop(0, steps, step, waves, unroll=4)
        for part in range(2):
            out[part, :, lanes] = whole[lh, part * rows : part * rows + rows, :].astype(BF16)


def body(tokens, w_in, taps, modes_gain, decay, skip):
    rows = tokens.shape[0]
    group = w_in.shape[2]
    width = group // 2
    k = w_in.shape[0]
    modes = decay.shape[0]
    depth = tokens.shape[1] * 8
    seq = rows * 32
    sizes = (rows, depth, width, modes, seq)
    y, h, c = (lax.axis_index(a) for a in CTX)
    pos = jnp.stack([y * 4 + h, y, h, c]).astype(jnp.int32)

    tie = lax.optimization_barrier
    with jax.named_scope("token_gather"):
        tok = lax.all_gather(tokens, ("c", *CH), axis=0, tiled=True)
        tail = tok.reshape(2, 8, rows, group)[1, :, rows - HALO :].reshape(8 * HALO, group)
        halo = lax.ppermute(tail, ("y", "h"), [(i, i + 1) for i in range(15)])

    with jax.named_scope("weight_gather"):
        halves = w_in.reshape(k, 3, 2, width).transpose(2, 0, 1, 3).reshape(2, k, 3 * width)
        own = lax.all_to_all(halves, "c", 0, 0, tiled=True).reshape(2 * k, 3 * width)
        beside, far = both_ways(own, "h"), both_ways(own, "y")
        beside, far = tie((beside, far))
        pair = jnp.concatenate(beside, 0)
        far_pair, farther = both_ways(pair, "y"), onward(*far, "y")
        opposite = onward(*beside, "h")
        far_pair, farther, opposite = tie((far_pair, farther, opposite))
        opposite = jnp.concatenate(opposite, 0)
        far_opposite, farther_pair = both_ways(opposite, "y"), onward(*far_pair, "y")
        far_opposite, farther_pair = tie((far_opposite, farther_pair))
        last = onward(*far_opposite, "y")
        pieces = [own, pair, opposite]
        for side in range(2):
            pieces += [far[side], far_pair[side], far_opposite[side]]
        pieces += [*farther, *farther_pair]

    vmem = pl.BlockSpec(memory_space=pltpu.VMEM)
    smem = pl.BlockSpec(memory_space=pltpu.SMEM)
    hbm = pl.BlockSpec(memory_space=pltpu.HBM)
    block = (2 * rows // SUB, SUB, width)
    full = jax.ShapeDtypeStruct(block, F32)
    lines = 2 * rows + HALO
    chunks = (3 * width // 128, lines, 128)
    sums = pl.pallas_call(
        functools.partial(project_kernel, sizes),
        out_shape=jax.ShapeDtypeStruct(chunks, F32),
        in_specs=[smem] + [hbm] * 15,
        out_specs=vmem,
        scratch_shapes=[
            pltpu.VMEM((lines, depth), BF16),
            pltpu.VMEM((depth, 3 * width), BF16),
            pltpu.SemaphoreType.DMA((24,)),
            pltpu.SemaphoreType.DMA((16,)),
        ],
        compiler_params=pltpu.CompilerParams(vmem_limit_bytes=20 * 2**20),
        cost_estimate=pl.CostEstimate(
            flops=2 * lines * depth * 3 * width, bytes_accessed=12_000_000, transcendentals=0
        ),
        name="project",
    )(pos, tok, halo, *pieces)
    params = pltpu.CompilerParams(vmem_limit_bytes=12 * 2**20)
    gate, product, inside, state = pl.pallas_call(
        functools.partial(state_kernel, sizes),
        out_shape=(
            full,
            full,
            jax.ShapeDtypeStruct((modes, SUB, width), F32),
            jax.ShapeDtypeStruct((modes, width), F32),
        ),
        in_specs=[smem] + [hbm] * 4 + [vmem] * 3,
        out_specs=(vmem,) * 4,
        scratch_shapes=[
            pltpu.VMEM((lines, depth // 16), BF16),
            pltpu.VMEM((depth // 16, 3 * width), BF16),
            pltpu.VMEM(chunks, F32),
            pltpu.SemaphoreType.DMA((5,)),
        ],
        compiler_params=params,
        name="states",
    )(pos, tok, halo, *last, sums, taps, decay)

    with jax.named_scope("state_exchange"):
        states = lax.all_to_all(
            jnp.broadcast_to(state, (16, *state.shape)), ("y", "h"), 0, 0, tiled=True
        )
    local = pl.pallas_call(
        functools.partial(local_kernel, sizes),
        out_shape=full,
        in_specs=[smem] + [vmem] * 4,
        out_specs=vmem,
        compiler_params=params,
        cost_estimate=pl.CostEstimate(flops=20_000_000, bytes_accessed=1_000_000, transcendentals=0),
        name="local",
    )(pos, product, modes_gain, decay, skip.reshape(1, group))
    out = pl.pallas_call(
        functools.partial(finish_kernel, sizes),
        out_shape=jax.ShapeDtypeStruct((2, rows, width), BF16),
        in_specs=[smem] + [vmem] * 6,
        out_specs=vmem,
        scratch_shapes=[pltpu.VMEM((modes, width), F32), pltpu.VMEM((width // 128, 2 * rows, 128), F32)],
        compiler_params=params,
        name="finish",
    )(pos, gate, local, inside, states, modes_gain, decay)
    with jax.named_scope("result_swap"):
        both = lax.all_to_all(out, "c", 0, 0, tiled=True)
        return both.transpose(1, 0, 2).reshape(rows, group)


def solution(mesh):
    split = Mesh(mesh.devices.reshape(4, 4, 2, 2, 4), AXES)
    return jax.shard_map(
        body,
        mesh=split,
        in_specs=(
            P(CTX, CH),
            P(CTX, None, CH),
            P(None, None, CH),
            P(None, CH),
            P(None, CH),
            P(CH),
        ),
        out_specs=P(CTX, CH),
        check_vma=False,
    )
```

```python
import functools

import jax
import jax.numpy as jnp
from jax import lax
from jax.experimental import pallas as pl
from jax.experimental.pallas import tpu as pltpu
from jax.sharding import Mesh
from jax.sharding import PartitionSpec as P

AXES = ("y", "h", "c", "l", "x")
CTX = ("y", "h", "c")
CH = ("l", "x")
F32 = jnp.float32
BF16 = jnp.bfloat16
HALO = 16
SUB = 8


def shifted(array, axis, step):
    n = lax.axis_size(axis)
    return lax.ppermute(array, axis, [(i, (i + step) % n) for i in range(n)])


def both_ways(piece, axis):
    return shifted(piece, axis, 1), shifted(piece, axis, -1)


def onward(behind, ahead, axis):
    half = behind.shape[0] // 2
    return shifted(behind[:half], axis, 1), shifted(ahead[half:], axis, -1)


def place(sizes, pos, dy, dh):
    rows, depth, width, modes, seq = sizes
    k = depth // 16
    ys, hs = lax.rem(pos[1] - dy + 4, 4), lax.rem(pos[2] - dh + 4, 4)
    return pl.multiple_of((ys * 4 + hs) * k, k)


def project_kernel(sizes, *refs):
    rows, depth, width, modes, seq = sizes
    pos, tok, halo, *pieces = refs[:16]
    acc, tokv, wv, tok_sem, w_sem = refs[16:]
    k = depth // 16
    half = k // 2
    top = rows + HALO

    copies = []
    for ch in range(8):
        lanes = pl.ds((ch % 2 * 4 + ch // 2) * (depth // 8), depth // 8)
        copies.append((halo.at[pl.ds(ch * HALO, HALO), :], tokv.at[pl.ds(0, HALO), lanes]))
        for core in range(2):
            at = (core * 8 + ch) * rows
            copies.append(
                (tok.at[pl.ds(at, rows), :], tokv.at[pl.ds(HALO + core * rows, rows), lanes])
            )
    copies = [pltpu.make_async_copy(a, b, tok_sem.at[i]) for i, (a, b) in enumerate(copies)]
    lie = {}
    parts = iter(pieces)
    for dy in (0, 1, -1):
        for run in (((0, 0, k),), ((1, 0, k), (-1, 0, k)), ((2, 0, k),)):
            piece, at = next(parts), 0
            for dh, skip, n in run:
                lie.setdefault(dy, []).append((piece, at, dh, skip, n))
                at += n
    for run in (((0, 0, half),), ((0, half, half),), ((1, 0, k),), ((-1, 0, k),)):
        for dh, skip, n in run:
            lie.setdefault(2, []).append((next(parts), 0, dh, skip, n))
    groups, number = {}, 0
    for dy, list_ in lie.items():
        for piece, at, dh, skip, n in list_:
            to = pl.multiple_of(place(sizes, pos, dy, dh) + skip, half)
            copy = pltpu.make_async_copy(
                piece.at[pl.ds(at, n), :], wv.at[pl.ds(to, n), :], w_sem.at[number]
            )
            groups.setdefault(dy, []).append(copy)
            number += 1
    for copy in groups[0] + copies + groups[1] + groups[-1] + groups[2]:
        copy.start()
    for copy in copies:
        copy.wait()

    def add(at, n, first=False):
        @pl.loop(0, 3)
        def _(j):
            cols = pl.ds(pl.multiple_of(j * width, width), width)
            part = jnp.dot(tokv[:, pl.ds(at, n)], wv[pl.ds(at, n), cols], preferred_element_type=F32)
            for lh in range(width // 128):
                chunk = j * (width // 128) + lh
                new = part[:, lh * 128 : lh * 128 + 128]
                if first:
                    acc[chunk] = new
                else:
                    acc[chunk] += new

    for dy in (0, 1, -1):
        for copy in groups[dy]:
            copy.wait()
        at = pl.multiple_of(lax.rem(pos[1] - dy + 4, 4) * (4 * k), 4 * k)
        add(at, 4 * k, dy == 0)
    for copy in groups[2]:
        copy.wait()
    for dh in (0, 1, -1):
        add(place(sizes, pos, 2, dh), k)


def state_kernel(sizes, *refs):
    rows, depth, width, modes, seq = sizes
    pos, tok, halo, first, second, sums, taps, decay = refs[:8]
    gate, product, inside, state = refs[8:12]
    tokv, wv, acc, sem = refs[12:]
    c = pos[3]
    k = depth // 16
    half = k // 2
    at = place(sizes, pos, 2, 2)
    ch = lax.div(at, depth // 8)
    ch = lax.rem(ch, 4) * 2 + lax.div(ch, 4)
    lanes = pl.ds(pl.multiple_of(lax.rem(at, depth // 8), k), k)
    copies = [
        (halo.at[pl.ds(pl.multiple_of(ch * HALO, HALO), HALO), lanes], tokv.at[pl.ds(0, HALO), :]),
        (first, wv.at[pl.ds(0, half), :]),
        (second, wv.at[pl.ds(half, half), :]),
    ]
    for core in range(2):
        from_ = pl.multiple_of((core * 8 + ch) * rows, rows)
        copies.append(
            (tok.at[pl.ds(from_, rows), lanes], tokv.at[pl.ds(HALO + core * rows, rows), :])
        )
    copies = [pltpu.make_async_copy(a, b, sem.at[i]) for i, (a, b) in enumerate(copies)]
    for copy in copies:
        copy.start()
    for copy in copies:
        copy.wait()

    @pl.loop(0, 3)
    def _(j):
        cols = pl.ds(pl.multiple_of(j * width, width), width)
        part = jnp.dot(tokv[...], wv[:, cols], preferred_element_type=F32)
        for lh in range(width // 128):
            chunk = j * (width // 128) + lh
            new = part[:, lh * 128 : lh * 128 + 128]
            acc[chunk] = (sums[chunk] + new).astype(BF16).astype(F32)

    steps = 2 * rows // SUB
    for lh in range(width // 128):
        mine = pl.ds(pl.multiple_of(c * width + lh * 128, 128), 128)
        lanes = pl.ds(lh * 128, 128)
        weights = [[taps[lag, j : j + 1, mine] for j in range(3)] for lag in range(3)]
        rates = [jnp.broadcast_to(decay[m : m + 1, mine] / seq, (SUB, 128)) for m in range(modes)]
        factors = [jnp.exp(-rate) for rate in rates]

        def read(start):
            return [
                acc[j * (width // 128) + lh, pl.ds(start, SUB, stride=steps), :]
                for j in range(3)
            ]

        def step(t, carry):
            before, last, states = carry
            now = read(HALO + t)
            f = [
                weights[0][j] * now[j] + weights[1][j] * last[j] + weights[2][j] * before[j]
                for j in range(3)
            ]
            p = f[1] * f[2]
            gate[t, :, lanes] = f[0]
            product[t, :, lanes] = p
            return last, now, [a * s + p for a, s in zip(factors, states)]

        zero = jnp.zeros((SUB, 128), F32)
        carry = (read(HALO - 2), read(HALO - 1), [zero] * modes)
        states = lax.fori_loop(0, steps, step, carry, unroll=4)[2]
        line = lax.broadcasted_iota(jnp.int32, (SUB, 128), 0)

        def later(value, by):
            return jnp.where(line >= by, pltpu.roll(value, by, 0), 0.0)

        for m in range(modes):
            s = states[m]
            for by in (1, 2, 4):
                s = s + jnp.exp(-float(steps * by) * rates[m]) * later(s, by)
            inside[m, :, lanes] = later(s, 1)
            state[m : m + 1, lanes] = s[SUB - 1 :]


def local_kernel(sizes, pos, product, gain, decay, skip, local):
    rows, depth, width, modes, seq = sizes
    c = pos[3]
    steps = 2 * rows // SUB
    for lh in range(width // 128):
        mine = pl.ds(pl.multiple_of(c * width + lh * 128, 128), 128)
        lanes = pl.ds(lh * 128, 128)
        rates = [jnp.broadcast_to(decay[m : m + 1, mine] / seq, (SUB, 128)) for m in range(modes)]
        factors = [jnp.exp(-rate) for rate in rates]
        heights = [gain[m : m + 1, mine] * jnp.sqrt(2.0 * rates[m]) for m in range(modes)]
        direct = jnp.broadcast_to(skip[:, mine], (SUB, 128))

        def step(t, states):
            p = product[t, :, lanes]
            states = [a * s + p for a, s in zip(factors, states)]
            parts = [w * s for w, s in zip(heights, states)]
            while len(parts) > 1:
                parts = [a + b for a, b in zip(parts[::2], parts[1::2])]
            local[t, :, lanes] = parts[0] + direct * p
            return states

        lax.fori_loop(0, steps, step, [jnp.zeros((SUB, 128), F32)] * modes, unroll=4)


def finish_kernel(sizes, pos, gate, local, inside, states, gain, decay, out, start, whole):
    rows, depth, width, modes, seq = sizes
    rank, c = pos[0], pos[3]
    steps = 2 * rows // SUB
    length = 2 * rows
    for lh in range(width // 128):
        mine = pl.ds(pl.multiple_of(c * width + lh * 128, 128), 128)
        lanes = pl.ds(lh * 128, 128)
        over = jnp.exp(-float(length) * (decay[:, mine] / seq))
        entering = jnp.zeros((modes, 128), F32)
        for r in range(16):
            entering = jnp.where(r < rank, over * entering + states[r, :, lanes], entering)
        start[:, lanes] = entering
        line = lax.broadcasted_iota(jnp.int32, (SUB, 128), 0).astype(F32) * float(steps)
        factors, waves = [], []
        for m in range(modes):
            rate = jnp.broadcast_to(decay[m : m + 1, mine] / seq, (SUB, 128))
            factors.append(jnp.exp(-rate))
            height = gain[m : m + 1, mine] * jnp.sqrt(2.0 * rate)
            waves.append(height * (inside[m, :, lanes] + jnp.exp(-rate * line) * start[m : m + 1, lanes]))

        def step(t, waves):
            waves = [a * z for a, z in zip(factors, waves)]
            parts = waves
            while len(parts) > 1:
                parts = [a + b for a, b in zip(parts[::2], parts[1::2])]
            whole[lh, pl.ds(t, SUB, stride=steps), :] = gate[t, :, lanes] * (local[t, :, lanes] + parts[0])
            return waves

        lax.fori_loop(0, steps, step, waves, unroll=4)
        for part in range(2):
            out[part, :, lanes] = whole[lh, part * rows : part * rows + rows, :].astype(BF16)


def body(tokens, w_in, taps, modes_gain, decay, skip):
    rows = tokens.shape[0]
    group = w_in.shape[2]
    width = group // 2
    k = w_in.shape[0]
    modes = decay.shape[0]
    depth = tokens.shape[1] * 8
    seq = rows * 32
    sizes = (rows, depth, width, modes, seq)
    y, h, c = (lax.axis_index(a) for a in CTX)
    pos = jnp.stack([y * 4 + h, y, h, c]).astype(jnp.int32)

    tie = lax.optimization_barrier
    with jax.named_scope("weight_gather"):
        halves = w_in.reshape(k, 3, 2, width).transpose(2, 0, 1, 3).reshape(2, k, 3 * width)
        own = lax.all_to_all(halves, "c", 0, 0, tiled=True).reshape(2 * k, 3 * width)
        beside, far = both_ways(own, "h"), both_ways(own, "y")
    with jax.named_scope("token_swap"):
        other = lax.ppermute(tokens, "l", [(0, 1), (1, 0)])
    beside, far, other = tie((beside, far, other))
    with jax.named_scope("token_gather"):
        here = lax.axis_index("l") == 0
        wide = jnp.stack([jnp.where(here, tokens, other), jnp.where(here, other, tokens)])
        tok = lax.all_gather(wide, ("c", "x"), axis=0)
        tok = tok.reshape(2, 4, 2, rows, group)
        tail = tok[1, :, :, rows - HALO :].reshape(8 * HALO, group)
        tok = tok.reshape(16 * rows, group)
        halo = lax.ppermute(tail, ("y", "h"), [(i, i + 1) for i in range(15)])
    with jax.named_scope("weight_rings"):
        pair = jnp.concatenate(beside, 0)
        far_pair, farther = both_ways(pair, "y"), onward(*far, "y")
        opposite = onward(*beside, "h")
        far_pair, farther, opposite = tie((far_pair, farther, opposite))
        opposite = jnp.concatenate(opposite, 0)
        far_opposite, farther_pair = both_ways(opposite, "y"), onward(*far_pair, "y")
        far_opposite, farther_pair = tie((far_opposite, farther_pair))
        last = onward(*far_opposite, "y")
        pieces = [own, pair, opposite]
        for side in range(2):
            pieces += [far[side], far_pair[side], far_opposite[side]]
        pieces += [*farther, *farther_pair]

    vmem = pl.BlockSpec(memory_space=pltpu.VMEM)
    smem = pl.BlockSpec(memory_space=pltpu.SMEM)
    hbm = pl.BlockSpec(memory_space=pltpu.HBM)
    block = (2 * rows // SUB, SUB, width)
    full = jax.ShapeDtypeStruct(block, F32)
    lines = 2 * rows + HALO
    chunks = (3 * width // 128, lines, 128)
    sums = pl.pallas_call(
        functools.partial(project_kernel, sizes),
        out_shape=jax.ShapeDtypeStruct(chunks, F32),
        in_specs=[smem] + [hbm] * 15,
        out_specs=vmem,
        scratch_shapes=[
            pltpu.VMEM((lines, depth), BF16),
            pltpu.VMEM((depth, 3 * width), BF16),
            pltpu.SemaphoreType.DMA((24,)),
            pltpu.SemaphoreType.DMA((16,)),
        ],
        compiler_params=pltpu.CompilerParams(vmem_limit_bytes=20 * 2**20),
        cost_estimate=pl.CostEstimate(
            flops=2 * lines * depth * 3 * width, bytes_accessed=12_000_000, transcendentals=0
        ),
        name="project",
    )(pos, tok, halo, *pieces)
    params = pltpu.CompilerParams(vmem_limit_bytes=12 * 2**20)
    gate, product, inside, state = pl.pallas_call(
        functools.partial(state_kernel, sizes),
        out_shape=(
            full,
            full,
            jax.ShapeDtypeStruct((modes, SUB, width), F32),
            jax.ShapeDtypeStruct((modes, width), F32),
        ),
        in_specs=[smem] + [hbm] * 4 + [vmem] * 3,
        out_specs=(vmem,) * 4,
        scratch_shapes=[
            pltpu.VMEM((lines, depth // 16), BF16),
            pltpu.VMEM((depth // 16, 3 * width), BF16),
            pltpu.VMEM(chunks, F32),
            pltpu.SemaphoreType.DMA((5,)),
        ],
        compiler_params=params,
        name="states",
    )(pos, tok, halo, *last, sums, taps, decay)

    with jax.named_scope("state_exchange"):
        states = lax.all_to_all(
            jnp.broadcast_to(state, (16, *state.shape)), ("y", "h"), 0, 0, tiled=True
        )
    local = pl.pallas_call(
        functools.partial(local_kernel, sizes),
        out_shape=full,
        in_specs=[smem] + [vmem] * 4,
        out_specs=vmem,
        compiler_params=params,
        cost_estimate=pl.CostEstimate(flops=20_000_000, bytes_accessed=1_000_000, transcendentals=0),
        name="local",
    )(pos, product, modes_gain, decay, skip.reshape(1, group))
    out = pl.pallas_call(
        functools.partial(finish_kernel, sizes),
        out_shape=jax.ShapeDtypeStruct((2, rows, width), BF16),
        in_specs=[smem] + [vmem] * 6,
        out_specs=vmem,
        scratch_shapes=[pltpu.VMEM((modes, width), F32), pltpu.VMEM((width // 128, 2 * rows, 128), F32)],
        compiler_params=params,
        name="finish",
    )(pos, gate, local, inside, states, modes_gain, decay)
    with jax.named_scope("result_swap"):
        both = lax.all_to_all(out, "c", 0, 0, tiled=True)
        return both.transpose(1, 0, 2).reshape(rows, group)


def solution(mesh):
    split = Mesh(mesh.devices.reshape(4, 4, 2, 2, 4), AXES)
    return jax.shard_map(
        body,
        mesh=split,
        in_specs=(
            P(CTX, CH),
            P(CTX, None, CH),
            P(None, None, CH),
            P(None, CH),
            P(None, CH),
            P(CH),
        ),
        out_specs=P(CTX, CH),
        check_vma=False,
    )
```

```python
import functools

import jax
import jax.numpy as jnp
from jax import lax
from jax.experimental import pallas as pl
from jax.experimental.pallas import tpu as pltpu
from jax.sharding import Mesh
from jax.sharding import PartitionSpec as P

AXES = ("y", "h", "c", "l", "x")
CTX = ("y", "h", "c")
CH = ("l", "x")
F32 = jnp.float32
BF16 = jnp.bfloat16
HALO = 16
SUB = 8


def shifted(array, axis, step):
    n = lax.axis_size(axis)
    return lax.ppermute(array, axis, [(i, (i + step) % n) for i in range(n)])


def both_ways(piece, axis):
    return shifted(piece, axis, 1), shifted(piece, axis, -1)


def onward(behind, ahead, axis):
    half = behind.shape[0] // 2
    return shifted(behind[:half], axis, 1), shifted(ahead[half:], axis, -1)


def fetched(sizes, pos, tokens, halo, pieces, blocks, tokv, wv, sem):
    rows, depth, width, modes, seq = sizes
    k = depth // 16
    copies, at, seen = [], 0, set()

    def add(source, target):
        copies.append(pltpu.make_async_copy(source, target, sem.at[len(copies)]))
        return copies[-1]

    for piece, first, n, dy, dh, skip in blocks:
        add(pieces[piece].at[pl.ds(first, n), :], wv.at[pl.ds(at + skip, n), :]).start()
        if (dy, dh) not in seen:
            seen.add((dy, dh))
            ys, hs = lax.rem(pos[1] - dy + 4, 4), lax.rem(pos[2] - dh + 4, 4)
            ch = 2 * ys + lax.div(hs, 2)
            lanes = pl.ds(pl.multiple_of(lax.rem(hs, 2) * k, k), k)
            x = lax.rem(ch, 4)
            swapped = lax.rem(lax.div(ch, 4) + pos[4], 2)
            to = pl.ds(at, k)
            line = pl.ds(pl.multiple_of((4 * swapped + x) * HALO, HALO), HALO)
            add(halo.at[line, lanes], tokv.at[pl.ds(0, HALO), to]).start()
            for core in range(2):
                line = pl.ds(pl.multiple_of((4 * core + x) * rows, rows), rows)
                target = tokv.at[pl.ds(HALO + core * rows, rows), to]
                copy = add(tokens[0].at[line, lanes], target)
                pl.when(swapped == 0)(copy.start)
                copy = pltpu.make_async_copy(tokens[1].at[line, lanes], target, sem.at[len(copies) - 1])
                pl.when(swapped == 1)(copy.start)
        if skip + n == k:
            at += k
    return copies


def project_kernel(sizes, blocks, *refs):
    rows, depth, width, modes, seq = sizes
    pos, near, swapped, halo, *pieces = refs[:-4]
    sums, tokv, wv, sem = refs[-4:]
    for copy in fetched(sizes, pos, (near, swapped), halo, pieces, blocks, tokv, wv, sem):
        copy.wait()

    @pl.loop(0, 3)
    def _(j):
        cols = pl.ds(pl.multiple_of(j * width, width), width)
        part = jnp.dot(tokv[...], wv[:, cols], preferred_element_type=F32)
        for lh in range(width // 128):
            sums[j * (width // 128) + lh] = part[:, lh * 128 : lh * 128 + 128]


def state_kernel(sizes, blocks, *refs):
    rows, depth, width, modes, seq = sizes
    pos, near, swapped, halo, *pieces = refs[:-11]
    sums, taps, decay, gate, product, inside, state, tokv, wv, acc, sem = refs[-11:]
    c = pos[3]
    for copy in fetched(sizes, pos, (near, swapped), halo, pieces, blocks, tokv, wv, sem):
        copy.wait()

    @pl.loop(0, 3)
    def _(j):
        cols = pl.ds(pl.multiple_of(j * width, width), width)
        part = jnp.dot(tokv[...], wv[:, cols], preferred_element_type=F32)
        for lh in range(width // 128):
            chunk = j * (width // 128) + lh
            new = part[:, lh * 128 : lh * 128 + 128]
            acc[chunk] = (sums[chunk] + new).astype(BF16).astype(F32)

    steps = 2 * rows // SUB
    for lh in range(width // 128):
        mine = pl.ds(pl.multiple_of(c * width + lh * 128, 128), 128)
        lanes = pl.ds(lh * 128, 128)
        weights = [[taps[lag, j : j + 1, mine] for j in range(3)] for lag in range(3)]
        rates = [jnp.broadcast_to(decay[m : m + 1, mine] / seq, (SUB, 128)) for m in range(modes)]
        factors = [jnp.exp(-rate) for rate in rates]

        def read(start):
            return [
                acc[j * (width // 128) + lh, pl.ds(start, SUB, stride=steps), :]
                for j in range(3)
            ]

        def step(t, carry):
            before, last, states = carry
            now = read(HALO + t)
            f = [
                weights[0][j] * now[j] + weights[1][j] * last[j] + weights[2][j] * before[j]
                for j in range(3)
            ]
            p = f[1] * f[2]
            gate[t, :, lanes] = f[0]
            product[t, :, lanes] = p
            return last, now, [a * s + p for a, s in zip(factors, states)]

        zero = jnp.zeros((SUB, 128), F32)
        carry = (read(HALO - 2), read(HALO - 1), [zero] * modes)
        states = lax.fori_loop(0, steps, step, carry, unroll=4)[2]
        line = lax.broadcasted_iota(jnp.int32, (SUB, 128), 0)

        def later(value, by):
            return jnp.where(line >= by, pltpu.roll(value, by, 0), 0.0)

        for m in range(modes):
            s = states[m]
            for by in (1, 2, 4):
                s = s + jnp.exp(-float(steps * by) * rates[m]) * later(s, by)
            inside[m, :, lanes] = later(s, 1)
            state[m : m + 1, lanes] = s[SUB - 1 :]


def local_kernel(sizes, pos, product, gain, decay, skip, local):
    rows, depth, width, modes, seq = sizes
    c = pos[3]
    steps = 2 * rows // SUB
    for lh in range(width // 128):
        mine = pl.ds(pl.multiple_of(c * width + lh * 128, 128), 128)
        lanes = pl.ds(lh * 128, 128)
        rates = [jnp.broadcast_to(decay[m : m + 1, mine] / seq, (SUB, 128)) for m in range(modes)]
        factors = [jnp.exp(-rate) for rate in rates]
        heights = [gain[m : m + 1, mine] * jnp.sqrt(2.0 * rates[m]) for m in range(modes)]
        direct = jnp.broadcast_to(skip[:, mine], (SUB, 128))

        def step(t, states):
            p = product[t, :, lanes]
            states = [a * s + p for a, s in zip(factors, states)]
            parts = [w * s for w, s in zip(heights, states)]
            while len(parts) > 1:
                parts = [a + b for a, b in zip(parts[::2], parts[1::2])]
            local[t, :, lanes] = parts[0] + direct * p
            return states

        lax.fori_loop(0, steps, step, [jnp.zeros((SUB, 128), F32)] * modes, unroll=4)


def finish_kernel(sizes, pos, gate, local, inside, states, gain, decay, out, start, whole):
    rows, depth, width, modes, seq = sizes
    rank, c = pos[0], pos[3]
    steps = 2 * rows // SUB
    length = 2 * rows
    for lh in range(width // 128):
        mine = pl.ds(pl.multiple_of(c * width + lh * 128, 128), 128)
        lanes = pl.ds(lh * 128, 128)
        over = jnp.exp(-float(length) * (decay[:, mine] / seq))
        entering = jnp.zeros((modes, 128), F32)
        for r in range(16):
            entering = jnp.where(r < rank, over * entering + states[r, :, lanes], entering)
        start[:, lanes] = entering
        line = lax.broadcasted_iota(jnp.int32, (SUB, 128), 0).astype(F32) * float(steps)
        factors, waves = [], []
        for m in range(modes):
            rate = jnp.broadcast_to(decay[m : m + 1, mine] / seq, (SUB, 128))
            factors.append(jnp.exp(-rate))
            height = gain[m : m + 1, mine] * jnp.sqrt(2.0 * rate)
            waves.append(height * (inside[m, :, lanes] + jnp.exp(-rate * line) * start[m : m + 1, lanes]))

        def step(t, waves):
            waves = [a * z for a, z in zip(factors, waves)]
            parts = waves
            while len(parts) > 1:
                parts = [a + b for a, b in zip(parts[::2], parts[1::2])]
            whole[lh, pl.ds(t, SUB, stride=steps), :] = gate[t, :, lanes] * (local[t, :, lanes] + parts[0])
            return waves

        lax.fori_loop(0, steps, step, waves, unroll=4)
        for part in range(2):
            out[part, :, lanes] = whole[lh, part * rows : part * rows + rows, :].astype(BF16)


def body(tokens, w_in, taps, modes_gain, decay, skip):
    rows = tokens.shape[0]
    group = w_in.shape[2]
    width = group // 2
    k = w_in.shape[0]
    modes = decay.shape[0]
    depth = tokens.shape[1] * 8
    seq = rows * 32
    sizes = (rows, depth, width, modes, seq)
    y, h, c = (lax.axis_index(a) for a in CTX)
    pos = jnp.stack([y * 4 + h, y, h, c, lax.axis_index("l")]).astype(jnp.int32)

    tie = lax.optimization_barrier
    with jax.named_scope("weight_gather"):
        halves = w_in.reshape(k, 3, 2, width).transpose(2, 0, 1, 3).reshape(2, k, 3 * width)
        own = lax.all_to_all(halves, "c", 0, 0, tiled=True).reshape(2 * k, 3 * width)
        beside, far = both_ways(own, "h"), both_ways(own, "y")
    with jax.named_scope("token_swap"):
        other = lax.ppermute(tokens, "l", [(0, 1), (1, 0)])
        other, far = tie((other, far))
    farther = onward(*far, "y")
    beside, far, farther = tie((beside, far, farther))
    with jax.named_scope("token_gather"):
        near = lax.all_gather(tokens, ("c", "x"), axis=0, tiled=True)
        swapped = lax.all_gather(other, ("c", "x"), axis=0, tiled=True)
        tails = [t.reshape(2, 4, rows, group)[1, :, rows - HALO :] for t in (near, swapped)]
        tail = jnp.stack(tails).reshape(8 * HALO, group)
        halo = lax.ppermute(tail, ("y", "h"), [(i, i + 1) for i in range(15)])
    with jax.named_scope("weight_rings"):
        pair = jnp.concatenate(beside, 0)
        far_pair, opposite = both_ways(pair, "y"), onward(*beside, "h")
        far_pair, opposite = tie((far_pair, opposite))
        opposite = jnp.concatenate(opposite, 0)
        far_opposite, farther_pair = both_ways(opposite, "y"), onward(*far_pair, "y")
        last = shifted(opposite, "y", 2)

    two = 2 * k
    half = k
    early = [own, pair, opposite, *far, *far_pair, *farther]
    early_blocks = [(0, 0, two, 0, 0, 0), (1, 0, two, 0, 1, 0), (1, two, two, 0, -1, 0), (2, 0, two, 0, 2, 0)]
    for side, dy in enumerate((1, -1)):
        early_blocks += [
            (3 + side, 0, two, dy, 0, 0),
            (5 + side, 0, two, dy, 1, 0),
            (5 + side, two, two, dy, -1, 0),
        ]
    early_blocks += [(7, 0, half, 2, 0, 0), (8, 0, half, 2, 0, half)]
    late = [*farther_pair, *far_opposite, last]
    late_blocks = [
        (0, 0, two, 2, 1, 0),
        (1, 0, two, 2, -1, 0),
        (2, 0, two, 1, 2, 0),
        (3, 0, two, -1, 2, 0),
        (4, 0, two, 2, 2, 0),
    ]

    vmem = pl.BlockSpec(memory_space=pltpu.VMEM)
    smem = pl.BlockSpec(memory_space=pltpu.SMEM)
    hbm = pl.BlockSpec(memory_space=pltpu.HBM)
    block = (2 * rows // SUB, SUB, width)
    full = jax.ShapeDtypeStruct(block, F32)
    lines = 2 * rows + HALO
    chunks = (3 * width // 128, lines, 128)

    def held(n):
        return [pltpu.VMEM((lines, n * two), BF16), pltpu.VMEM((n * two, 3 * width), BF16)]

    def sems(blocks, n):
        return pltpu.SemaphoreType.DMA((len(blocks) + 3 * n,))

    sums = pl.pallas_call(
        functools.partial(project_kernel, sizes, early_blocks),
        out_shape=jax.ShapeDtypeStruct(chunks, F32),
        in_specs=[smem] + [hbm] * (3 + len(early)),
        out_specs=vmem,
        scratch_shapes=[*held(11), sems(early_blocks, 11)],
        compiler_params=pltpu.CompilerParams(vmem_limit_bytes=14 * 2**20),
        cost_estimate=pl.CostEstimate(
            flops=2 * lines * 11 * two * 3 * width, bytes_accessed=9_000_000, transcendentals=0
        ),
        name="project",
    )(pos, near, swapped, halo, *early)
    params = pltpu.CompilerParams(vmem_limit_bytes=12 * 2**20)
    gate, product, inside, state = pl.pallas_call(
        functools.partial(state_kernel, sizes, late_blocks),
        out_shape=(
            full,
            full,
            jax.ShapeDtypeStruct((modes, SUB, width), F32),
            jax.ShapeDtypeStruct((modes, width), F32),
        ),
        in_specs=[smem] + [hbm] * (3 + len(late)) + [vmem] * 3,
        out_specs=(vmem,) * 4,
        scratch_shapes=[*held(5), pltpu.VMEM(chunks, F32), sems(late_blocks, 5)],
        compiler_params=params,
        name="states",
    )(pos, near, swapped, halo, *late, sums, taps, decay)

    with jax.named_scope("state_exchange"):
        states = lax.all_to_all(
            jnp.broadcast_to(state, (16, *state.shape)), ("y", "h"), 0, 0, tiled=True
        )
    local = pl.pallas_call(
        functools.partial(local_kernel, sizes),
        out_shape=full,
        in_specs=[smem] + [vmem] * 4,
        out_specs=vmem,
        compiler_params=params,
        cost_estimate=pl.CostEstimate(flops=20_000_000, bytes_accessed=1_000_000, transcendentals=0),
        name="local",
    )(pos, product, modes_gain, decay, skip.reshape(1, group))
    out = pl.pallas_call(
        functools.partial(finish_kernel, sizes),
        out_shape=jax.ShapeDtypeStruct((2, rows, width), BF16),
        in_specs=[smem] + [vmem] * 6,
        out_specs=vmem,
        scratch_shapes=[pltpu.VMEM((modes, width), F32), pltpu.VMEM((width // 128, 2 * rows, 128), F32)],
        compiler_params=params,
        name="finish",
    )(pos, gate, local, inside, states, modes_gain, decay)
    with jax.named_scope("result_swap"):
        both = lax.all_to_all(out, "c", 0, 0, tiled=True)
        return both.transpose(1, 0, 2).reshape(rows, group)


def solution(mesh):
    split = Mesh(mesh.devices.reshape(4, 4, 2, 2, 4), AXES)
    return jax.shard_map(
        body,
        mesh=split,
        in_specs=(
            P(CTX, CH),
            P(CTX, None, CH),
            P(None, None, CH),
            P(None, CH),
            P(None, CH),
            P(CH),
        ),
        out_specs=P(CTX, CH),
        check_vma=False,
    )
```

```python
import functools

import jax
import jax.numpy as jnp
from jax import lax
from jax.experimental import pallas as pl
from jax.experimental.pallas import tpu as pltpu
from jax.sharding import Mesh
from jax.sharding import PartitionSpec as P

AXES = ("y", "h", "c", "l", "x")
CTX = ("y", "h", "c")
CH = ("l", "x")
F32 = jnp.float32
BF16 = jnp.bfloat16
HALO = 16
SUB = 8


def shifted(array, axis, step):
    n = lax.axis_size(axis)
    return lax.ppermute(array, axis, [(i, (i + step) % n) for i in range(n)])


def both_ways(piece, axis):
    return shifted(piece, axis, 1), shifted(piece, axis, -1)


def onward(behind, ahead, axis):
    half = behind.shape[0] // 2
    return shifted(behind[:half], axis, 1), shifted(ahead[half:], axis, -1)


def fetched(sizes, pos, tokens, pieces, blocks, tokv, wv, sem):
    rows, depth, width, modes, seq = sizes
    k = depth // 16
    lines = rows + HALO
    copies, at, seen = [], 0, set()

    def add(source, target):
        copies.append(pltpu.make_async_copy(source, target, sem.at[len(copies)]))
        return copies[-1]

    for piece, first, n, dy, dh, skip in blocks:
        add(pieces[piece].at[pl.ds(first, n), :], wv.at[pl.ds(at + skip, n), :]).start()
        if (dy, dh) not in seen:
            seen.add((dy, dh))
            ys, hs = lax.rem(pos[1] - dy + 4, 4), lax.rem(pos[2] - dh + 4, 4)
            ch = 2 * ys + lax.div(hs, 2)
            lanes = pl.ds(pl.multiple_of(lax.rem(hs, 2) * k, k), k)
            x = lax.rem(ch, 4)
            swapped = lax.rem(lax.div(ch, 4) + pos[4], 2)
            to = pl.ds(at, k)
            for core in range(2):
                skipped = HALO * core
                line = pl.ds(
                    pl.multiple_of((4 * core + x) * lines + skipped, HALO), lines - skipped
                )
                target = tokv.at[pl.ds(core * lines, lines - skipped), to]
                copy = add(tokens[0].at[line, lanes], target)
                pl.when(swapped == 0)(copy.start)
                copy = pltpu.make_async_copy(tokens[1].at[line, lanes], target, sem.at[len(copies) - 1])
                pl.when(swapped == 1)(copy.start)
        if skip + n == k:
            at += k
    return copies


def project_kernel(sizes, blocks, *refs):
    rows, depth, width, modes, seq = sizes
    pos, near, swapped, *pieces = refs[:-4]
    sums, tokv, wv, sem = refs[-4:]
    for copy in fetched(sizes, pos, (near, swapped), pieces, blocks, tokv, wv, sem):
        copy.wait()

    @pl.loop(0, 3)
    def _(j):
        cols = pl.ds(pl.multiple_of(j * width, width), width)
        part = jnp.dot(tokv[...], wv[:, cols], preferred_element_type=F32)
        for lh in range(width // 128):
            sums[j * (width // 128) + lh] = part[:, lh * 128 : lh * 128 + 128]


def state_kernel(sizes, blocks, *refs):
    rows, depth, width, modes, seq = sizes
    pos, near, swapped, *pieces = refs[:-11]
    sums, taps, decay, gate, product, inside, state, tokv, wv, acc, sem = refs[-11:]
    c = pos[3]
    for copy in fetched(sizes, pos, (near, swapped), pieces, blocks, tokv, wv, sem):
        copy.wait()

    @pl.loop(0, 3)
    def _(j):
        cols = pl.ds(pl.multiple_of(j * width, width), width)
        part = jnp.dot(tokv[...], wv[:, cols], preferred_element_type=F32)
        for lh in range(width // 128):
            chunk = j * (width // 128) + lh
            new = part[:, lh * 128 : lh * 128 + 128]
            acc[chunk] = (sums[chunk] + new).astype(BF16).astype(F32)

    steps = 2 * rows // SUB
    for lh in range(width // 128):
        mine = pl.ds(pl.multiple_of(c * width + lh * 128, 128), 128)
        lanes = pl.ds(lh * 128, 128)
        weights = [[taps[lag, j : j + 1, mine] for j in range(3)] for lag in range(3)]
        rates = [jnp.broadcast_to(decay[m : m + 1, mine] / seq, (SUB, 128)) for m in range(modes)]
        factors = [jnp.exp(-rate) for rate in rates]

        def read(start):
            return [
                acc[j * (width // 128) + lh, pl.ds(start, SUB, stride=steps), :]
                for j in range(3)
            ]

        def step(t, carry):
            before, last, states = carry
            now = read(HALO + t)
            f = [
                weights[0][j] * now[j] + weights[1][j] * last[j] + weights[2][j] * before[j]
                for j in range(3)
            ]
            p = f[1] * f[2]
            gate[t, :, lanes] = f[0]
            product[t, :, lanes] = p
            return last, now, [a * s + p for a, s in zip(factors, states)]

        zero = jnp.zeros((SUB, 128), F32)
        carry = (read(HALO - 2), read(HALO - 1), [zero] * modes)
        states = lax.fori_loop(0, steps, step, carry, unroll=4)[2]
        line = lax.broadcasted_iota(jnp.int32, (SUB, 128), 0)

        def later(value, by):
            return jnp.where(line >= by, pltpu.roll(value, by, 0), 0.0)

        for m in range(modes):
            s = states[m]
            for by in (1, 2, 4):
                s = s + jnp.exp(-float(steps * by) * rates[m]) * later(s, by)
            inside[m, :, lanes] = later(s, 1)
            state[m : m + 1, lanes] = s[SUB - 1 :]


def local_kernel(sizes, pos, product, gain, decay, skip, local):
    rows, depth, width, modes, seq = sizes
    c = pos[3]
    steps = 2 * rows // SUB
    for lh in range(width // 128):
        mine = pl.ds(pl.multiple_of(c * width + lh * 128, 128), 128)
        lanes = pl.ds(lh * 128, 128)
        rates = [jnp.broadcast_to(decay[m : m + 1, mine] / seq, (SUB, 128)) for m in range(modes)]
        factors = [jnp.exp(-rate) for rate in rates]
        heights = [gain[m : m + 1, mine] * jnp.sqrt(2.0 * rates[m]) for m in range(modes)]
        direct = jnp.broadcast_to(skip[:, mine], (SUB, 128))

        def step(t, states):
            p = product[t, :, lanes]
            states = [a * s + p for a, s in zip(factors, states)]
            parts = [w * s for w, s in zip(heights, states)]
            while len(parts) > 1:
                parts = [a + b for a, b in zip(parts[::2], parts[1::2])]
            local[t, :, lanes] = parts[0] + direct * p
            return states

        lax.fori_loop(0, steps, step, [jnp.zeros((SUB, 128), F32)] * modes, unroll=4)


def finish_kernel(sizes, pos, gate, local, inside, states, gain, decay, out, start, whole):
    rows, depth, width, modes, seq = sizes
    rank, c = pos[0], pos[3]
    steps = 2 * rows // SUB
    length = 2 * rows
    for lh in range(width // 128):
        mine = pl.ds(pl.multiple_of(c * width + lh * 128, 128), 128)
        lanes = pl.ds(lh * 128, 128)
        over = jnp.exp(-float(length) * (decay[:, mine] / seq))
        entering = jnp.zeros((modes, 128), F32)
        for r in range(16):
            entering = jnp.where(r < rank, over * entering + states[r, :, lanes], entering)
        start[:, lanes] = entering
        line = lax.broadcasted_iota(jnp.int32, (SUB, 128), 0).astype(F32) * float(steps)
        factors, waves = [], []
        for m in range(modes):
            rate = jnp.broadcast_to(decay[m : m + 1, mine] / seq, (SUB, 128))
            factors.append(jnp.exp(-rate))
            height = gain[m : m + 1, mine] * jnp.sqrt(2.0 * rate)
            waves.append(height * (inside[m, :, lanes] + jnp.exp(-rate * line) * start[m : m + 1, lanes]))

        def step(t, waves):
            waves = [a * z for a, z in zip(factors, waves)]
            parts = waves
            while len(parts) > 1:
                parts = [a + b for a, b in zip(parts[::2], parts[1::2])]
            whole[lh, pl.ds(t, SUB, stride=steps), :] = gate[t, :, lanes] * (local[t, :, lanes] + parts[0])
            return waves

        lax.fori_loop(0, steps, step, waves, unroll=4)
        for part in range(2):
            out[part, :, lanes] = whole[lh, part * rows : part * rows + rows, :].astype(BF16)


def body(tokens, w_in, taps, modes_gain, decay, skip):
    rows = tokens.shape[0]
    group = w_in.shape[2]
    width = group // 2
    k = w_in.shape[0]
    modes = decay.shape[0]
    depth = tokens.shape[1] * 8
    seq = rows * 32
    sizes = (rows, depth, width, modes, seq)
    y, h, c = (lax.axis_index(a) for a in CTX)
    pos = jnp.stack([y * 4 + h, y, h, c, lax.axis_index("l")]).astype(jnp.int32)

    tie = lax.optimization_barrier
    with jax.named_scope("weight_gather"):
        halves = w_in.reshape(k, 3, 2, width).transpose(2, 0, 1, 3).reshape(2, k, 3 * width)
        own = lax.all_to_all(halves, "c", 0, 0, tiled=True).reshape(2 * k, 3 * width)
        beside, far = both_ways(own, "h"), both_ways(own, "y")
    with jax.named_scope("token_swap"):
        halo = lax.ppermute(tokens[rows - HALO :], CTX, [(i, i + 1) for i in range(1, 31, 2)])
        tokens = jnp.concatenate([halo, tokens], 0)
        other = lax.ppermute(tokens, "l", [(0, 1), (1, 0)])
    farther = onward(*far, "y")
    beside, far, farther, other = tie((beside, far, farther, other))
    with jax.named_scope("token_gather"):
        near = lax.all_gather(tokens, ("c", "x"), axis=0, tiled=True)
        swapped = lax.all_gather(other, ("c", "x"), axis=0, tiled=True)
    with jax.named_scope("weight_rings"):
        pair = jnp.concatenate(beside, 0)
        far_pair, opposite = both_ways(pair, "y"), onward(*beside, "h")
        far_pair, opposite = tie((far_pair, opposite))
        opposite = jnp.concatenate(opposite, 0)
        far_opposite, farther_pair = both_ways(opposite, "y"), onward(*far_pair, "y")
        last = shifted(opposite, "y", 2)

    two = 2 * k
    half = k
    early = [own, pair, opposite, *far, *far_pair, *farther]
    early_blocks = [(0, 0, two, 0, 0, 0), (1, 0, two, 0, 1, 0), (1, two, two, 0, -1, 0), (2, 0, two, 0, 2, 0)]
    for side, dy in enumerate((1, -1)):
        early_blocks += [
            (3 + side, 0, two, dy, 0, 0),
            (5 + side, 0, two, dy, 1, 0),
            (5 + side, two, two, dy, -1, 0),
        ]
    early_blocks += [(7, 0, half, 2, 0, 0), (8, 0, half, 2, 0, half)]
    late = [*farther_pair, *far_opposite, last]
    late_blocks = [
        (0, 0, two, 2, 1, 0),
        (1, 0, two, 2, -1, 0),
        (2, 0, two, 1, 2, 0),
        (3, 0, two, -1, 2, 0),
        (4, 0, two, 2, 2, 0),
    ]

    vmem = pl.BlockSpec(memory_space=pltpu.VMEM)
    smem = pl.BlockSpec(memory_space=pltpu.SMEM)
    hbm = pl.BlockSpec(memory_space=pltpu.HBM)
    block = (2 * rows // SUB, SUB, width)
    full = jax.ShapeDtypeStruct(block, F32)
    lines = 2 * rows + HALO
    chunks = (3 * width // 128, lines, 128)

    def held(n):
        return [pltpu.VMEM((lines, n * two), BF16), pltpu.VMEM((n * two, 3 * width), BF16)]

    def sems(blocks, n):
        return pltpu.SemaphoreType.DMA((len(blocks) + 2 * n,))

    sums = pl.pallas_call(
        functools.partial(project_kernel, sizes, early_blocks),
        out_shape=jax.ShapeDtypeStruct(chunks, F32),
        in_specs=[smem] + [hbm] * (2 + len(early)),
        out_specs=vmem,
        scratch_shapes=[*held(11), sems(early_blocks, 11)],
        compiler_params=pltpu.CompilerParams(vmem_limit_bytes=14 * 2**20),
        cost_estimate=pl.CostEstimate(
            flops=2 * lines * 11 * two * 3 * width, bytes_accessed=9_000_000, transcendentals=0
        ),
        name="project",
    )(pos, near, swapped, *early)
    params = pltpu.CompilerParams(vmem_limit_bytes=12 * 2**20)
    gate, product, inside, state = pl.pallas_call(
        functools.partial(state_kernel, sizes, late_blocks),
        out_shape=(
            full,
            full,
            jax.ShapeDtypeStruct((modes, SUB, width), F32),
            jax.ShapeDtypeStruct((modes, width), F32),
        ),
        in_specs=[smem] + [hbm] * (2 + len(late)) + [vmem] * 3,
        out_specs=(vmem,) * 4,
        scratch_shapes=[*held(5), pltpu.VMEM(chunks, F32), sems(late_blocks, 5)],
        compiler_params=params,
        name="states",
    )(pos, near, swapped, *late, sums, taps, decay)

    with jax.named_scope("state_exchange"):
        states = lax.all_to_all(
            jnp.broadcast_to(state, (16, *state.shape)), ("y", "h"), 0, 0, tiled=True
        )
    local = pl.pallas_call(
        functools.partial(local_kernel, sizes),
        out_shape=full,
        in_specs=[smem] + [vmem] * 4,
        out_specs=vmem,
        compiler_params=params,
        cost_estimate=pl.CostEstimate(flops=20_000_000, bytes_accessed=1_000_000, transcendentals=0),
        name="local",
    )(pos, product, modes_gain, decay, skip.reshape(1, group))
    out = pl.pallas_call(
        functools.partial(finish_kernel, sizes),
        out_shape=jax.ShapeDtypeStruct((2, rows, width), BF16),
        in_specs=[smem] + [vmem] * 6,
        out_specs=vmem,
        scratch_shapes=[pltpu.VMEM((modes, width), F32), pltpu.VMEM((width // 128, 2 * rows, 128), F32)],
        compiler_params=params,
        name="finish",
    )(pos, gate, local, inside, states, modes_gain, decay)
    with jax.named_scope("result_swap"):
        both = lax.all_to_all(out, "c", 0, 0, tiled=True)
        return both.transpose(1, 0, 2).reshape(rows, group)


def solution(mesh):
    split = Mesh(mesh.devices.reshape(4, 4, 2, 2, 4), AXES)
    return jax.shard_map(
        body,
        mesh=split,
        in_specs=(
            P(CTX, CH),
            P(CTX, None, CH),
            P(None, None, CH),
            P(None, CH),
            P(None, CH),
            P(CH),
        ),
        out_specs=P(CTX, CH),
        check_vma=False,
    )
```

```python
import functools

import jax
import jax.numpy as jnp
from jax import lax
from jax.experimental import pallas as pl
from jax.experimental.pallas import tpu as pltpu
from jax.sharding import Mesh
from jax.sharding import PartitionSpec as P

AXES = ("y", "h", "c", "l", "x")
CTX = ("y", "h", "c")
CH = ("l", "x")
F32 = jnp.float32
BF16 = jnp.bfloat16
HALO = 16
SUB = 8


def shifted(array, axis, step):
    n = lax.axis_size(axis)
    return lax.ppermute(array, axis, [(i, (i + step) % n) for i in range(n)])


def both_ways(piece, axis):
    return shifted(piece, axis, 1), shifted(piece, axis, -1)


def onward(behind, ahead, axis):
    half = behind.shape[0] // 2
    return shifted(behind[:half], axis, 1), shifted(ahead[half:], axis, -1)


def fetched(sizes, pos, tok, pieces, blocks, tokv, wv, sem):
    rows, depth, width, modes, seq = sizes
    k = depth // 16
    lines = rows + HALO
    copies, at, seen = [], 0, set()

    def start(source, target):
        copies.append(pltpu.make_async_copy(source, target, sem.at[len(copies)]))
        copies[-1].start()

    for piece, first, n, dy, dh, skip in blocks:
        start(pieces[piece].at[pl.ds(first, n), :], wv.at[pl.ds(at + skip, n), :])
        if (dy, dh) not in seen:
            seen.add((dy, dh))
            ys, hs = lax.rem(pos[1] - dy + 4, 4), lax.rem(pos[2] - dh + 4, 4)
            ch = 2 * ys + lax.div(hs, 2)
            lanes = pl.ds(pl.multiple_of(lax.rem(hs, 2) * k, k), k)
            part = 2 * lax.rem(ch, 4) + lax.rem(lax.div(ch, 4) + pos[4], 2)
            for core in range(2):
                skipped = HALO * core
                line = pl.multiple_of((8 * core + part) * lines + skipped, HALO)
                start(
                    tok.at[pl.ds(line, lines - skipped), lanes],
                    tokv.at[pl.ds(core * lines, lines - skipped), pl.ds(at, k)],
                )
        if skip + n == k:
            at += k
    return copies


def project_kernel(sizes, blocks, *refs):
    rows, depth, width, modes, seq = sizes
    pos, tok, *pieces = refs[:-4]
    sums, tokv, wv, sem = refs[-4:]
    for copy in fetched(sizes, pos, tok, pieces, blocks, tokv, wv, sem):
        copy.wait()

    @pl.loop(0, 3)
    def _(j):
        cols = pl.ds(pl.multiple_of(j * width, width), width)
        part = jnp.dot(tokv[...], wv[:, cols], preferred_element_type=F32)
        for lh in range(width // 128):
            sums[j * (width // 128) + lh] = part[:, lh * 128 : lh * 128 + 128]


def state_kernel(sizes, blocks, *refs):
    rows, depth, width, modes, seq = sizes
    pos, tok, *pieces = refs[:-11]
    sums, taps, decay, gate, product, inside, state, tokv, wv, acc, sem = refs[-11:]
    c = pos[3]
    for copy in fetched(sizes, pos, tok, pieces, blocks, tokv, wv, sem):
        copy.wait()

    @pl.loop(0, 3)
    def _(j):
        cols = pl.ds(pl.multiple_of(j * width, width), width)
        part = jnp.dot(tokv[...], wv[:, cols], preferred_element_type=F32)
        for lh in range(width // 128):
            chunk = j * (width // 128) + lh
            new = part[:, lh * 128 : lh * 128 + 128]
            acc[chunk] = (sums[chunk] + new).astype(BF16).astype(F32)

    steps = 2 * rows // SUB
    for lh in range(width // 128):
        mine = pl.ds(pl.multiple_of(c * width + lh * 128, 128), 128)
        lanes = pl.ds(lh * 128, 128)
        weights = [[taps[lag, j : j + 1, mine] for j in range(3)] for lag in range(3)]
        rates = [jnp.broadcast_to(decay[m : m + 1, mine] / seq, (SUB, 128)) for m in range(modes)]
        factors = [jnp.exp(-rate) for rate in rates]

        def read(start):
            return [
                acc[j * (width // 128) + lh, pl.ds(start, SUB, stride=steps), :]
                for j in range(3)
            ]

        def step(t, carry):
            before, last, states = carry
            now = read(HALO + t)
            f = [
                weights[0][j] * now[j] + weights[1][j] * last[j] + weights[2][j] * before[j]
                for j in range(3)
            ]
            p = f[1] * f[2]
            gate[t, :, lanes] = f[0]
            product[t, :, lanes] = p
            return last, now, [a * s + p for a, s in zip(factors, states)]

        zero = jnp.zeros((SUB, 128), F32)
        carry = (read(HALO - 2), read(HALO - 1), [zero] * modes)
        states = lax.fori_loop(0, steps, step, carry, unroll=4)[2]
        line = lax.broadcasted_iota(jnp.int32, (SUB, 128), 0)

        def later(value, by):
            return jnp.where(line >= by, pltpu.roll(value, by, 0), 0.0)

        for m in range(modes):
            s = states[m]
            for by in (1, 2, 4):
                s = s + jnp.exp(-float(steps * by) * rates[m]) * later(s, by)
            inside[m, :, lanes] = later(s, 1)
            state[m : m + 1, lanes] = s[SUB - 1 :]


def local_kernel(sizes, pos, product, gain, decay, skip, local):
    rows, depth, width, modes, seq = sizes
    c = pos[3]
    steps = 2 * rows // SUB
    for lh in range(width // 128):
        mine = pl.ds(pl.multiple_of(c * width + lh * 128, 128), 128)
        lanes = pl.ds(lh * 128, 128)
        rates = [jnp.broadcast_to(decay[m : m + 1, mine] / seq, (SUB, 128)) for m in range(modes)]
        factors = [jnp.exp(-rate) for rate in rates]
        heights = [gain[m : m + 1, mine] * jnp.sqrt(2.0 * rates[m]) for m in range(modes)]
        direct = jnp.broadcast_to(skip[:, mine], (SUB, 128))

        def step(t, states):
            p = product[t, :, lanes]
            states = [a * s + p for a, s in zip(factors, states)]
            parts = [w * s for w, s in zip(heights, states)]
            while len(parts) > 1:
                parts = [a + b for a, b in zip(parts[::2], parts[1::2])]
            local[t, :, lanes] = parts[0] + direct * p
            return states

        lax.fori_loop(0, steps, step, [jnp.zeros((SUB, 128), F32)] * modes, unroll=4)


def finish_kernel(sizes, pos, gate, local, inside, states, gain, decay, out, start, whole):
    rows, depth, width, modes, seq = sizes
    rank, c = pos[0], pos[3]
    steps = 2 * rows // SUB
    length = 2 * rows
    for lh in range(width // 128):
        mine = pl.ds(pl.multiple_of(c * width + lh * 128, 128), 128)
        lanes = pl.ds(lh * 128, 128)
        over = jnp.exp(-float(length) * (decay[:, mine] / seq))
        entering = jnp.zeros((modes, 128), F32)
        for r in range(16):
            entering = jnp.where(r < rank, over * entering + states[r, :, lanes], entering)
        start[:, lanes] = entering
        line = lax.broadcasted_iota(jnp.int32, (SUB, 128), 0).astype(F32) * float(steps)
        factors, waves = [], []
        for m in range(modes):
            rate = jnp.broadcast_to(decay[m : m + 1, mine] / seq, (SUB, 128))
            factors.append(jnp.exp(-rate))
            height = gain[m : m + 1, mine] * jnp.sqrt(2.0 * rate)
            waves.append(height * (inside[m, :, lanes] + jnp.exp(-rate * line) * start[m : m + 1, lanes]))

        def step(t, waves):
            waves = [a * z for a, z in zip(factors, waves)]
            parts = waves
            while len(parts) > 1:
                parts = [a + b for a, b in zip(parts[::2], parts[1::2])]
            whole[lh, pl.ds(t, SUB, stride=steps), :] = gate[t, :, lanes] * (local[t, :, lanes] + parts[0])
            return waves

        lax.fori_loop(0, steps, step, waves, unroll=4)
        for part in range(2):
            out[part, :, lanes] = whole[lh, part * rows : part * rows + rows, :].astype(BF16)


def body(tokens, w_in, taps, modes_gain, decay, skip):
    rows = tokens.shape[0]
    group = w_in.shape[2]
    width = group // 2
    k = w_in.shape[0]
    modes = decay.shape[0]
    depth = tokens.shape[1] * 8
    seq = rows * 32
    sizes = (rows, depth, width, modes, seq)
    y, h, c = (lax.axis_index(a) for a in CTX)
    pos = jnp.stack([y * 4 + h, y, h, c, lax.axis_index("l")]).astype(jnp.int32)

    tie = lax.optimization_barrier
    with jax.named_scope("weight_gather"):
        halves = w_in.reshape(k, 3, 2, width).transpose(2, 0, 1, 3).reshape(2, k, 3 * width)
        own = lax.all_to_all(halves, "c", 0, 0, tiled=True).reshape(2 * k, 3 * width)
        tail, own = tie((tokens[rows - HALO :], own))
    with jax.named_scope("token_swap"):
        other = lax.ppermute(tokens, "l", [(0, 1), (1, 0)])
        route = [(4 * r + 2 + side, 4 * r + 4 + side) for r in range(15) for side in range(2)]
        halo = lax.ppermute(tail, (*CTX, "l"), route)
        other_halo = lax.ppermute(tail, (*CTX, "l"), [(i, j ^ 1) for i, j in route])
    with jax.named_scope("weight_rings"):
        farther = shifted(own, "y", 2)
        far = both_ways(own, "y")
        beside = both_ways(own, "h")
    first = (halo, other_halo, other, farther, far, beside)
    halo, other_halo, other, farther, far, beside = tie(first)
    with jax.named_scope("token_gather"):
        wide = jnp.concatenate([halo, tokens, other_halo, other], 0)
        tok = lax.all_gather(wide, ("c", "x"), axis=0, tiled=True)
    with jax.named_scope("weight_rings"):
        two, half = 2 * k, k
        pair = jnp.concatenate(beside, 0)
        far_pair, opposite = both_ways(pair, "y"), onward(*beside, "h")
        far_pair, opposite = tie((far_pair, opposite))
        opposite = jnp.concatenate(opposite, 0)
        last = shifted(opposite, "y", 2)
        farther_pair = onward(*far_pair, "y")
        firsts = jnp.concatenate([p[:half] for p in far_pair], 0)
        seconds = jnp.concatenate([p[two + half :] for p in far_pair], 0)
        far_opposite = shifted(firsts, "h", 1), shifted(seconds, "h", -1)

    early = [own, pair, opposite, *far, *far_pair, farther]
    early_blocks = [(0, 0, two, 0, 0, 0), (1, 0, two, 0, 1, 0), (1, two, two, 0, -1, 0), (2, 0, two, 0, 2, 0)]
    for side, dy in enumerate((1, -1)):
        early_blocks += [
            (3 + side, 0, two, dy, 0, 0),
            (5 + side, 0, two, dy, 1, 0),
            (5 + side, two, two, dy, -1, 0),
        ]
    early_blocks += [(7, 0, two, 2, 0, 0)]
    late = [*farther_pair, *far_opposite, last]
    late_blocks = [
        (0, 0, two, 2, 1, 0),
        (1, 0, two, 2, -1, 0),
        (2, 0, half, 1, 2, 0),
        (3, 0, half, 1, 2, half),
        (2, half, half, -1, 2, 0),
        (3, half, half, -1, 2, half),
        (4, 0, two, 2, 2, 0),
    ]

    vmem = pl.BlockSpec(memory_space=pltpu.VMEM)
    smem = pl.BlockSpec(memory_space=pltpu.SMEM)
    hbm = pl.BlockSpec(memory_space=pltpu.HBM)
    block = (2 * rows // SUB, SUB, width)
    full = jax.ShapeDtypeStruct(block, F32)
    lines = 2 * rows + HALO
    chunks = (3 * width // 128, lines, 128)

    def held(n):
        return [pltpu.VMEM((lines, n * two), BF16), pltpu.VMEM((n * two, 3 * width), BF16)]

    def sems(blocks, n):
        return pltpu.SemaphoreType.DMA((len(blocks) + 2 * n,))

    sums = pl.pallas_call(
        functools.partial(project_kernel, sizes, early_blocks),
        out_shape=jax.ShapeDtypeStruct(chunks, F32),
        in_specs=[smem] + [hbm] * (1 + len(early)),
        out_specs=vmem,
        scratch_shapes=[*held(11), sems(early_blocks, 11)],
        compiler_params=pltpu.CompilerParams(vmem_limit_bytes=14 * 2**20),
        cost_estimate=pl.CostEstimate(
            flops=2 * lines * 11 * two * 3 * width, bytes_accessed=9_000_000, transcendentals=0
        ),
        name="project",
    )(pos, tok, *early)
    params = pltpu.CompilerParams(vmem_limit_bytes=12 * 2**20)
    gate, product, inside, state = pl.pallas_call(
        functools.partial(state_kernel, sizes, late_blocks),
        out_shape=(
            full,
            full,
            jax.ShapeDtypeStruct((modes, SUB, width), F32),
            jax.ShapeDtypeStruct((modes, width), F32),
        ),
        in_specs=[smem] + [hbm] * (1 + len(late)) + [vmem] * 3,
        out_specs=(vmem,) * 4,
        scratch_shapes=[*held(5), pltpu.VMEM(chunks, F32), sems(late_blocks, 5)],
        compiler_params=params,
        name="states",
    )(pos, tok, *late, sums, taps, decay)

    with jax.named_scope("state_exchange"):
        states = lax.all_to_all(
            jnp.broadcast_to(state, (16, *state.shape)), ("y", "h"), 0, 0, tiled=True
        )
    local = pl.pallas_call(
        functools.partial(local_kernel, sizes),
        out_shape=full,
        in_specs=[smem] + [vmem] * 4,
        out_specs=vmem,
        compiler_params=params,
        cost_estimate=pl.CostEstimate(flops=20_000_000, bytes_accessed=1_000_000, transcendentals=0),
        name="local",
    )(pos, product, modes_gain, decay, skip.reshape(1, group))
    out = pl.pallas_call(
        functools.partial(finish_kernel, sizes),
        out_shape=jax.ShapeDtypeStruct((2, rows, width), BF16),
        in_specs=[smem] + [vmem] * 6,
        out_specs=vmem,
        scratch_shapes=[pltpu.VMEM((modes, width), F32), pltpu.VMEM((width // 128, 2 * rows, 128), F32)],
        compiler_params=params,
        name="finish",
    )(pos, gate, local, inside, states, modes_gain, decay)
    with jax.named_scope("result_swap"):
        both = lax.all_to_all(out, "c", 0, 0, tiled=True)
        return both.transpose(1, 0, 2).reshape(rows, group)


def solution(mesh):
    split = Mesh(mesh.devices.reshape(4, 4, 2, 2, 4), AXES)
    return jax.shard_map(
        body,
        mesh=split,
        in_specs=(
            P(CTX, CH),
            P(CTX, None, CH),
            P(None, None, CH),
            P(None, CH),
            P(None, CH),
            P(CH),
        ),
        out_specs=P(CTX, CH),
        check_vma=False,
    )
```

```python
import functools

import jax
import jax.numpy as jnp
from jax import lax
from jax.experimental import pallas as pl
from jax.experimental.pallas import tpu as pltpu
from jax.sharding import Mesh
from jax.sharding import PartitionSpec as P

AXES = ("y", "h", "c", "l", "x")
CTX = ("y", "h", "c")
CH = ("l", "x")
F32 = jnp.float32
BF16 = jnp.bfloat16
HALO = 16
SWAP = [(0, 1), (1, 0)]
SUB = 8


def shifted(array, axis, step):
    n = lax.axis_size(axis)
    return lax.ppermute(array, axis, [(i, (i + step) % n) for i in range(n)])


def in_order(mine_first, mine, theirs, axis):
    first, second = jnp.where(mine_first, mine, theirs), jnp.where(mine_first, theirs, mine)
    return jnp.concatenate([first, second], axis)


def both_ways(piece, axis):
    return shifted(piece, axis, 1), shifted(piece, axis, -1)


def onward(behind, ahead, axis):
    half = behind.shape[0] // 2
    return shifted(behind[:half], axis, 1), shifted(ahead[half:], axis, -1)


def fetched(sizes, pos, near, swapped, pieces, blocks, tokv, wv, sem):
    rows, depth, width, modes, seq = sizes
    k = depth // 16
    lines = rows + 2 * HALO
    copies, at, seen = [], 0, set()

    def add(source, target):
        copies.append(pltpu.make_async_copy(source, target, sem.at[len(copies)]))
        return copies[-1]

    for piece, first, n, dy, dh, skip in blocks:
        add(pieces[piece].at[pl.ds(first, n), :], wv.at[pl.ds(at + skip, n), :]).start()
        if (dy, dh) not in seen:
            seen.add((dy, dh))
            ys, hs = lax.rem(pos[1] - dy + 4, 4), lax.rem(pos[2] - dh + 4, 4)
            ch = 2 * ys + lax.div(hs, 2)
            lanes = pl.ds(pl.multiple_of(lax.rem(hs, 2) * k, k), k)
            x = lax.rem(ch, 4)
            other = lax.rem(lax.div(ch, 4) + pos[4], 2)
            to = pl.ds(at, k)
            line = pl.multiple_of(x * lines + HALO * other, HALO)
            add(swapped.at[pl.ds(line, HALO), lanes], tokv.at[pl.ds(0, HALO), to]).start()
            for core in range(2):
                target = tokv.at[pl.ds(HALO + core * rows, rows), to]
                line = pl.multiple_of((4 * core + x) * rows, rows)
                copy = add(near.at[pl.ds(line, rows), lanes], target)
                pl.when(other == 0)(copy.start)
                line = pl.multiple_of((4 * core + x) * lines + 2 * HALO, HALO)
                source = swapped.at[pl.ds(line, rows), lanes]
                copy = pltpu.make_async_copy(source, target, sem.at[len(copies) - 1])
                pl.when(other == 1)(copy.start)
        if skip + n == k:
            at += k
    return copies


def project_kernel(sizes, blocks, *refs):
    rows, depth, width, modes, seq = sizes
    pos, near, swapped, *pieces = refs[:-4]
    sums, tokv, wv, sem = refs[-4:]
    for copy in fetched(sizes, pos, near, swapped, pieces, blocks, tokv, wv, sem):
        copy.wait()

    @pl.loop(0, 3)
    def _(j):
        cols = pl.ds(pl.multiple_of(j * width, width), width)
        part = jnp.dot(tokv[...], wv[:, cols], preferred_element_type=F32)
        for lh in range(width // 128):
            sums[j * (width // 128) + lh] = part[:, lh * 128 : lh * 128 + 128]


def state_kernel(sizes, blocks, *refs):
    rows, depth, width, modes, seq = sizes
    pos, near, swapped, *pieces = refs[:-11]
    sums, taps, decay, gate, product, inside, state, tokv, wv, acc, sem = refs[-11:]
    c = pos[3]
    for copy in fetched(sizes, pos, near, swapped, pieces, blocks, tokv, wv, sem):
        copy.wait()

    @pl.loop(0, 3)
    def _(j):
        cols = pl.ds(pl.multiple_of(j * width, width), width)
        part = jnp.dot(tokv[...], wv[:, cols], preferred_element_type=F32)
        for lh in range(width // 128):
            chunk = j * (width // 128) + lh
            new = part[:, lh * 128 : lh * 128 + 128]
            acc[chunk] = (sums[chunk] + new).astype(BF16).astype(F32)

    steps = 2 * rows // SUB
    for lh in range(width // 128):
        mine = pl.ds(pl.multiple_of(c * width + lh * 128, 128), 128)
        lanes = pl.ds(lh * 128, 128)
        weights = [[taps[lag, j : j + 1, mine] for j in range(3)] for lag in range(3)]
        rates = [jnp.broadcast_to(decay[m : m + 1, mine] / seq, (SUB, 128)) for m in range(modes)]
        factors = [jnp.exp(-rate) for rate in rates]

        def read(start):
            return [
                acc[j * (width // 128) + lh, pl.ds(start, SUB, stride=steps), :]
                for j in range(3)
            ]

        def step(t, carry):
            before, last, states = carry
            now = read(HALO + t)
            f = [
                weights[0][j] * now[j] + weights[1][j] * last[j] + weights[2][j] * before[j]
                for j in range(3)
            ]
            p = f[1] * f[2]
            gate[t, :, lanes] = f[0]
            product[t, :, lanes] = p
            return last, now, [a * s + p for a, s in zip(factors, states)]

        zero = jnp.zeros((SUB, 128), F32)
        carry = (read(HALO - 2), read(HALO - 1), [zero] * modes)
        states = lax.fori_loop(0, steps, step, carry, unroll=4)[2]
        line = lax.broadcasted_iota(jnp.int32, (SUB, 128), 0)

        def later(value, by):
            return jnp.where(line >= by, pltpu.roll(value, by, 0), 0.0)

        for m in range(modes):
            s = states[m]
            for by in (1, 2, 4):
                s = s + jnp.exp(-float(steps * by) * rates[m]) * later(s, by)
            inside[m, :, lanes] = later(s, 1)
            state[m : m + 1, lanes] = s[SUB - 1 :]


def local_kernel(sizes, pos, product, gain, decay, skip, local):
    rows, depth, width, modes, seq = sizes
    c = pos[3]
    steps = 2 * rows // SUB
    for lh in range(width // 128):
        mine = pl.ds(pl.multiple_of(c * width + lh * 128, 128), 128)
        lanes = pl.ds(lh * 128, 128)
        rates = [jnp.broadcast_to(decay[m : m + 1, mine] / seq, (SUB, 128)) for m in range(modes)]
        factors = [jnp.exp(-rate) for rate in rates]
        heights = [gain[m : m + 1, mine] * jnp.sqrt(2.0 * rates[m]) for m in range(modes)]
        direct = jnp.broadcast_to(skip[:, mine], (SUB, 128))

        def step(t, states):
            p = product[t, :, lanes]
            states = [a * s + p for a, s in zip(factors, states)]
            parts = [w * s for w, s in zip(heights, states)]
            while len(parts) > 1:
                parts = [a + b for a, b in zip(parts[::2], parts[1::2])]
            local[t, :, lanes] = parts[0] + direct * p
            return states

        lax.fori_loop(0, steps, step, [jnp.zeros((SUB, 128), F32)] * modes, unroll=4)


def finish_kernel(sizes, pos, gate, local, inside, states, gain, decay, mine_out, their_out, start, whole):
    rows, depth, width, modes, seq = sizes
    rank, c = pos[0], pos[3]
    steps = 2 * rows // SUB
    length = 2 * rows
    for lh in range(width // 128):
        mine = pl.ds(pl.multiple_of(c * width + lh * 128, 128), 128)
        lanes = pl.ds(lh * 128, 128)
        over = jnp.exp(-float(length) * (decay[:, mine] / seq))
        entering = jnp.zeros((modes, 128), F32)
        for r in range(16):
            entering = jnp.where(r < rank, over * entering + states[r, :, lanes], entering)
        start[:, lanes] = entering
        line = lax.broadcasted_iota(jnp.int32, (SUB, 128), 0).astype(F32) * float(steps)
        factors, waves = [], []
        for m in range(modes):
            rate = jnp.broadcast_to(decay[m : m + 1, mine] / seq, (SUB, 128))
            factors.append(jnp.exp(-rate))
            height = gain[m : m + 1, mine] * jnp.sqrt(2.0 * rate)
            waves.append(height * (inside[m, :, lanes] + jnp.exp(-rate * line) * start[m : m + 1, lanes]))

        def step(t, waves):
            waves = [a * z for a, z in zip(factors, waves)]
            parts = waves
            while len(parts) > 1:
                parts = [a + b for a, b in zip(parts[::2], parts[1::2])]
            whole[lh, pl.ds(t, SUB, stride=steps), :] = gate[t, :, lanes] * (local[t, :, lanes] + parts[0])
            return waves

        lax.fori_loop(0, steps, step, waves, unroll=4)
        for out, core in ((mine_out, c), (their_out, 1 - c)):
            line = pl.ds(pl.multiple_of(core * rows, rows), rows)
            out[:, lanes] = whole[lh, line, :].astype(BF16)


def body(tokens, w_in, taps, modes_gain, decay, skip):
    rows = tokens.shape[0]
    group = w_in.shape[2]
    width = group // 2
    k = w_in.shape[0]
    modes = decay.shape[0]
    depth = tokens.shape[1] * 8
    seq = rows * 32
    sizes = (rows, depth, width, modes, seq)
    y, h, c = (lax.axis_index(a) for a in CTX)
    pos = jnp.stack([y * 4 + h, y, h, c, lax.axis_index("l")]).astype(jnp.int32)

    tie = lax.optimization_barrier
    with jax.named_scope("weight_gather"):
        halves = w_in.reshape(k, 3, 2, width).transpose(2, 0, 1, 3).reshape(2, k, 3 * width)
        mine = lax.dynamic_index_in_dim(halves, c, 0, keepdims=False)
        theirs = lax.ppermute(lax.dynamic_index_in_dim(halves, 1 - c, 0, keepdims=False), "c", SWAP)
        own = in_order(c == 0, mine, theirs, 0)
        tail, own = tie((tokens[rows - HALO :], own))
    with jax.named_scope("token_swap"):
        other = lax.ppermute(tokens, "l", SWAP)
        route = [(4 * r + 2 + side, 4 * r + 4 + side) for r in range(15) for side in range(2)]
        halo = lax.ppermute(tail, (*CTX, "l"), route)
        other_halo = lax.ppermute(tail, (*CTX, "l"), [(i, j ^ 1) for i, j in route])
    with jax.named_scope("weight_rings"):
        farther = shifted(own, "y", 2)
        far = both_ways(own, "y")
        beside = both_ways(own, "h")
    first = (halo, other_halo, other, farther, far, beside)
    halo, other_halo, other, farther, far, beside = tie(first)
    with jax.named_scope("token_gather"):
        near = lax.all_gather(tokens, ("c", "x"), axis=0, tiled=True)
        wide = jnp.concatenate([halo, other_halo, other], 0)
        swapped = lax.all_gather(wide, ("c", "x"), axis=0, tiled=True)
    with jax.named_scope("weight_rings"):
        two, half = 2 * k, k
        pair = jnp.concatenate(beside, 0)
        far_pair, opposite = both_ways(pair, "y"), onward(*beside, "h")
        far_pair, opposite = tie((far_pair, opposite))
        opposite = jnp.concatenate(opposite, 0)
        last = shifted(opposite, "y", 2)
        farther_pair = onward(*far_pair, "y")
        firsts = jnp.concatenate([p[:half] for p in far_pair], 0)
        seconds = jnp.concatenate([p[two + half :] for p in far_pair], 0)
        far_opposite = shifted(firsts, "h", 1), shifted(seconds, "h", -1)

    early = [own, pair, opposite, *far, *far_pair, farther]
    early_blocks = [(0, 0, two, 0, 0, 0), (1, 0, two, 0, 1, 0), (1, two, two, 0, -1, 0), (2, 0, two, 0, 2, 0)]
    for side, dy in enumerate((1, -1)):
        early_blocks += [
            (3 + side, 0, two, dy, 0, 0),
            (5 + side, 0, two, dy, 1, 0),
            (5 + side, two, two, dy, -1, 0),
        ]
    early_blocks += [(7, 0, two, 2, 0, 0)]
    late = [*farther_pair, *far_opposite, last]
    late_blocks = [
        (0, 0, two, 2, 1, 0),
        (1, 0, two, 2, -1, 0),
        (2, 0, half, 1, 2, 0),
        (3, 0, half, 1, 2, half),
        (2, half, half, -1, 2, 0),
        (3, half, half, -1, 2, half),
        (4, 0, two, 2, 2, 0),
    ]

    vmem = pl.BlockSpec(memory_space=pltpu.VMEM)
    smem = pl.BlockSpec(memory_space=pltpu.SMEM)
    hbm = pl.BlockSpec(memory_space=pltpu.HBM)
    block = (2 * rows // SUB, SUB, width)
    full = jax.ShapeDtypeStruct(block, F32)
    lines = 2 * rows + HALO
    chunks = (3 * width // 128, lines, 128)

    def held(n):
        return [pltpu.VMEM((lines, n * two), BF16), pltpu.VMEM((n * two, 3 * width), BF16)]

    def sems(blocks, n):
        return pltpu.SemaphoreType.DMA((len(blocks) + 3 * n,))

    sums = pl.pallas_call(
        functools.partial(project_kernel, sizes, early_blocks),
        out_shape=jax.ShapeDtypeStruct(chunks, F32),
        in_specs=[smem] + [hbm] * (2 + len(early)),
        out_specs=vmem,
        scratch_shapes=[*held(11), sems(early_blocks, 11)],
        compiler_params=pltpu.CompilerParams(vmem_limit_bytes=14 * 2**20),
        cost_estimate=pl.CostEstimate(
            flops=2 * lines * 11 * two * 3 * width, bytes_accessed=9_000_000, transcendentals=0
        ),
        name="project",
    )(pos, near, swapped, *early)
    params = pltpu.CompilerParams(vmem_limit_bytes=12 * 2**20)
    gate, product, inside, state = pl.pallas_call(
        functools.partial(state_kernel, sizes, late_blocks),
        out_shape=(
            full,
            full,
            jax.ShapeDtypeStruct((modes, SUB, width), F32),
            jax.ShapeDtypeStruct((modes, width), F32),
        ),
        in_specs=[smem] + [hbm] * (2 + len(late)) + [vmem] * 3,
        out_specs=(vmem,) * 4,
        scratch_shapes=[*held(5), pltpu.VMEM(chunks, F32), sems(late_blocks, 5)],
        compiler_params=params,
        name="states",
    )(pos, near, swapped, *late, sums, taps, decay)

    with jax.named_scope("state_exchange"):
        states = lax.all_to_all(
            jnp.broadcast_to(state, (16, *state.shape)), ("y", "h"), 0, 0, tiled=True
        )
    local = pl.pallas_call(
        functools.partial(local_kernel, sizes),
        out_shape=full,
        in_specs=[smem] + [vmem] * 4,
        out_specs=vmem,
        compiler_params=params,
        cost_estimate=pl.CostEstimate(flops=20_000_000, bytes_accessed=1_000_000, transcendentals=0),
        name="local",
    )(pos, product, modes_gain, decay, skip.reshape(1, group))
    mine, theirs = pl.pallas_call(
        functools.partial(finish_kernel, sizes),
        out_shape=(jax.ShapeDtypeStruct((rows, width), BF16),) * 2,
        in_specs=[smem] + [vmem] * 6,
        out_specs=(vmem, vmem),
        scratch_shapes=[pltpu.VMEM((modes, width), F32), pltpu.VMEM((width // 128, 2 * rows, 128), F32)],
        compiler_params=params,
        name="finish",
    )(pos, gate, local, inside, states, modes_gain, decay)
    with jax.named_scope("result_swap"):
        return in_order(c == 0, mine, lax.ppermute(theirs, "c", SWAP), 1)


def solution(mesh):
    split = Mesh(mesh.devices.reshape(4, 4, 2, 2, 4), AXES)
    return jax.shard_map(
        body,
        mesh=split,
        in_specs=(
            P(CTX, CH),
            P(CTX, None, CH),
            P(None, None, CH),
            P(None, CH),
            P(None, CH),
            P(CH),
        ),
        out_specs=P(CTX, CH),
        check_vma=False,
    )
```

```python
import functools

import jax
import jax.numpy as jnp
from jax import lax
from jax.experimental import pallas as pl
from jax.experimental.pallas import tpu as pltpu
from jax.sharding import Mesh
from jax.sharding import PartitionSpec as P

AXES = ("y", "h", "c", "l", "x")
CTX = ("y", "h", "c")
CH = ("l", "x")
F32 = jnp.float32
BF16 = jnp.bfloat16
HALO = 16
SWAP = [(0, 1), (1, 0)]
SUB = 8


def shifted(array, axis, step):
    n = lax.axis_size(axis)
    return lax.ppermute(array, axis, [(i, (i + step) % n) for i in range(n)])


def in_order(mine_first, mine, theirs, axis):
    first, second = jnp.where(mine_first, mine, theirs), jnp.where(mine_first, theirs, mine)
    return jnp.concatenate([first, second], axis)


def both_ways(piece, axis):
    return shifted(piece, axis, 1), shifted(piece, axis, -1)


def onward(behind, ahead, axis):
    half = behind.shape[0] // 2
    return shifted(behind[:half], axis, 1), shifted(ahead[half:], axis, -1)


def token_copies(sizes, pos, near, swapped, runs, tokv, sem):
    rows, depth, width, modes, seq = sizes
    k = depth // 16
    lines = rows + 2 * HALO
    copies, at = [], 0

    def add(source, target):
        copies.append(pltpu.make_async_copy(source, target, sem.at[len(copies)]))
        return copies[-1]

    for dy, dh, skip, n in runs:
        ys, hs = lax.rem(pos[1] - dy + 4, 4), lax.rem(pos[2] - dh + 4, 4)
        ch = 2 * ys + lax.div(hs, 2)
        lanes = pl.ds(pl.multiple_of(lax.rem(hs, 2) * k + skip, 128), n)
        x = lax.rem(ch, 4)
        other = lax.rem(lax.div(ch, 4) + pos[4], 2)
        to = pl.ds(at, n)
        line = pl.multiple_of(x * lines + HALO * other, HALO)
        add(swapped.at[pl.ds(line, HALO), lanes], tokv.at[pl.ds(0, HALO), to]).start()
        for core in range(2):
            target = tokv.at[pl.ds(HALO + core * rows, rows), to]
            line = pl.multiple_of((4 * core + x) * rows, rows)
            copy = add(near.at[pl.ds(line, rows), lanes], target)
            pl.when(other == 0)(copy.start)
            line = pl.multiple_of((4 * core + x) * lines + 2 * HALO, HALO)
            source = swapped.at[pl.ds(line, rows), lanes]
            copy = pltpu.make_async_copy(source, target, sem.at[len(copies) - 1])
            pl.when(other == 1)(copy.start)
        at += n
    return copies


def project_kernel(sizes, early, late, *refs):
    rows, depth, width, modes, seq = sizes
    pos, near, swapped, *pieces = refs[:-7]
    sums, late_tok, tokv, wv, tok_sem, late_sem, w_sem = refs[-7:]
    copies, at = [], 0
    for number, piece in enumerate(pieces):
        n = piece.shape[0]
        copies.append(pltpu.make_async_copy(piece, wv.at[pl.ds(at, n), :], w_sem.at[number]))
        copies[-1].start()
        at += n
    copies += token_copies(sizes, pos, near, swapped, early, tokv, tok_sem)
    late_copies = token_copies(sizes, pos, near, swapped, late, late_tok, late_sem)
    for copy in copies:
        copy.wait()

    @pl.loop(0, 3)
    def _(j):
        cols = pl.ds(pl.multiple_of(j * width, width), width)
        part = jnp.dot(tokv[...], wv[:, cols], preferred_element_type=F32)
        for lh in range(width // 128):
            sums[j * (width // 128) + lh] = part[:, lh * 128 : lh * 128 + 128]

    for copy in late_copies:
        copy.wait()


def state_kernel(sizes, *refs):
    rows, depth, width, modes, seq = sizes
    pos, late_tok, *pieces = refs[:-8]
    sums, taps, decay, gate, product, inside, state, acc = refs[-8:]
    c = pos[3]
    k = depth // 16

    @pl.loop(0, 3)
    def _(j):
        cols = pl.ds(pl.multiple_of(j * width, width), width)
        part = sum(
            jnp.dot(late_tok[:, i * k : i * k + k], piece[:, cols], preferred_element_type=F32)
            for i, piece in enumerate(pieces)
        )
        for lh in range(width // 128):
            chunk = j * (width // 128) + lh
            new = part[:, lh * 128 : lh * 128 + 128]
            acc[chunk] = (sums[chunk] + new).astype(BF16).astype(F32)

    steps = 2 * rows // SUB
    for lh in range(width // 128):
        mine = pl.ds(pl.multiple_of(c * width + lh * 128, 128), 128)
        lanes = pl.ds(lh * 128, 128)
        weights = [[taps[lag, j : j + 1, mine] for j in range(3)] for lag in range(3)]
        rates = [jnp.broadcast_to(decay[m : m + 1, mine] / seq, (SUB, 128)) for m in range(modes)]
        factors = [jnp.exp(-rate) for rate in rates]

        def read(start):
            return [
                acc[j * (width // 128) + lh, pl.ds(start, SUB, stride=steps), :]
                for j in range(3)
            ]

        def step(t, carry):
            before, last, states = carry
            now = read(HALO + t)
            f = [
                weights[0][j] * now[j] + weights[1][j] * last[j] + weights[2][j] * before[j]
                for j in range(3)
            ]
            p = f[1] * f[2]
            gate[t, :, lanes] = f[0]
            product[t, :, lanes] = p
            return last, now, [a * s + p for a, s in zip(factors, states)]

        zero = jnp.zeros((SUB, 128), F32)
        carry = (read(HALO - 2), read(HALO - 1), [zero] * modes)
        states = lax.fori_loop(0, steps, step, carry, unroll=4)[2]
        line = lax.broadcasted_iota(jnp.int32, (SUB, 128), 0)

        def later(value, by):
            return jnp.where(line >= by, pltpu.roll(value, by, 0), 0.0)

        for m in range(modes):
            s = states[m]
            for by in (1, 2, 4):
                s = s + jnp.exp(-float(steps * by) * rates[m]) * later(s, by)
            inside[m, :, lanes] = later(s, 1)
            state[m : m + 1, lanes] = s[SUB - 1 :]


def local_kernel(sizes, pos, product, gain, decay, skip, local):
    rows, depth, width, modes, seq = sizes
    c = pos[3]
    steps = 2 * rows // SUB
    for lh in range(width // 128):
        mine = pl.ds(pl.multiple_of(c * width + lh * 128, 128), 128)
        lanes = pl.ds(lh * 128, 128)
        rates = [jnp.broadcast_to(decay[m : m + 1, mine] / seq, (SUB, 128)) for m in range(modes)]
        factors = [jnp.exp(-rate) for rate in rates]
        heights = [gain[m : m + 1, mine] * jnp.sqrt(2.0 * rates[m]) for m in range(modes)]
        direct = jnp.broadcast_to(skip[:, mine], (SUB, 128))

        def step(t, states):
            p = product[t, :, lanes]
            states = [a * s + p for a, s in zip(factors, states)]
            parts = [w * s for w, s in zip(heights, states)]
            while len(parts) > 1:
                parts = [a + b for a, b in zip(parts[::2], parts[1::2])]
            local[t, :, lanes] = parts[0] + direct * p
            return states

        lax.fori_loop(0, steps, step, [jnp.zeros((SUB, 128), F32)] * modes, unroll=4)


def finish_kernel(sizes, pos, gate, local, inside, states, gain, decay, mine_out, their_out, start, whole):
    rows, depth, width, modes, seq = sizes
    rank, c = pos[0], pos[3]
    steps = 2 * rows // SUB
    length = 2 * rows
    for lh in range(width // 128):
        mine = pl.ds(pl.multiple_of(c * width + lh * 128, 128), 128)
        lanes = pl.ds(lh * 128, 128)
        over = jnp.exp(-float(length) * (decay[:, mine] / seq))
        entering = jnp.zeros((modes, 128), F32)
        for r in range(16):
            entering = jnp.where(r < rank, over * entering + states[r, :, lanes], entering)
        start[:, lanes] = entering
        line = lax.broadcasted_iota(jnp.int32, (SUB, 128), 0).astype(F32) * float(steps)
        factors, waves = [], []
        for m in range(modes):
            rate = jnp.broadcast_to(decay[m : m + 1, mine] / seq, (SUB, 128))
            factors.append(jnp.exp(-rate))
            height = gain[m : m + 1, mine] * jnp.sqrt(2.0 * rate)
            waves.append(height * (inside[m, :, lanes] + jnp.exp(-rate * line) * start[m : m + 1, lanes]))

        def step(t, waves):
            waves = [a * z for a, z in zip(factors, waves)]
            parts = waves
            while len(parts) > 1:
                parts = [a + b for a, b in zip(parts[::2], parts[1::2])]
            whole[lh, pl.ds(t, SUB, stride=steps), :] = gate[t, :, lanes] * (local[t, :, lanes] + parts[0])
            return waves

        lax.fori_loop(0, steps, step, waves, unroll=4)
        for out, core in ((mine_out, c), (their_out, 1 - c)):
            line = pl.ds(pl.multiple_of(core * rows, rows), rows)
            out[:, lanes] = whole[lh, line, :].astype(BF16)


def body(tokens, w_in, taps, modes_gain, decay, skip):
    rows = tokens.shape[0]
    group = w_in.shape[2]
    width = group // 2
    k = w_in.shape[0]
    modes = decay.shape[0]
    depth = tokens.shape[1] * 8
    seq = rows * 32
    sizes = (rows, depth, width, modes, seq)
    y, h, c = (lax.axis_index(a) for a in CTX)
    pos = jnp.stack([y * 4 + h, y, h, c, lax.axis_index("l")]).astype(jnp.int32)

    tie = lax.optimization_barrier
    with jax.named_scope("weight_gather"):
        halves = w_in.reshape(k, 3, 2, width).transpose(2, 0, 1, 3).reshape(2, k, 3 * width)
        mine = lax.dynamic_index_in_dim(halves, c, 0, keepdims=False)
        theirs = lax.ppermute(lax.dynamic_index_in_dim(halves, 1 - c, 0, keepdims=False), "c", SWAP)
        own = in_order(c == 0, mine, theirs, 0)
        tail, own = tie((tokens[rows - HALO :], own))
    with jax.named_scope("token_swap"):
        other = lax.ppermute(tokens, "l", SWAP)
        route = [(4 * r + 2 + side, 4 * r + 4 + side) for r in range(15) for side in range(2)]
        halo = lax.ppermute(tail, (*CTX, "l"), route)
        other_halo = lax.ppermute(tail, (*CTX, "l"), [(i, j ^ 1) for i, j in route])
    with jax.named_scope("weight_rings"):
        farther = shifted(own, "y", 2)
        far = both_ways(own, "y")
        beside = both_ways(own, "h")
    first = (halo, other_halo, other, farther, far, beside)
    halo, other_halo, other, farther, far, beside = tie(first)
    with jax.named_scope("token_gather"):
        near = lax.all_gather(tokens, ("c", "x"), axis=0, tiled=True)
        wide = jnp.concatenate([halo, other_halo, other], 0)
        swapped = lax.all_gather(wide, ("c", "x"), axis=0, tiled=True)
    with jax.named_scope("weight_rings"):
        two, half = 2 * k, k
        pair = jnp.concatenate(beside, 0)
        far_pair, opposite = both_ways(pair, "y"), onward(pair[:two], pair[two:], "h")
        far_pair, opposite = tie((far_pair, opposite))
        opposite = jnp.concatenate(opposite, 0)
        last = shifted(opposite, "y", 2)
        farther_pair = onward(*far_pair, "y")
        firsts = jnp.concatenate([p[:half] for p in far_pair], 0)
        seconds = jnp.concatenate([p[two + half :] for p in far_pair], 0)
        far_opposite = shifted(firsts, "h", 1), shifted(seconds, "h", -1)

    early = [own, pair, opposite]
    early_runs = [(0, dh, 0, two) for dh in (0, 1, -1, 2)]
    for side, dy in enumerate((1, -1)):
        early += [far[side], far_pair[side]]
        early_runs += [(dy, dh, 0, two) for dh in (0, 1, -1)]
    early += [farther]
    early_runs += [(2, 0, 0, two)]
    late = [*farther_pair, *far_opposite, last]
    late_runs = [(2, 1, 0, two), (2, -1, 0, two)]
    late_runs += [(dy, 2, skip, half) for skip in (0, half) for dy in (1, -1)]
    late_runs += [(2, 2, 0, two)]

    vmem = pl.BlockSpec(memory_space=pltpu.VMEM)
    smem = pl.BlockSpec(memory_space=pltpu.SMEM)
    hbm = pl.BlockSpec(memory_space=pltpu.HBM)
    block = (2 * rows // SUB, SUB, width)
    full = jax.ShapeDtypeStruct(block, F32)
    lines = 2 * rows + HALO
    chunks = (3 * width // 128, lines, 128)

    def dma(n):
        return pltpu.SemaphoreType.DMA((n,))

    sums, late_tok = pl.pallas_call(
        functools.partial(project_kernel, sizes, early_runs, late_runs),
        out_shape=(
            jax.ShapeDtypeStruct(chunks, F32),
            jax.ShapeDtypeStruct((lines, 5 * two), BF16),
        ),
        in_specs=[smem] + [hbm] * (2 + len(early)),
        out_specs=(vmem, vmem),
        scratch_shapes=[
            pltpu.VMEM((lines, 11 * two), BF16),
            pltpu.VMEM((11 * two, 3 * width), BF16),
            dma(3 * len(early_runs)),
            dma(3 * len(late_runs)),
            dma(len(early)),
        ],
        compiler_params=pltpu.CompilerParams(vmem_limit_bytes=14 * 2**20),
        cost_estimate=pl.CostEstimate(
            flops=2 * lines * 11 * two * 3 * width, bytes_accessed=9_000_000, transcendentals=0
        ),
        name="project",
    )(pos, near, swapped, *early)
    params = pltpu.CompilerParams(vmem_limit_bytes=8 * 2**20)
    gate, product, inside, state = pl.pallas_call(
        functools.partial(state_kernel, sizes),
        out_shape=(
            full,
            full,
            jax.ShapeDtypeStruct((modes, SUB, width), F32),
            jax.ShapeDtypeStruct((modes, width), F32),
        ),
        in_specs=[smem] + [vmem] * (4 + len(late)),
        out_specs=(vmem,) * 4,
        scratch_shapes=[pltpu.VMEM(chunks, F32)],
        compiler_params=params,
        name="states",
    )(pos, late_tok, *late, sums, taps, decay)

    with jax.named_scope("state_exchange"):
        states = lax.all_to_all(
            jnp.broadcast_to(state, (16, *state.shape)), ("y", "h"), 0, 0, tiled=True
        )
    local = pl.pallas_call(
        functools.partial(local_kernel, sizes),
        out_shape=full,
        in_specs=[smem] + [vmem] * 4,
        out_specs=vmem,
        compiler_params=params,
        cost_estimate=pl.CostEstimate(flops=20_000_000, bytes_accessed=1_000_000, transcendentals=0),
        name="local",
    )(pos, product, modes_gain, decay, skip.reshape(1, group))
    mine, theirs = pl.pallas_call(
        functools.partial(finish_kernel, sizes),
        out_shape=(jax.ShapeDtypeStruct((rows, width), BF16),) * 2,
        in_specs=[smem] + [vmem] * 6,
        out_specs=(vmem, vmem),
        scratch_shapes=[pltpu.VMEM((modes, width), F32), pltpu.VMEM((width // 128, 2 * rows, 128), F32)],
        compiler_params=params,
        name="finish",
    )(pos, gate, local, inside, states, modes_gain, decay)
    with jax.named_scope("result_swap"):
        return in_order(c == 0, mine, lax.ppermute(theirs, "c", SWAP), 1)


def solution(mesh):
    split = Mesh(mesh.devices.reshape(4, 4, 2, 2, 4), AXES)
    return jax.shard_map(
        body,
        mesh=split,
        in_specs=(
            P(CTX, CH),
            P(CTX, None, CH),
            P(None, None, CH),
            P(None, CH),
            P(None, CH),
            P(CH),
        ),
        out_specs=P(CTX, CH),
        check_vma=False,
    )
```

```python
import functools

import jax
import jax.numpy as jnp
from jax import lax
from jax.experimental import pallas as pl
from jax.experimental.pallas import tpu as pltpu
from jax.sharding import Mesh
from jax.sharding import PartitionSpec as P

AXES = ("y", "h", "c", "l", "x")
CTX = ("y", "h", "c")
CH = ("l", "x")
F32 = jnp.float32
BF16 = jnp.bfloat16
HALO = 16
SWAP = [(0, 1), (1, 0)]
SUB = 8


def shifted(array, axis, step):
    n = lax.axis_size(axis)
    return lax.ppermute(array, axis, [(i, (i + step) % n) for i in range(n)])


def in_order(mine_first, mine, theirs, axis):
    first, second = jnp.where(mine_first, mine, theirs), jnp.where(mine_first, theirs, mine)
    return jnp.concatenate([first, second], axis)


def both_ways(piece, axis):
    return shifted(piece, axis, 1), shifted(piece, axis, -1)


def relay_kernel(moves, count, *refs):
    sources, targets, sem = refs[:count], refs[count:-1], refs[-1]
    copies = []
    for number, (source, first, n, target, at) in enumerate(moves):
        copies.append(
            pltpu.make_async_copy(
                sources[source].at[pl.ds(first, n), :],
                targets[target].at[pl.ds(at, n), :],
                sem.at[number],
            )
        )
        copies[-1].start()
    for copy in copies:
        copy.wait()


def relayed(sources, moves, name):
    heights = [max(at + n for _, _, n, target, at in moves if target == t) for t in range(1 + max(m[3] for m in moves))]
    anywhere = pl.BlockSpec(memory_space=pl.ANY)
    return pl.pallas_call(
        functools.partial(relay_kernel, moves, len(sources)),
        out_shape=[jax.ShapeDtypeStruct((h, sources[0].shape[1]), sources[0].dtype) for h in heights],
        in_specs=[anywhere] * len(sources),
        out_specs=[anywhere] * len(heights),
        scratch_shapes=[pltpu.SemaphoreType.DMA((len(moves),))],
        cost_estimate=pl.CostEstimate(flops=0, bytes_accessed=2_000_000, transcendentals=0),
        compiler_params=pltpu.CompilerParams(vmem_limit_bytes=2**20),
        name=name,
    )(*sources)


def token_copies(sizes, pos, near, swapped, runs, tokv, sem):
    rows, depth, width, modes, seq = sizes
    k = depth // 16
    lines = rows + 2 * HALO
    copies, at = [], 0

    def add(source, target):
        copies.append(pltpu.make_async_copy(source, target, sem.at[len(copies)]))
        return copies[-1]

    for dy, dh, skip, n in runs:
        ys, hs = lax.rem(pos[1] - dy + 4, 4), lax.rem(pos[2] - dh + 4, 4)
        ch = 2 * ys + lax.div(hs, 2)
        lanes = pl.ds(pl.multiple_of(lax.rem(hs, 2) * k + skip, 128), n)
        x = lax.rem(ch, 4)
        other = lax.rem(lax.div(ch, 4) + pos[4], 2)
        to = pl.ds(at, n)
        line = pl.multiple_of(x * lines + HALO * other, HALO)
        add(swapped.at[pl.ds(line, HALO), lanes], tokv.at[pl.ds(0, HALO), to]).start()
        for core in range(2):
            target = tokv.at[pl.ds(HALO + core * rows, rows), to]
            line = pl.multiple_of((4 * core + x) * rows, rows)
            copy = add(near.at[pl.ds(line, rows), lanes], target)
            pl.when(other == 0)(copy.start)
            line = pl.multiple_of((4 * core + x) * lines + 2 * HALO, HALO)
            source = swapped.at[pl.ds(line, rows), lanes]
            copy = pltpu.make_async_copy(source, target, sem.at[len(copies) - 1])
            pl.when(other == 1)(copy.start)
        at += n
    return copies


def project_kernel(sizes, early, late, *refs):
    rows, depth, width, modes, seq = sizes
    pos, near, swapped, *pieces = refs[:-7]
    sums, late_tok, tokv, wv, tok_sem, late_sem, w_sem = refs[-7:]
    copies, at = [], 0
    for number, piece in enumerate(pieces):
        n = piece.shape[0]
        copies.append(pltpu.make_async_copy(piece, wv.at[pl.ds(at, n), :], w_sem.at[number]))
        copies[-1].start()
        at += n
    copies += token_copies(sizes, pos, near, swapped, early, tokv, tok_sem)
    late_copies = token_copies(sizes, pos, near, swapped, late, late_tok, late_sem)
    for copy in copies:
        copy.wait()

    @pl.loop(0, 3)
    def _(j):
        cols = pl.ds(pl.multiple_of(j * width, width), width)
        part = jnp.dot(tokv[...], wv[:, cols], preferred_element_type=F32)
        for lh in range(width // 128):
            sums[j * (width // 128) + lh] = part[:, lh * 128 : lh * 128 + 128]

    for copy in late_copies:
        copy.wait()


def state_kernel(sizes, *refs):
    rows, depth, width, modes, seq = sizes
    pos, late_tok, *pieces = refs[:-9]
    sums, taps, decay, gate, product, inside, states_out, acc, state = refs[-9:]
    c = pos[3]
    k = depth // 16

    @pl.loop(0, 3)
    def _(j):
        cols = pl.ds(pl.multiple_of(j * width, width), width)
        part = sum(
            jnp.dot(late_tok[:, i * k : i * k + k], piece[:, cols], preferred_element_type=F32)
            for i, piece in enumerate(pieces)
        )
        for lh in range(width // 128):
            chunk = j * (width // 128) + lh
            new = part[:, lh * 128 : lh * 128 + 128]
            acc[chunk] = (sums[chunk] + new).astype(BF16).astype(F32)

    steps = 2 * rows // SUB
    for lh in range(width // 128):
        mine = pl.ds(pl.multiple_of(c * width + lh * 128, 128), 128)
        lanes = pl.ds(lh * 128, 128)
        weights = [[taps[lag, j : j + 1, mine] for j in range(3)] for lag in range(3)]
        rates = [jnp.broadcast_to(decay[m : m + 1, mine] / seq, (SUB, 128)) for m in range(modes)]
        factors = [jnp.exp(-rate) for rate in rates]

        def read(start):
            return [
                acc[j * (width // 128) + lh, pl.ds(start, SUB, stride=steps), :]
                for j in range(3)
            ]

        def step(t, carry):
            before, last, states = carry
            now = read(HALO + t)
            f = [
                weights[0][j] * now[j] + weights[1][j] * last[j] + weights[2][j] * before[j]
                for j in range(3)
            ]
            p = f[1] * f[2]
            gate[t, :, lanes] = f[0]
            product[t, :, lanes] = p
            return last, now, [a * s + p for a, s in zip(factors, states)]

        zero = jnp.zeros((SUB, 128), F32)
        carry = (read(HALO - 2), read(HALO - 1), [zero] * modes)
        states = lax.fori_loop(0, steps, step, carry, unroll=4)[2]
        line = lax.broadcasted_iota(jnp.int32, (SUB, 128), 0)

        def later(value, by):
            return jnp.where(line >= by, pltpu.roll(value, by, 0), 0.0)

        for m in range(modes):
            s = states[m]
            for by in (1, 2, 4):
                s = s + jnp.exp(-float(steps * by) * rates[m]) * later(s, by)
            inside[m, :, lanes] = later(s, 1)
            state[m : m + 1, lanes] = s[SUB - 1 :]
    for r in range(16):
        states_out[r] = state[...]


def local_kernel(sizes, pos, product, gain, decay, skip, local):
    rows, depth, width, modes, seq = sizes
    c = pos[3]
    steps = 2 * rows // SUB
    for lh in range(width // 128):
        mine = pl.ds(pl.multiple_of(c * width + lh * 128, 128), 128)
        lanes = pl.ds(lh * 128, 128)
        rates = [jnp.broadcast_to(decay[m : m + 1, mine] / seq, (SUB, 128)) for m in range(modes)]
        factors = [jnp.exp(-rate) for rate in rates]
        heights = [gain[m : m + 1, mine] * jnp.sqrt(2.0 * rates[m]) for m in range(modes)]
        direct = jnp.broadcast_to(skip[:, mine], (SUB, 128))

        def step(t, states):
            p = product[t, :, lanes]
            states = [a * s + p for a, s in zip(factors, states)]
            parts = [w * s for w, s in zip(heights, states)]
            while len(parts) > 1:
                parts = [a + b for a, b in zip(parts[::2], parts[1::2])]
            local[t, :, lanes] = parts[0] + direct * p
            return states

        lax.fori_loop(0, steps, step, [jnp.zeros((SUB, 128), F32)] * modes, unroll=4)


def finish_kernel(sizes, pos, gate, local, inside, states, gain, decay, mine_out, their_out, start, whole):
    rows, depth, width, modes, seq = sizes
    rank, c = pos[0], pos[3]
    steps = 2 * rows // SUB
    length = 2 * rows
    for lh in range(width // 128):
        mine = pl.ds(pl.multiple_of(c * width + lh * 128, 128), 128)
        lanes = pl.ds(lh * 128, 128)
        over = jnp.exp(-float(length) * (decay[:, mine] / seq))
        entering = jnp.zeros((modes, 128), F32)
        for r in range(16):
            entering = jnp.where(r < rank, over * entering + states[r, :, lanes], entering)
        start[:, lanes] = entering
        line = lax.broadcasted_iota(jnp.int32, (SUB, 128), 0).astype(F32) * float(steps)
        factors, waves = [], []
        for m in range(modes):
            rate = jnp.broadcast_to(decay[m : m + 1, mine] / seq, (SUB, 128))
            factors.append(jnp.exp(-rate))
            height = gain[m : m + 1, mine] * jnp.sqrt(2.0 * rate)
            waves.append(height * (inside[m, :, lanes] + jnp.exp(-rate * line) * start[m : m + 1, lanes]))

        def step(t, waves):
            waves = [a * z for a, z in zip(factors, waves)]
            parts = waves
            while len(parts) > 1:
                parts = [a + b for a, b in zip(parts[::2], parts[1::2])]
            whole[lh, pl.ds(t, SUB, stride=steps), :] = gate[t, :, lanes] * (local[t, :, lanes] + parts[0])
            return waves

        lax.fori_loop(0, steps, step, waves, unroll=4)
        for out, core in ((mine_out, c), (their_out, 1 - c)):
            line = pl.ds(pl.multiple_of(core * rows, rows), rows)
            out[:, lanes] = whole[lh, line, :].astype(BF16)


def body(tokens, w_in, taps, modes_gain, decay, skip):
    rows = tokens.shape[0]
    group = w_in.shape[2]
    width = group // 2
    k = w_in.shape[0]
    modes = decay.shape[0]
    depth = tokens.shape[1] * 8
    seq = rows * 32
    sizes = (rows, depth, width, modes, seq)
    y, h, c = (lax.axis_index(a) for a in CTX)
    pos = jnp.stack([y * 4 + h, y, h, c, lax.axis_index("l")]).astype(jnp.int32)

    tie = lax.optimization_barrier
    with jax.named_scope("weight_gather"):
        halves = w_in.reshape(k, 3, 2, width).transpose(2, 0, 1, 3).reshape(2, k, 3 * width)
        mine = lax.dynamic_index_in_dim(halves, c, 0, keepdims=False)
        theirs = lax.ppermute(lax.dynamic_index_in_dim(halves, 1 - c, 0, keepdims=False), "c", SWAP)
        own = in_order(c == 0, mine, theirs, 0)
        tail, own = tie((tokens[rows - HALO :], own))
    with jax.named_scope("token_swap"):
        other = lax.ppermute(tokens, "l", SWAP)
        route = [(4 * r + 2 + side, 4 * r + 4 + side) for r in range(15) for side in range(2)]
        halo = lax.ppermute(tail, (*CTX, "l"), route)
        other_halo = lax.ppermute(tail, (*CTX, "l"), [(i, j ^ 1) for i, j in route])
    with jax.named_scope("weight_rings"):
        farther = shifted(own, "y", 2)
        far = both_ways(own, "y")
        beside = both_ways(own, "h")
    first = (halo, other_halo, other, farther, far, beside)
    halo, other_halo, other, farther, far, beside = tie(first)
    with jax.named_scope("token_gather"):
        near = lax.all_gather(tokens, ("c", "x"), axis=0, tiled=True)
        wide = jnp.concatenate([halo, other_halo, other], 0)
        swapped = lax.all_gather(wide, ("c", "x"), axis=0, tiled=True)
    with jax.named_scope("weight_rings"):
        two, half = 2 * k, k
        moves = [(0, 0, two, 0, 0), (1, 0, two, 0, two), (0, 0, half, 1, 0), (1, half, half, 2, 0)]
        pair, low, high = relayed(beside, moves, "relay_pair")
        far_pair = both_ways(pair, "y")
        opposite = shifted(low, "h", 1), shifted(high, "h", -1)
        far_pair, opposite = tie((far_pair, opposite))
        moves = [(0, 0, two, 0, 0), (1, two, two, 1, 0)]
        moves += [(side, 0, half, 2, side * half) for side in range(2)]
        moves += [(side, two + half, half, 3, side * half) for side in range(2)]
        moves += [(2 + side, 0, half, 4, side * half) for side in range(2)]
        behind, ahead, firsts, seconds, opposite = relayed([*far_pair, *opposite], moves, "relay_far")
        last = shifted(opposite, "y", 2)
        farther_pair = shifted(behind, "y", 1), shifted(ahead, "y", -1)
        far_opposite = shifted(firsts, "h", 1), shifted(seconds, "h", -1)

    early = [own, pair, opposite]
    early_runs = [(0, dh, 0, two) for dh in (0, 1, -1, 2)]
    for side, dy in enumerate((1, -1)):
        early += [far[side], far_pair[side]]
        early_runs += [(dy, dh, 0, two) for dh in (0, 1, -1)]
    early += [farther]
    early_runs += [(2, 0, 0, two)]
    late = [*farther_pair, *far_opposite, last]
    late_runs = [(2, 1, 0, two), (2, -1, 0, two)]
    late_runs += [(dy, 2, skip, half) for skip in (0, half) for dy in (1, -1)]
    late_runs += [(2, 2, 0, two)]

    vmem = pl.BlockSpec(memory_space=pltpu.VMEM)
    smem = pl.BlockSpec(memory_space=pltpu.SMEM)
    hbm = pl.BlockSpec(memory_space=pltpu.HBM)
    block = (2 * rows // SUB, SUB, width)
    full = jax.ShapeDtypeStruct(block, F32)
    lines = 2 * rows + HALO
    chunks = (3 * width // 128, lines, 128)

    def dma(n):
        return pltpu.SemaphoreType.DMA((n,))

    sums, late_tok = pl.pallas_call(
        functools.partial(project_kernel, sizes, early_runs, late_runs),
        out_shape=(
            jax.ShapeDtypeStruct(chunks, F32),
            jax.ShapeDtypeStruct((lines, 5 * two), BF16),
        ),
        in_specs=[smem] + [hbm] * (2 + len(early)),
        out_specs=(vmem, vmem),
        scratch_shapes=[
            pltpu.VMEM((lines, 11 * two), BF16),
            pltpu.VMEM((11 * two, 3 * width), BF16),
            dma(3 * len(early_runs)),
            dma(3 * len(late_runs)),
            dma(len(early)),
        ],
        compiler_params=pltpu.CompilerParams(vmem_limit_bytes=14 * 2**20),
        cost_estimate=pl.CostEstimate(
            flops=2 * lines * 11 * two * 3 * width, bytes_accessed=9_000_000, transcendentals=0
        ),
        name="project",
    )(pos, near, swapped, *early)
    params = pltpu.CompilerParams(vmem_limit_bytes=8 * 2**20)
    gate, product, inside, state = pl.pallas_call(
        functools.partial(state_kernel, sizes),
        out_shape=(
            full,
            full,
            jax.ShapeDtypeStruct((modes, SUB, width), F32),
            jax.ShapeDtypeStruct((16, modes, width), F32),
        ),
        in_specs=[smem] + [vmem] * (4 + len(late)),
        out_specs=(vmem,) * 4,
        scratch_shapes=[pltpu.VMEM(chunks, F32), pltpu.VMEM((modes, width), F32)],
        compiler_params=params,
        name="states",
    )(pos, late_tok, *late, sums, taps, decay)

    with jax.named_scope("state_exchange"):
        states = lax.all_to_all(state, ("y", "h"), 0, 0, tiled=True)
    local = pl.pallas_call(
        functools.partial(local_kernel, sizes),
        out_shape=full,
        in_specs=[smem] + [vmem] * 4,
        out_specs=vmem,
        compiler_params=params,
        cost_estimate=pl.CostEstimate(flops=20_000_000, bytes_accessed=1_000_000, transcendentals=0),
        name="local",
    )(pos, product, modes_gain, decay, skip.reshape(1, group))
    mine, theirs = pl.pallas_call(
        functools.partial(finish_kernel, sizes),
        out_shape=(jax.ShapeDtypeStruct((rows, width), BF16),) * 2,
        in_specs=[smem] + [vmem] * 6,
        out_specs=(vmem, vmem),
        scratch_shapes=[pltpu.VMEM((modes, width), F32), pltpu.VMEM((width // 128, 2 * rows, 128), F32)],
        compiler_params=params,
        name="finish",
    )(pos, gate, local, inside, states, modes_gain, decay)
    with jax.named_scope("result_swap"):
        return in_order(c == 0, mine, lax.ppermute(theirs, "c", SWAP), 1)


def solution(mesh):
    split = Mesh(mesh.devices.reshape(4, 4, 2, 2, 4), AXES)
    return jax.shard_map(
        body,
        mesh=split,
        in_specs=(
            P(CTX, CH),
            P(CTX, None, CH),
            P(None, None, CH),
            P(None, CH),
            P(None, CH),
            P(CH),
        ),
        out_specs=P(CTX, CH),
        check_vma=False,
    )
```

```python
import functools

import jax
import jax.numpy as jnp
from jax import lax
from jax.experimental import pallas as pl
from jax.experimental.pallas import tpu as pltpu
from jax.sharding import Mesh
from jax.sharding import PartitionSpec as P

AXES = ("y", "h", "c", "l", "x")
CTX = ("y", "h", "c")
CH = ("l", "x")
F32 = jnp.float32
BF16 = jnp.bfloat16
HALO = 16
SWAP = [(0, 1), (1, 0)]
SUB = 8


def shifted(array, axis, step):
    n = lax.axis_size(axis)
    return lax.ppermute(array, axis, [(i, (i + step) % n) for i in range(n)])


def in_order(mine_first, mine, theirs, axis):
    first, second = jnp.where(mine_first, mine, theirs), jnp.where(mine_first, theirs, mine)
    return jnp.concatenate([first, second], axis)


def both_ways(piece, axis):
    return shifted(piece, axis, 1), shifted(piece, axis, -1)


def relay_kernel(moves, count, *refs):
    sources, targets, sem = refs[:count], refs[count:-1], refs[-1]
    copies = []
    for number, (source, first, n, target, at) in enumerate(moves):
        copies.append(
            pltpu.make_async_copy(
                sources[source].at[pl.ds(first, n), :],
                targets[target].at[pl.ds(at, n), :],
                sem.at[number],
            )
        )
        copies[-1].start()
    for copy in copies:
        copy.wait()


def relayed(sources, moves, name):
    heights = [max(at + n for _, _, n, target, at in moves if target == t) for t in range(1 + max(m[3] for m in moves))]
    anywhere = pl.BlockSpec(memory_space=pl.ANY)
    return pl.pallas_call(
        functools.partial(relay_kernel, moves, len(sources)),
        out_shape=[jax.ShapeDtypeStruct((h, sources[0].shape[1]), sources[0].dtype) for h in heights],
        in_specs=[anywhere] * len(sources),
        out_specs=[anywhere] * len(heights),
        scratch_shapes=[pltpu.SemaphoreType.DMA((len(moves),))],
        cost_estimate=pl.CostEstimate(flops=0, bytes_accessed=2_000_000, transcendentals=0),
        compiler_params=pltpu.CompilerParams(vmem_limit_bytes=2**20),
        name=name,
    )(*sources)


def token_copies(sizes, pos, near, swapped, runs, tokv, sem):
    rows, depth, width, modes, seq = sizes
    k = depth // 16
    lines = rows + 2 * HALO
    copies, at = [], 0

    def add(source, target):
        copies.append(pltpu.make_async_copy(source, target, sem.at[len(copies)]))
        return copies[-1]

    for dy, dh, skip, n in runs:
        ys, hs = lax.rem(pos[1] - dy + 4, 4), lax.rem(pos[2] - dh + 4, 4)
        ch = 2 * ys + lax.div(hs, 2)
        lanes = pl.ds(pl.multiple_of(lax.rem(hs, 2) * k + skip, 128), n)
        x = lax.rem(ch, 4)
        other = lax.rem(lax.div(ch, 4) + pos[4], 2)
        to = pl.ds(at, n)
        line = pl.multiple_of(x * lines + HALO * other, HALO)
        add(swapped.at[pl.ds(line, HALO), lanes], tokv.at[pl.ds(0, HALO), to]).start()
        for core in range(2):
            target = tokv.at[pl.ds(HALO + core * rows, rows), to]
            line = pl.multiple_of((4 * core + x) * rows, rows)
            copy = add(near.at[pl.ds(line, rows), lanes], target)
            pl.when(other == 0)(copy.start)
            line = pl.multiple_of((4 * core + x) * lines + 2 * HALO, HALO)
            source = swapped.at[pl.ds(line, rows), lanes]
            copy = pltpu.make_async_copy(source, target, sem.at[len(copies) - 1])
            pl.when(other == 1)(copy.start)
        at += n
    return copies


def project_kernel(sizes, early, late, *refs):
    rows, depth, width, modes, seq = sizes
    pos, near, swapped, *pieces = refs[:-7]
    sums, late_tok, tokv, wv, tok_sem, late_sem, w_sem = refs[-7:]
    copies, at = [], 0
    for number, piece in enumerate(pieces):
        n = piece.shape[0]
        copies.append(pltpu.make_async_copy(piece, wv.at[pl.ds(at, n), :], w_sem.at[number]))
        copies[-1].start()
        at += n
    copies += token_copies(sizes, pos, near, swapped, early, tokv, tok_sem)
    late_copies = token_copies(sizes, pos, near, swapped, late, late_tok, late_sem)
    for copy in copies:
        copy.wait()

    @pl.loop(0, 3)
    def _(j):
        cols = pl.ds(pl.multiple_of(j * width, width), width)
        part = jnp.dot(tokv[...], wv[:, cols], preferred_element_type=F32)
        for lh in range(width // 128):
            sums[j * (width // 128) + lh] = part[:, lh * 128 : lh * 128 + 128]

    for copy in late_copies:
        copy.wait()


def late_products(sizes, signals, late_tok, pieces, sums, acc):
    rows, depth, width, modes, seq = sizes
    k = depth // 16
    first, last = signals
    halves = width // 128

    @pl.loop(first, last)
    def _(j):
        cols = pl.ds(pl.multiple_of(j * width, width), width)
        part = sum(
            jnp.dot(late_tok[:, i * k : i * k + k], piece[:, cols], preferred_element_type=F32)
            for i, piece in enumerate(pieces)
        )
        for lh in range(halves):
            new = part[:, lh * 128 : lh * 128 + 128]
            acc[(j - first) * halves + lh] = (sums[j * halves + lh] + new).astype(BF16).astype(F32)


def filtered(sizes, signals, lh, acc, taps, mine):
    rows, depth, width, modes, seq = sizes
    steps = 2 * rows // SUB
    halves = width // 128
    count = signals[1] - signals[0]
    weights = [[taps[lag, j : j + 1, mine] for j in range(*signals)] for lag in range(3)]

    def read(start):
        return [acc[j * halves + lh, pl.ds(start, SUB, stride=steps), :] for j in range(count)]

    def features(now, last, before):
        return [
            weights[0][j] * now[j] + weights[1][j] * last[j] + weights[2][j] * before[j]
            for j in range(count)
        ]

    return read, features


def state_kernel(sizes, *refs):
    rows, depth, width, modes, seq = sizes
    pos, late_tok, *pieces = refs[:-8]
    sums, taps, decay, product, gated, states_out, acc, state = refs[-8:]
    c = pos[3]
    late_products(sizes, (0, 1), late_tok, pieces, sums, gated)
    late_products(sizes, (1, 3), late_tok, pieces, sums, acc)
    steps = 2 * rows // SUB
    for lh in range(width // 128):
        mine = pl.ds(pl.multiple_of(c * width + lh * 128, 128), 128)
        lanes = pl.ds(lh * 128, 128)
        read, features = filtered(sizes, (1, 3), lh, acc, taps, mine)
        rates = [jnp.broadcast_to(decay[m : m + 1, mine] / seq, (SUB, 128)) for m in range(modes)]
        factors = [jnp.exp(-rate) for rate in rates]

        def step(t, carry):
            before, last, states = carry
            now = read(HALO + t)
            f = features(now, last, before)
            p = f[0] * f[1]
            product[t, :, lanes] = p
            return last, now, [a * s + p for a, s in zip(factors, states)]

        zero = jnp.zeros((SUB, 128), F32)
        carry = (read(HALO - 2), read(HALO - 1), [zero] * modes)
        states = lax.fori_loop(0, steps, step, carry, unroll=8)[2]
        line = lax.broadcasted_iota(jnp.int32, (SUB, 128), 0).astype(F32)
        left = (SUB - 1.0 - line) * float(steps)
        for m in range(modes):
            total = jnp.sum(jnp.exp(-rates[m] * left) * states[m], axis=0, keepdims=True)
            state[m : m + 1, lanes] = total
    for r in range(16):
        states_out[r] = state[...]


def local_kernel(sizes, pos, gated, taps, product, gain, decay, skip, gate, local, inside):
    rows, depth, width, modes, seq = sizes
    c = pos[3]
    steps = 2 * rows // SUB
    for lh in range(width // 128):
        mine = pl.ds(pl.multiple_of(c * width + lh * 128, 128), 128)
        lanes = pl.ds(lh * 128, 128)
        read, features = filtered(sizes, (0, 1), lh, gated, taps, mine)
        rates = [jnp.broadcast_to(decay[m : m + 1, mine] / seq, (SUB, 128)) for m in range(modes)]
        factors = [jnp.exp(-rate) for rate in rates]
        heights = [gain[m : m + 1, mine] * jnp.sqrt(2.0 * rates[m]) for m in range(modes)]
        direct = jnp.broadcast_to(skip[:, mine], (SUB, 128))

        def gates(t, carry):
            before, last = carry
            now = read(HALO + t)
            gate[t, :, lanes] = features(now, last, before)[0]
            return last, now

        lax.fori_loop(0, steps, gates, (read(HALO - 2), read(HALO - 1)), unroll=8)

        def step(t, states):
            p = product[t, :, lanes]
            states = [a * s + p for a, s in zip(factors, states)]
            parts = [w * s for w, s in zip(heights, states)]
            while len(parts) > 1:
                parts = [a + b for a, b in zip(parts[::2], parts[1::2])]
            local[t, :, lanes] = parts[0] + direct * p
            return states

        states = lax.fori_loop(0, steps, step, [jnp.zeros((SUB, 128), F32)] * modes, unroll=4)
        line = lax.broadcasted_iota(jnp.int32, (SUB, 128), 0)

        def later(value, by):
            return jnp.where(line >= by, pltpu.roll(value, by, 0), 0.0)

        for m in range(modes):
            s = states[m]
            for by in (1, 2, 4):
                s = s + jnp.exp(-float(steps * by) * rates[m]) * later(s, by)
            inside[m, :, lanes] = later(s, 1)


def finish_kernel(sizes, pos, gate, local, inside, states, gain, decay, mine_out, their_out, start, whole):
    rows, depth, width, modes, seq = sizes
    rank, c = pos[0], pos[3]
    steps = 2 * rows // SUB
    length = 2 * rows
    for lh in range(width // 128):
        mine = pl.ds(pl.multiple_of(c * width + lh * 128, 128), 128)
        lanes = pl.ds(lh * 128, 128)
        over = jnp.exp(-float(length) * (decay[:, mine] / seq))
        entering = jnp.zeros((modes, 128), F32)
        for r in range(16):
            entering = jnp.where(r < rank, over * entering + states[r, :, lanes], entering)
        start[:, lanes] = entering
        line = lax.broadcasted_iota(jnp.int32, (SUB, 128), 0).astype(F32) * float(steps)
        factors, waves = [], []
        for m in range(modes):
            rate = jnp.broadcast_to(decay[m : m + 1, mine] / seq, (SUB, 128))
            factors.append(jnp.exp(-rate))
            height = gain[m : m + 1, mine] * jnp.sqrt(2.0 * rate)
            waves.append(height * (inside[m, :, lanes] + jnp.exp(-rate * line) * start[m : m + 1, lanes]))

        def step(t, waves):
            waves = [a * z for a, z in zip(factors, waves)]
            parts = waves
            while len(parts) > 1:
                parts = [a + b for a, b in zip(parts[::2], parts[1::2])]
            whole[lh, pl.ds(t, SUB, stride=steps), :] = gate[t, :, lanes] * (local[t, :, lanes] + parts[0])
            return waves

        lax.fori_loop(0, steps, step, waves, unroll=4)
        for out, core in ((mine_out, c), (their_out, 1 - c)):
            line = pl.ds(pl.multiple_of(core * rows, rows), rows)
            out[:, lanes] = whole[lh, line, :].astype(BF16)


def body(tokens, w_in, taps, modes_gain, decay, skip):
    rows = tokens.shape[0]
    group = w_in.shape[2]
    width = group // 2
    k = w_in.shape[0]
    modes = decay.shape[0]
    depth = tokens.shape[1] * 8
    seq = rows * 32
    sizes = (rows, depth, width, modes, seq)
    y, h, c = (lax.axis_index(a) for a in CTX)
    pos = jnp.stack([y * 4 + h, y, h, c, lax.axis_index("l")]).astype(jnp.int32)

    tie = lax.optimization_barrier
    with jax.named_scope("weight_gather"):
        halves = w_in.reshape(k, 3, 2, width).transpose(2, 0, 1, 3).reshape(2, k, 3 * width)
        mine = lax.dynamic_index_in_dim(halves, c, 0, keepdims=False)
        theirs = lax.ppermute(lax.dynamic_index_in_dim(halves, 1 - c, 0, keepdims=False), "c", SWAP)
        own = in_order(c == 0, mine, theirs, 0)
        tail, own = tie((tokens[rows - HALO :], own))
    with jax.named_scope("token_swap"):
        other = lax.ppermute(tokens, "l", SWAP)
        route = [(4 * r + 2 + side, 4 * r + 4 + side) for r in range(15) for side in range(2)]
        halo = lax.ppermute(tail, (*CTX, "l"), route)
        other_halo = lax.ppermute(tail, (*CTX, "l"), [(i, j ^ 1) for i, j in route])
    with jax.named_scope("weight_rings"):
        farther = shifted(own, "y", 2)
        far = both_ways(own, "y")
        beside = both_ways(own, "h")
    first = (halo, other_halo, other, farther, beside, far)
    halo, other_halo, other, farther, beside, far = tie(first)
    with jax.named_scope("token_gather"):
        near = lax.all_gather(tokens, ("c", "x"), axis=0, tiled=True)
        wide = jnp.concatenate([halo, other_halo, other], 0)
        swapped = lax.all_gather(wide, ("c", "x"), axis=0, tiled=True)
    with jax.named_scope("weight_rings"):
        two, half = 2 * k, k
        moves = [(0, 0, two, 0, 0), (1, 0, two, 0, two), (0, 0, half, 1, 0), (1, half, half, 2, 0)]
        pair, low, high = relayed(beside, moves, "relay_pair")
        far_pair = both_ways(pair, "y")
        opposite = shifted(low, "h", 1), shifted(high, "h", -1)
        far_pair, opposite = tie((far_pair, opposite))
        moves = [(0, 0, two, 0, 0), (1, two, two, 1, 0)]
        moves += [(side, 0, half, 2, side * half) for side in range(2)]
        moves += [(side, two + half, half, 3, side * half) for side in range(2)]
        moves += [(2 + side, 0, half, 4, side * half) for side in range(2)]
        behind, ahead, firsts, seconds, opposite = relayed([*far_pair, *opposite], moves, "relay_far")
        last = shifted(opposite, "y", 2)
        farther_pair = shifted(behind, "y", 1), shifted(ahead, "y", -1)
        far_opposite = shifted(firsts, "h", 1), shifted(seconds, "h", -1)

    early = [own, pair, opposite]
    early_runs = [(0, dh, 0, two) for dh in (0, 1, -1, 2)]
    for side, dy in enumerate((1, -1)):
        early += [far[side], far_pair[side]]
        early_runs += [(dy, dh, 0, two) for dh in (0, 1, -1)]
    early += [farther]
    early_runs += [(2, 0, 0, two)]
    late = [*far_opposite, *farther_pair, last]
    late_runs = [(dy, 2, skip, half) for skip in (0, half) for dy in (1, -1)]
    late_runs += [(2, 1, 0, two), (2, -1, 0, two), (2, 2, 0, two)]

    vmem = pl.BlockSpec(memory_space=pltpu.VMEM)
    smem = pl.BlockSpec(memory_space=pltpu.SMEM)
    hbm = pl.BlockSpec(memory_space=pltpu.HBM)
    block = (2 * rows // SUB, SUB, width)
    full = jax.ShapeDtypeStruct(block, F32)
    lines = 2 * rows + HALO
    chunks = (3 * width // 128, lines, 128)

    def dma(n):
        return pltpu.SemaphoreType.DMA((n,))

    sums, late_tok = pl.pallas_call(
        functools.partial(project_kernel, sizes, early_runs, late_runs),
        out_shape=(
            jax.ShapeDtypeStruct(chunks, F32),
            jax.ShapeDtypeStruct((lines, 5 * two), BF16),
        ),
        in_specs=[smem] + [hbm] * (2 + len(early)),
        out_specs=(vmem, vmem),
        scratch_shapes=[
            pltpu.VMEM((lines, 11 * two), BF16),
            pltpu.VMEM((11 * two, 3 * width), BF16),
            dma(3 * len(early_runs)),
            dma(3 * len(late_runs)),
            dma(len(early)),
        ],
        compiler_params=pltpu.CompilerParams(vmem_limit_bytes=14 * 2**20),
        cost_estimate=pl.CostEstimate(
            flops=2 * lines * 11 * two * 3 * width, bytes_accessed=9_000_000, transcendentals=0
        ),
        name="project",
    )(pos, near, swapped, *early)
    params = pltpu.CompilerParams(vmem_limit_bytes=8 * 2**20)
    product, gated, state = pl.pallas_call(
        functools.partial(state_kernel, sizes),
        out_shape=(
            full,
            jax.ShapeDtypeStruct((width // 128, lines, 128), F32),
            jax.ShapeDtypeStruct((16, modes, width), F32),
        ),
        in_specs=[smem] + [vmem] * (4 + len(late)),
        out_specs=(vmem,) * 3,
        scratch_shapes=[
            pltpu.VMEM((2 * width // 128, lines, 128), F32),
            pltpu.VMEM((modes, width), F32),
        ],
        compiler_params=params,
        name="states",
    )(pos, late_tok, *late, sums, taps, decay)

    with jax.named_scope("state_exchange"):
        states = lax.all_to_all(state, ("y", "h"), 0, 0, tiled=True)
    gate, local, inside = pl.pallas_call(
        functools.partial(local_kernel, sizes),
        out_shape=(full, full, jax.ShapeDtypeStruct((modes, SUB, width), F32)),
        in_specs=[smem] + [vmem] * 6,
        out_specs=(vmem,) * 3,
        compiler_params=params,
        cost_estimate=pl.CostEstimate(
            flops=30_000_000, bytes_accessed=2_000_000, transcendentals=0
        ),
        name="local",
    )(pos, gated, taps, product, modes_gain, decay, skip.reshape(1, group))
    mine, theirs = pl.pallas_call(
        functools.partial(finish_kernel, sizes),
        out_shape=(jax.ShapeDtypeStruct((rows, width), BF16),) * 2,
        in_specs=[smem] + [vmem] * 6,
        out_specs=(vmem, vmem),
        scratch_shapes=[pltpu.VMEM((modes, width), F32), pltpu.VMEM((width // 128, 2 * rows, 128), F32)],
        compiler_params=params,
        name="finish",
    )(pos, gate, local, inside, states, modes_gain, decay)
    with jax.named_scope("result_swap"):
        return in_order(c == 0, mine, lax.ppermute(theirs, "c", SWAP), 1)


def solution(mesh):
    split = Mesh(mesh.devices.reshape(4, 4, 2, 2, 4), AXES)
    return jax.shard_map(
        body,
        mesh=split,
        in_specs=(
            P(CTX, CH),
            P(CTX, None, CH),
            P(None, None, CH),
            P(None, CH),
            P(None, CH),
            P(CH),
        ),
        out_specs=P(CTX, CH),
        check_vma=False,
    )
```

```python
import functools

import jax
import jax.numpy as jnp
from jax import lax
from jax.experimental import pallas as pl
from jax.experimental.pallas import tpu as pltpu
from jax.sharding import Mesh
from jax.sharding import PartitionSpec as P

AXES = ("y", "h", "c", "l", "x")
CTX = ("y", "h", "c")
CH = ("l", "x")
F32 = jnp.float32
BF16 = jnp.bfloat16
HALO = 16
SWAP = [(0, 1), (1, 0)]
SUB = 8


def shifted(array, axis, step):
    n = lax.axis_size(axis)
    return lax.ppermute(array, axis, [(i, (i + step) % n) for i in range(n)])


def in_order(mine_first, mine, theirs, axis):
    first, second = jnp.where(mine_first, mine, theirs), jnp.where(mine_first, theirs, mine)
    return jnp.concatenate([first, second], axis)


def both_ways(piece, axis):
    return shifted(piece, axis, 1), shifted(piece, axis, -1)


def relay_kernel(moves, count, *refs):
    sources, targets, sem = refs[:count], refs[count:-1], refs[-1]
    copies = []
    for number, (source, first, n, target, at) in enumerate(moves):
        copies.append(
            pltpu.make_async_copy(
                sources[source].at[pl.ds(first, n), :],
                targets[target].at[pl.ds(at, n), :],
                sem.at[number],
            )
        )
        copies[-1].start()
    for copy in copies:
        copy.wait()


def relayed(sources, moves, name):
    heights = [max(at + n for _, _, n, target, at in moves if target == t) for t in range(1 + max(m[3] for m in moves))]
    anywhere = pl.BlockSpec(memory_space=pl.ANY)
    return pl.pallas_call(
        functools.partial(relay_kernel, moves, len(sources)),
        out_shape=[jax.ShapeDtypeStruct((h, sources[0].shape[1]), sources[0].dtype) for h in heights],
        in_specs=[anywhere] * len(sources),
        out_specs=[anywhere] * len(heights),
        scratch_shapes=[pltpu.SemaphoreType.DMA((len(moves),))],
        cost_estimate=pl.CostEstimate(flops=0, bytes_accessed=2_000_000, transcendentals=0),
        compiler_params=pltpu.CompilerParams(vmem_limit_bytes=2**20),
        name=name,
    )(*sources)


def token_copies(sizes, pos, near, swapped, runs, tokv, sem):
    rows, depth, width, modes, seq = sizes
    k = depth // 16
    lines = rows + 2 * HALO
    copies, at = [], 0

    def add(source, target):
        copies.append(pltpu.make_async_copy(source, target, sem.at[len(copies)]))
        return copies[-1]

    for dy, dh, skip, n in runs:
        ys, hs = lax.rem(pos[1] - dy + 4, 4), lax.rem(pos[2] - dh + 4, 4)
        ch = 2 * ys + lax.div(hs, 2)
        lanes = pl.ds(pl.multiple_of(lax.rem(hs, 2) * k + skip, 128), n)
        x = lax.rem(ch, 4)
        other = lax.rem(lax.div(ch, 4) + pos[4], 2)
        to = pl.ds(at, n)
        line = pl.multiple_of(x * lines + HALO * other, HALO)
        add(swapped.at[pl.ds(line, HALO), lanes], tokv.at[pl.ds(0, HALO), to]).start()
        for core in range(2):
            target = tokv.at[pl.ds(HALO + core * rows, rows), to]
            line = pl.multiple_of((4 * core + x) * rows, rows)
            copy = add(near.at[pl.ds(line, rows), lanes], target)
            pl.when(other == 0)(copy.start)
            line = pl.multiple_of((4 * core + x) * lines + 2 * HALO, HALO)
            source = swapped.at[pl.ds(line, rows), lanes]
            copy = pltpu.make_async_copy(source, target, sem.at[len(copies) - 1])
            pl.when(other == 1)(copy.start)
        at += n
    return copies


def project_kernel(sizes, early, late, *refs):
    rows, depth, width, modes, seq = sizes
    pos, near, swapped, *pieces = refs[:-7]
    sums, late_tok, tokv, wv, tok_sem, late_sem, w_sem = refs[-7:]
    copies, at = [], 0
    for number, piece in enumerate(pieces):
        n = piece.shape[0]
        copies.append(pltpu.make_async_copy(piece, wv.at[pl.ds(at, n), :], w_sem.at[number]))
        copies[-1].start()
        at += n
    copies += token_copies(sizes, pos, near, swapped, early, tokv, tok_sem)
    late_copies = token_copies(sizes, pos, near, swapped, late, late_tok, late_sem)
    for copy in copies:
        copy.wait()

    @pl.loop(0, 3)
    def _(j):
        cols = pl.ds(pl.multiple_of(j * width, width), width)
        part = jnp.dot(tokv[...], wv[:, cols], preferred_element_type=F32)
        for lh in range(width // 128):
            sums[j * (width // 128) + lh] = part[:, lh * 128 : lh * 128 + 128]

    for copy in late_copies:
        copy.wait()


def late_products(sizes, signals, late_tok, pieces, sums, acc):
    rows, depth, width, modes, seq = sizes
    k = depth // 16
    first, last = signals
    halves = width // 128

    @pl.loop(first, last)
    def _(j):
        cols = pl.ds(pl.multiple_of(j * width, width), width)
        part = sum(
            jnp.dot(late_tok[:, i * k : i * k + k], piece[:, cols], preferred_element_type=F32)
            for i, piece in enumerate(pieces)
        )
        for lh in range(halves):
            new = part[:, lh * 128 : lh * 128 + 128]
            acc[(j - first) * halves + lh] = (sums[j * halves + lh] + new).astype(BF16).astype(F32)


def filtered(sizes, signals, lh, acc, taps, mine):
    rows, depth, width, modes, seq = sizes
    steps = 2 * rows // SUB
    halves = width // 128
    count = signals[1] - signals[0]
    weights = [[taps[lag, j : j + 1, mine] for j in range(*signals)] for lag in range(3)]

    def read(start):
        return [acc[j * halves + lh, pl.ds(start, SUB, stride=steps), :] for j in range(count)]

    def features(now, last, before):
        return [
            weights[0][j] * now[j] + weights[1][j] * last[j] + weights[2][j] * before[j]
            for j in range(count)
        ]

    return read, features


def state_kernel(sizes, *refs):
    rows, depth, width, modes, seq = sizes
    pos, late_tok, *pieces = refs[:-8]
    sums, taps, decay, product, gated, states_out, acc, state = refs[-8:]
    c = pos[3]
    late_products(sizes, (0, 1), late_tok, pieces, sums, gated)
    late_products(sizes, (1, 3), late_tok, pieces, sums, acc)
    steps = 2 * rows // SUB
    for lh in range(width // 128):
        mine = pl.ds(pl.multiple_of(c * width + lh * 128, 128), 128)
        lanes = pl.ds(lh * 128, 128)
        read, features = filtered(sizes, (1, 3), lh, acc, taps, mine)
        rates = [jnp.broadcast_to(decay[m : m + 1, mine] / seq, (SUB, 128)) for m in range(modes)]
        factors = [jnp.exp(-rate) for rate in rates]

        def step(t, carry):
            before, last, states = carry
            now = read(HALO + t)
            f = features(now, last, before)
            p = f[0] * f[1]
            product[t, :, lanes] = p
            return last, now, [a * s + p for a, s in zip(factors, states)]

        zero = jnp.zeros((SUB, 128), F32)
        carry = (read(HALO - 2), read(HALO - 1), [zero] * modes)
        states = lax.fori_loop(0, steps, step, carry, unroll=8)[2]
        line = lax.broadcasted_iota(jnp.int32, (SUB, 128), 0).astype(F32)
        left = (SUB - 1.0 - line) * float(steps)
        for m in range(modes):
            total = jnp.sum(jnp.exp(-rates[m] * left) * states[m], axis=0, keepdims=True)
            state[m : m + 1, lanes] = total
    for r in range(16):
        states_out[r] = state[...]


def local_kernel(sizes, pos, gated, taps, product, gain, decay, skip, gate, local, inside):
    rows, depth, width, modes, seq = sizes
    c = pos[3]
    steps = 2 * rows // SUB
    for lh in range(width // 128):
        mine = pl.ds(pl.multiple_of(c * width + lh * 128, 128), 128)
        lanes = pl.ds(lh * 128, 128)
        read, features = filtered(sizes, (0, 1), lh, gated, taps, mine)
        rates = [jnp.broadcast_to(decay[m : m + 1, mine] / seq, (SUB, 128)) for m in range(modes)]
        factors = [jnp.exp(-rate) for rate in rates]
        heights = [gain[m : m + 1, mine] * jnp.sqrt(2.0 * rates[m]) for m in range(modes)]
        direct = jnp.broadcast_to(skip[:, mine], (SUB, 128))

        def gates(t, carry):
            before, last = carry
            now = read(HALO + t)
            gate[t, :, lanes] = features(now, last, before)[0]
            return last, now

        lax.fori_loop(0, steps, gates, (read(HALO - 2), read(HALO - 1)), unroll=8)

        def step(t, states):
            p = product[t, :, lanes]
            states = [a * s + p for a, s in zip(factors, states)]
            parts = [w * s for w, s in zip(heights, states)]
            while len(parts) > 1:
                parts = [a + b for a, b in zip(parts[::2], parts[1::2])]
            local[t, :, lanes] = parts[0] + direct * p
            return states

        states = lax.fori_loop(0, steps, step, [jnp.zeros((SUB, 128), F32)] * modes, unroll=4)
        line = lax.broadcasted_iota(jnp.int32, (SUB, 128), 0)

        def later(value, by):
            return jnp.where(line >= by, pltpu.roll(value, by, 0), 0.0)

        for m in range(modes):
            s = states[m]
            for by in (1, 2, 4):
                s = s + jnp.exp(-float(steps * by) * rates[m]) * later(s, by)
            inside[m, :, lanes] = later(s, 1)


def finish_kernel(sizes, pos, gate, local, inside, states, gain, decay, mine_out, their_out, start, whole):
    rows, depth, width, modes, seq = sizes
    rank, c = pos[0], pos[3]
    steps = 2 * rows // SUB
    length = 2 * rows
    for lh in range(width // 128):
        mine = pl.ds(pl.multiple_of(c * width + lh * 128, 128), 128)
        lanes = pl.ds(lh * 128, 128)
        over = jnp.exp(-float(length) * (decay[:, mine] / seq))
        entering = jnp.zeros((modes, 128), F32)
        for r in range(16):
            entering = jnp.where(r < rank, over * entering + states[r, :, lanes], entering)
        start[:, lanes] = entering
        line = lax.broadcasted_iota(jnp.int32, (SUB, 128), 0).astype(F32) * float(steps)
        factors, waves = [], []
        for m in range(modes):
            rate = jnp.broadcast_to(decay[m : m + 1, mine] / seq, (SUB, 128))
            factors.append(jnp.exp(-rate))
            height = gain[m : m + 1, mine] * jnp.sqrt(2.0 * rate)
            waves.append(height * (inside[m, :, lanes] + jnp.exp(-rate * line) * start[m : m + 1, lanes]))

        def step(t, waves):
            waves = [a * z for a, z in zip(factors, waves)]
            parts = waves
            while len(parts) > 1:
                parts = [a + b for a, b in zip(parts[::2], parts[1::2])]
            whole[lh, pl.ds(t, SUB, stride=steps), :] = gate[t, :, lanes] * (local[t, :, lanes] + parts[0])
            return waves

        lax.fori_loop(0, steps, step, waves, unroll=4)
        for out, core in ((mine_out, c), (their_out, 1 - c)):
            line = pl.ds(pl.multiple_of(core * rows, rows), rows)
            out[:, lanes] = whole[lh, line, :].astype(BF16)


def body(tokens, w_in, taps, modes_gain, decay, skip):
    rows = tokens.shape[0]
    group = w_in.shape[2]
    width = group // 2
    k = w_in.shape[0]
    modes = decay.shape[0]
    depth = tokens.shape[1] * 8
    seq = rows * 32
    sizes = (rows, depth, width, modes, seq)
    y, h, c = (lax.axis_index(a) for a in CTX)
    pos = jnp.stack([y * 4 + h, y, h, c, lax.axis_index("l")]).astype(jnp.int32)

    tie = lax.optimization_barrier
    with jax.named_scope("weight_gather"):
        halves = w_in.reshape(k, 3, 2, width).transpose(2, 0, 1, 3).reshape(2, k, 3 * width)
        mine = lax.dynamic_index_in_dim(halves, c, 0, keepdims=False)
        theirs = lax.ppermute(lax.dynamic_index_in_dim(halves, 1 - c, 0, keepdims=False), "c", SWAP)
        own = in_order(c == 0, mine, theirs, 0)
        tail, own = tie((tokens[rows - HALO :], own))
    with jax.named_scope("token_swap"):
        other = lax.ppermute(tokens, "l", SWAP)
        route = [(4 * r + 2 + side, 4 * r + 4 + side) for r in range(15) for side in range(2)]
        halo = lax.ppermute(tail, (*CTX, "l"), route)
        other_halo = lax.ppermute(tail, (*CTX, "l"), [(i, j ^ 1) for i, j in route])
    with jax.named_scope("weight_rings"):
        farther = shifted(own, "y", 2)
        far = both_ways(own, "y")
        beside = both_ways(own, "h")
    first = (halo, other_halo, other, farther, far, beside)
    halo, other_halo, other, farther, far, beside = tie(first)
    with jax.named_scope("token_gather"):
        near = lax.all_gather(tokens, ("c", "x"), axis=0, tiled=True)
        wide = jnp.concatenate([halo, other_halo, other], 0)
        swapped = lax.all_gather(wide, ("c", "x"), axis=0, tiled=True)
    with jax.named_scope("weight_rings"):
        two, half = 2 * k, k
        moves = [(0, 0, two, 0, 0), (1, 0, two, 0, two), (0, 0, half, 1, 0), (1, half, half, 2, 0)]
        pair, low, high = relayed(beside, moves, "relay_pair")
        far_pair = both_ways(pair, "y")
        opposite = shifted(low, "h", 1), shifted(high, "h", -1)
        far_pair, opposite = tie((far_pair, opposite))
        moves = [(0, 0, two, 0, 0), (1, two, two, 1, 0)]
        moves += [(side, 0, half, 2, side * half) for side in range(2)]
        moves += [(side, two + half, half, 3, side * half) for side in range(2)]
        moves += [(2 + side, 0, half, 4, side * half) for side in range(2)]
        behind, ahead, firsts, seconds, opposite = relayed([*far_pair, *opposite], moves, "relay_far")
        last = shifted(opposite, "y", 2)
        farther_pair = shifted(behind, "y", 1), shifted(ahead, "y", -1)
        far_opposite = shifted(firsts, "h", 1), shifted(seconds, "h", -1)

    early = [own, pair, opposite]
    early_runs = [(0, dh, 0, two) for dh in (0, 1, -1, 2)]
    for side, dy in enumerate((1, -1)):
        early += [far[side], far_pair[side]]
        early_runs += [(dy, dh, 0, two) for dh in (0, 1, -1)]
    early += [farther]
    early_runs += [(2, 0, 0, two)]
    late = [*farther_pair, *far_opposite, last]
    late_runs = [(2, 1, 0, two), (2, -1, 0, two)]
    late_runs += [(dy, 2, skip, half) for skip in (0, half) for dy in (1, -1)]
    late_runs += [(2, 2, 0, two)]

    vmem = pl.BlockSpec(memory_space=pltpu.VMEM)
    smem = pl.BlockSpec(memory_space=pltpu.SMEM)
    hbm = pl.BlockSpec(memory_space=pltpu.HBM)
    block = (2 * rows // SUB, SUB, width)
    full = jax.ShapeDtypeStruct(block, F32)
    lines = 2 * rows + HALO
    chunks = (3 * width // 128, lines, 128)

    def dma(n):
        return pltpu.SemaphoreType.DMA((n,))

    sums, late_tok = pl.pallas_call(
        functools.partial(project_kernel, sizes, early_runs, late_runs),
        out_shape=(
            jax.ShapeDtypeStruct(chunks, F32),
            jax.ShapeDtypeStruct((lines, 5 * two), BF16),
        ),
        in_specs=[smem] + [hbm] * (2 + len(early)),
        out_specs=(vmem, vmem),
        scratch_shapes=[
            pltpu.VMEM((lines, 11 * two), BF16),
            pltpu.VMEM((11 * two, 3 * width), BF16),
            dma(3 * len(early_runs)),
            dma(3 * len(late_runs)),
            dma(len(early)),
        ],
        compiler_params=pltpu.CompilerParams(vmem_limit_bytes=14 * 2**20),
        cost_estimate=pl.CostEstimate(
            flops=2 * lines * 11 * two * 3 * width, bytes_accessed=9_000_000, transcendentals=0
        ),
        name="project",
    )(pos, near, swapped, *early)
    params = pltpu.CompilerParams(vmem_limit_bytes=8 * 2**20)
    product, gated, state = pl.pallas_call(
        functools.partial(state_kernel, sizes),
        out_shape=(
            full,
            jax.ShapeDtypeStruct((width // 128, lines, 128), F32),
            jax.ShapeDtypeStruct((16, modes, width), F32),
        ),
        in_specs=[smem] + [vmem] * (4 + len(late)),
        out_specs=(vmem,) * 3,
        scratch_shapes=[
            pltpu.VMEM((2 * width // 128, lines, 128), F32),
            pltpu.VMEM((modes, width), F32),
        ],
        compiler_params=params,
        name="states",
    )(pos, late_tok, *late, sums, taps, decay)

    with jax.named_scope("state_exchange"):
        states = lax.all_to_all(state, ("y", "h"), 0, 0, tiled=True)
    gate, local, inside = pl.pallas_call(
        functools.partial(local_kernel, sizes),
        out_shape=(full, full, jax.ShapeDtypeStruct((modes, SUB, width), F32)),
        in_specs=[smem] + [vmem] * 6,
        out_specs=(vmem,) * 3,
        compiler_params=params,
        cost_estimate=pl.CostEstimate(
            flops=30_000_000, bytes_accessed=2_000_000, transcendentals=0
        ),
        name="local",
    )(pos, gated, taps, product, modes_gain, decay, skip.reshape(1, group))
    mine, theirs = pl.pallas_call(
        functools.partial(finish_kernel, sizes),
        out_shape=(jax.ShapeDtypeStruct((rows, width), BF16),) * 2,
        in_specs=[smem] + [vmem] * 6,
        out_specs=(vmem, vmem),
        scratch_shapes=[pltpu.VMEM((modes, width), F32), pltpu.VMEM((width // 128, 2 * rows, 128), F32)],
        compiler_params=params,
        name="finish",
    )(pos, gate, local, inside, states, modes_gain, decay)
    with jax.named_scope("result_swap"):
        return in_order(c == 0, mine, lax.ppermute(theirs, "c", SWAP), 1)


def solution(mesh):
    split = Mesh(mesh.devices.reshape(4, 4, 2, 2, 4), AXES)
    return jax.shard_map(
        body,
        mesh=split,
        in_specs=(
            P(CTX, CH),
            P(CTX, None, CH),
            P(None, None, CH),
            P(None, CH),
            P(None, CH),
            P(CH),
        ),
        out_specs=P(CTX, CH),
        check_vma=False,
    )
```

```python
import functools

import jax
import jax.numpy as jnp
from jax import lax
from jax.experimental import pallas as pl
from jax.experimental.pallas import tpu as pltpu
from jax.sharding import Mesh
from jax.sharding import PartitionSpec as P

AXES = ("y", "h", "c", "l", "x")
CTX = ("y", "h", "c")
CH = ("l", "x")
F32 = jnp.float32
BF16 = jnp.bfloat16
HALO = 16
SWAP = [(0, 1), (1, 0)]
SUB = 8


def shifted(array, axis, step):
    n = lax.axis_size(axis)
    return lax.ppermute(array, axis, [(i, (i + step) % n) for i in range(n)])


def in_order(mine_first, mine, theirs, axis):
    first, second = jnp.where(mine_first, mine, theirs), jnp.where(mine_first, theirs, mine)
    return jnp.concatenate([first, second], axis)


def both_ways(piece, axis):
    return shifted(piece, axis, 1), shifted(piece, axis, -1)


def relay_kernel(moves, count, *refs):
    sources, targets, sem = refs[:count], refs[count:-1], refs[-1]
    copies = []
    for number, (source, first, n, target, at) in enumerate(moves):
        copies.append(
            pltpu.make_async_copy(
                sources[source].at[pl.ds(first, n), :],
                targets[target].at[pl.ds(at, n), :],
                sem.at[number],
            )
        )
        copies[-1].start()
    for copy in copies:
        copy.wait()


def relayed(sources, moves, name):
    heights = [max(at + n for _, _, n, target, at in moves if target == t) for t in range(1 + max(m[3] for m in moves))]
    anywhere = pl.BlockSpec(memory_space=pl.ANY)
    return pl.pallas_call(
        functools.partial(relay_kernel, moves, len(sources)),
        out_shape=[jax.ShapeDtypeStruct((h, sources[0].shape[1]), sources[0].dtype) for h in heights],
        in_specs=[anywhere] * len(sources),
        out_specs=[anywhere] * len(heights),
        scratch_shapes=[pltpu.SemaphoreType.DMA((len(moves),))],
        cost_estimate=pl.CostEstimate(flops=0, bytes_accessed=2_000_000, transcendentals=0),
        compiler_params=pltpu.CompilerParams(vmem_limit_bytes=2**20),
        name=name,
    )(*sources)


def token_copies(sizes, pos, near, swapped, runs, tokv, sem):
    rows, depth, width, modes, seq = sizes
    k = depth // 16
    lines = rows + 2 * HALO
    copies, at = [], 0

    def add(source, target):
        copies.append(pltpu.make_async_copy(source, target, sem.at[len(copies)]))
        return copies[-1]

    for dy, dh, skip, n in runs:
        ys, hs = lax.rem(pos[1] - dy + 4, 4), lax.rem(pos[2] - dh + 4, 4)
        ch = 2 * ys + lax.div(hs, 2)
        lanes = pl.ds(pl.multiple_of(lax.rem(hs, 2) * k + skip, 128), n)
        x = lax.rem(ch, 4)
        other = lax.rem(lax.div(ch, 4) + pos[4], 2)
        to = pl.ds(at, n)
        line = pl.multiple_of(x * lines + HALO * other, HALO)
        add(swapped.at[pl.ds(line, HALO), lanes], tokv.at[pl.ds(0, HALO), to]).start()
        for core in range(2):
            target = tokv.at[pl.ds(HALO + core * rows, rows), to]
            line = pl.multiple_of((4 * core + x) * rows, rows)
            copy = add(near.at[pl.ds(line, rows), lanes], target)
            pl.when(other == 0)(copy.start)
            line = pl.multiple_of((4 * core + x) * lines + 2 * HALO, HALO)
            source = swapped.at[pl.ds(line, rows), lanes]
            copy = pltpu.make_async_copy(source, target, sem.at[len(copies) - 1])
            pl.when(other == 1)(copy.start)
        at += n
    return copies


def project_kernel(sizes, early, late, *refs):
    rows, depth, width, modes, seq = sizes
    pos, near, swapped, *pieces = refs[:-7]
    sums, late_tok, tokv, wv, tok_sem, late_sem, w_sem = refs[-7:]
    copies, at = [], 0
    for number, piece in enumerate(pieces):
        n = piece.shape[0]
        copies.append(pltpu.make_async_copy(piece, wv.at[pl.ds(at, n), :], w_sem.at[number]))
        copies[-1].start()
        at += n
    copies += token_copies(sizes, pos, near, swapped, early, tokv, tok_sem)
    late_copies = token_copies(sizes, pos, near, swapped, late, late_tok, late_sem)
    for copy in copies:
        copy.wait()

    @pl.loop(0, 3)
    def _(j):
        cols = pl.ds(pl.multiple_of(j * width, width), width)
        part = jnp.dot(tokv[...], wv[:, cols], preferred_element_type=F32)
        for lh in range(width // 128):
            sums[j * (width // 128) + lh] = part[:, lh * 128 : lh * 128 + 128]

    for copy in late_copies:
        copy.wait()


def late_products(sizes, signals, late_tok, pieces, sums, acc):
    rows, depth, width, modes, seq = sizes
    k = depth // 16
    first, last = signals
    halves = width // 128

    @pl.loop(first, last)
    def _(j):
        cols = pl.ds(pl.multiple_of(j * width, width), width)
        part = sum(
            jnp.dot(late_tok[:, i * k : i * k + k], piece[:, cols], preferred_element_type=F32)
            for i, piece in enumerate(pieces)
        )
        for lh in range(halves):
            new = part[:, lh * 128 : lh * 128 + 128]
            acc[(j - first) * halves + lh] = (sums[j * halves + lh] + new).astype(BF16).astype(F32)


def filtered(sizes, signals, lh, acc, taps, mine):
    rows, depth, width, modes, seq = sizes
    steps = 2 * rows // SUB
    halves = width // 128
    count = signals[1] - signals[0]
    weights = [[taps[lag, j : j + 1, mine] for j in range(*signals)] for lag in range(3)]

    def read(start):
        return [acc[j * halves + lh, pl.ds(start, SUB, stride=steps), :] for j in range(count)]

    def features(now, last, before):
        return [
            weights[0][j] * now[j] + weights[1][j] * last[j] + weights[2][j] * before[j]
            for j in range(count)
        ]

    return read, features


def state_kernel(sizes, *refs):
    rows, depth, width, modes, seq = sizes
    pos, late_tok, *pieces = refs[:-8]
    sums, taps, decay, product, gated, states_out, acc, state = refs[-8:]
    c = pos[3]
    late_products(sizes, (0, 1), late_tok, pieces, sums, gated)
    late_products(sizes, (1, 3), late_tok, pieces, sums, acc)
    steps = 2 * rows // SUB
    for lh in range(width // 128):
        mine = pl.ds(pl.multiple_of(c * width + lh * 128, 128), 128)
        lanes = pl.ds(lh * 128, 128)
        read, features = filtered(sizes, (1, 3), lh, acc, taps, mine)
        rates = [jnp.broadcast_to(decay[m : m + 1, mine] / seq, (SUB, 128)) for m in range(modes)]
        factors = [jnp.exp(-rate) for rate in rates]

        def step(t, carry):
            before, last, states = carry
            now = read(HALO + t)
            f = features(now, last, before)
            p = f[0] * f[1]
            product[t, :, lanes] = p
            return last, now, [a * s + p for a, s in zip(factors, states)]

        zero = jnp.zeros((SUB, 128), F32)
        carry = (read(HALO - 2), read(HALO - 1), [zero] * modes)
        states = lax.fori_loop(0, steps, step, carry, unroll=8)[2]
        line = lax.broadcasted_iota(jnp.int32, (SUB, 128), 0).astype(F32)
        left = (SUB - 1.0 - line) * float(steps)
        for m in range(modes):
            total = jnp.sum(jnp.exp(-rates[m] * left) * states[m], axis=0, keepdims=True)
            state[m : m + 1, lanes] = total
    for r in range(16):
        states_out[r] = state[...]


def local_kernel(sizes, pos, gated, taps, product, gain, decay, skip, gate, local, inside):
    rows, depth, width, modes, seq = sizes
    c = pos[3]
    steps = 2 * rows // SUB
    for lh in range(width // 128):
        mine = pl.ds(pl.multiple_of(c * width + lh * 128, 128), 128)
        lanes = pl.ds(lh * 128, 128)
        read, features = filtered(sizes, (0, 1), lh, gated, taps, mine)
        rates = [jnp.broadcast_to(decay[m : m + 1, mine] / seq, (SUB, 128)) for m in range(modes)]
        factors = [jnp.exp(-rate) for rate in rates]
        heights = [gain[m : m + 1, mine] * jnp.sqrt(2.0 * rates[m]) for m in range(modes)]
        direct = jnp.broadcast_to(skip[:, mine], (SUB, 128))

        def gates(t, carry):
            before, last = carry
            now = read(HALO + t)
            gate[t, :, lanes] = features(now, last, before)[0]
            return last, now

        lax.fori_loop(0, steps, gates, (read(HALO - 2), read(HALO - 1)), unroll=8)

        def step(t, states):
            p = product[t, :, lanes]
            states = [a * s + p for a, s in zip(factors, states)]
            parts = [w * s for w, s in zip(heights, states)]
            while len(parts) > 1:
                parts = [a + b for a, b in zip(parts[::2], parts[1::2])]
            local[t, :, lanes] = parts[0] + direct * p
            return states

        states = lax.fori_loop(0, steps, step, [jnp.zeros((SUB, 128), F32)] * modes, unroll=4)
        line = lax.broadcasted_iota(jnp.int32, (SUB, 128), 0)

        def later(value, by):
            return jnp.where(line >= by, pltpu.roll(value, by, 0), 0.0)

        for m in range(modes):
            s = states[m]
            for by in (1, 2, 4):
                s = s + jnp.exp(-float(steps * by) * rates[m]) * later(s, by)
            inside[m, :, lanes] = later(s, 1)


def finish_kernel(sizes, pos, gate, local, inside, states, gain, decay, mine_out, their_out, start, whole):
    rows, depth, width, modes, seq = sizes
    rank, c = pos[0], pos[3]
    steps = 2 * rows // SUB
    length = 2 * rows
    for lh in range(width // 128):
        mine = pl.ds(pl.multiple_of(c * width + lh * 128, 128), 128)
        lanes = pl.ds(lh * 128, 128)
        over = jnp.exp(-float(length) * (decay[:, mine] / seq))
        entering = jnp.zeros((modes, 128), F32)
        for r in range(16):
            entering = jnp.where(r < rank, over * entering + states[r, :, lanes], entering)
        start[:, lanes] = entering
        line = lax.broadcasted_iota(jnp.int32, (SUB, 128), 0).astype(F32) * float(steps)
        factors, waves = [], []
        for m in range(modes):
            rate = jnp.broadcast_to(decay[m : m + 1, mine] / seq, (SUB, 128))
            factors.append(jnp.exp(-rate))
            height = gain[m : m + 1, mine] * jnp.sqrt(2.0 * rate)
            waves.append(height * (inside[m, :, lanes] + jnp.exp(-rate * line) * start[m : m + 1, lanes]))

        def step(t, waves):
            waves = [a * z for a, z in zip(factors, waves)]
            parts = waves
            while len(parts) > 1:
                parts = [a + b for a, b in zip(parts[::2], parts[1::2])]
            whole[lh, pl.ds(t, SUB, stride=steps), :] = gate[t, :, lanes] * (local[t, :, lanes] + parts[0])
            return waves

        lax.fori_loop(0, steps, step, waves, unroll=4)
        for out, core in ((mine_out, c), (their_out, 1 - c)):
            line = pl.ds(pl.multiple_of(core * rows, rows), rows)
            out[:, lanes] = whole[lh, line, :].astype(BF16)


def body(tokens, w_in, taps, modes_gain, decay, skip):
    rows = tokens.shape[0]
    group = w_in.shape[2]
    width = group // 2
    k = w_in.shape[0]
    modes = decay.shape[0]
    depth = tokens.shape[1] * 8
    seq = rows * 32
    sizes = (rows, depth, width, modes, seq)
    y, h, c = (lax.axis_index(a) for a in CTX)
    pos = jnp.stack([y * 4 + h, y, h, c, lax.axis_index("l")]).astype(jnp.int32)

    tie = lax.optimization_barrier
    with jax.named_scope("weight_gather"):
        halves = w_in.reshape(k, 3, 2, width).transpose(2, 0, 1, 3).reshape(2, k, 3 * width)
        mine = lax.dynamic_index_in_dim(halves, c, 0, keepdims=False)
        theirs = lax.ppermute(lax.dynamic_index_in_dim(halves, 1 - c, 0, keepdims=False), "c", SWAP)
        own = in_order(c == 0, mine, theirs, 0)
    with jax.named_scope("token_swap"):
        other = lax.ppermute(tokens, "l", SWAP)
    with jax.named_scope("weight_rings"):
        farther = shifted(own, "y", 2)
        far = both_ways(own, "y")
        beside = both_ways(own, "h")
        other, far = tie((other, far))
        tails = jnp.concatenate([tokens[rows - HALO :], other[rows - HALO :]], 0)
        halos = lax.ppermute(tails, CTX, [(i, i + 1) for i in range(1, 31, 2)])
    first = (halos, other, farther, far, beside)
    halos, other, farther, far, beside = tie(first)
    with jax.named_scope("token_gather"):
        near = lax.all_gather(tokens, ("c", "x"), axis=0, tiled=True)
        wide = jnp.concatenate([halos, other], 0)
        swapped = lax.all_gather(wide, ("c", "x"), axis=0, tiled=True)
    with jax.named_scope("weight_rings"):
        two, half = 2 * k, k
        moves = [(0, 0, two, 0, 0), (1, 0, two, 0, two), (0, 0, half, 1, 0), (1, half, half, 2, 0)]
        pair, low, high = relayed(beside, moves, "relay_pair")
        far_pair = both_ways(pair, "y")
        opposite = shifted(low, "h", 1), shifted(high, "h", -1)
        far_pair, opposite = tie((far_pair, opposite))
        moves = [(0, 0, two, 0, 0), (1, two, two, 1, 0)]
        moves += [(side, 0, half, 2, side * half) for side in range(2)]
        moves += [(side, two + half, half, 3, side * half) for side in range(2)]
        moves += [(2 + side, 0, half, 4, side * half) for side in range(2)]
        behind, ahead, firsts, seconds, opposite = relayed([*far_pair, *opposite], moves, "relay_far")
        last = shifted(opposite, "y", 2)
        farther_pair = shifted(behind, "y", 1), shifted(ahead, "y", -1)
        far_opposite = shifted(firsts, "h", 1), shifted(seconds, "h", -1)

    early = [own, pair, opposite]
    early_runs = [(0, dh, 0, two) for dh in (0, 1, -1, 2)]
    for side, dy in enumerate((1, -1)):
        early += [far[side], far_pair[side]]
        early_runs += [(dy, dh, 0, two) for dh in (0, 1, -1)]
    early += [farther]
    early_runs += [(2, 0, 0, two)]
    late = [*farther_pair, *far_opposite, last]
    late_runs = [(2, 1, 0, two), (2, -1, 0, two)]
    late_runs += [(dy, 2, skip, half) for skip in (0, half) for dy in (1, -1)]
    late_runs += [(2, 2, 0, two)]

    vmem = pl.BlockSpec(memory_space=pltpu.VMEM)
    smem = pl.BlockSpec(memory_space=pltpu.SMEM)
    hbm = pl.BlockSpec(memory_space=pltpu.HBM)
    block = (2 * rows // SUB, SUB, width)
    full = jax.ShapeDtypeStruct(block, F32)
    lines = 2 * rows + HALO
    chunks = (3 * width // 128, lines, 128)

    def dma(n):
        return pltpu.SemaphoreType.DMA((n,))

    sums, late_tok = pl.pallas_call(
        functools.partial(project_kernel, sizes, early_runs, late_runs),
        out_shape=(
            jax.ShapeDtypeStruct(chunks, F32),
            jax.ShapeDtypeStruct((lines, 5 * two), BF16),
        ),
        in_specs=[smem] + [hbm] * (2 + len(early)),
        out_specs=(vmem, vmem),
        scratch_shapes=[
            pltpu.VMEM((lines, 11 * two), BF16),
            pltpu.VMEM((11 * two, 3 * width), BF16),
            dma(3 * len(early_runs)),
            dma(3 * len(late_runs)),
            dma(len(early)),
        ],
        compiler_params=pltpu.CompilerParams(vmem_limit_bytes=14 * 2**20),
        cost_estimate=pl.CostEstimate(
            flops=2 * lines * 11 * two * 3 * width, bytes_accessed=9_000_000, transcendentals=0
        ),
        name="project",
    )(pos, near, swapped, *early)
    params = pltpu.CompilerParams(vmem_limit_bytes=8 * 2**20)
    product, gated, state = pl.pallas_call(
        functools.partial(state_kernel, sizes),
        out_shape=(
            full,
            jax.ShapeDtypeStruct((width // 128, lines, 128), F32),
            jax.ShapeDtypeStruct((16, modes, width), F32),
        ),
        in_specs=[smem] + [vmem] * (4 + len(late)),
        out_specs=(vmem,) * 3,
        scratch_shapes=[
            pltpu.VMEM((2 * width // 128, lines, 128), F32),
            pltpu.VMEM((modes, width), F32),
        ],
        compiler_params=params,
        name="states",
    )(pos, late_tok, *late, sums, taps, decay)

    with jax.named_scope("state_exchange"):
        states = lax.all_to_all(state, ("y", "h"), 0, 0, tiled=True)
    gate, local, inside = pl.pallas_call(
        functools.partial(local_kernel, sizes),
        out_shape=(full, full, jax.ShapeDtypeStruct((modes, SUB, width), F32)),
        in_specs=[smem] + [vmem] * 6,
        out_specs=(vmem,) * 3,
        compiler_params=params,
        cost_estimate=pl.CostEstimate(
            flops=30_000_000, bytes_accessed=2_000_000, transcendentals=0
        ),
        name="local",
    )(pos, gated, taps, product, modes_gain, decay, skip.reshape(1, group))
    mine, theirs = pl.pallas_call(
        functools.partial(finish_kernel, sizes),
        out_shape=(jax.ShapeDtypeStruct((rows, width), BF16),) * 2,
        in_specs=[smem] + [vmem] * 6,
        out_specs=(vmem, vmem),
        scratch_shapes=[pltpu.VMEM((modes, width), F32), pltpu.VMEM((width // 128, 2 * rows, 128), F32)],
        compiler_params=params,
        name="finish",
    )(pos, gate, local, inside, states, modes_gain, decay)
    with jax.named_scope("result_swap"):
        return in_order(c == 0, mine, lax.ppermute(theirs, "c", SWAP), 1)


def solution(mesh):
    split = Mesh(mesh.devices.reshape(4, 4, 2, 2, 4), AXES)
    return jax.shard_map(
        body,
        mesh=split,
        in_specs=(
            P(CTX, CH),
            P(CTX, None, CH),
            P(None, None, CH),
            P(None, CH),
            P(None, CH),
            P(CH),
        ),
        out_specs=P(CTX, CH),
        check_vma=False,
    )
```

```python
import functools

import jax
import jax.numpy as jnp
from jax import lax
from jax.experimental import pallas as pl
from jax.experimental.pallas import tpu as pltpu
from jax.sharding import Mesh
from jax.sharding import PartitionSpec as P

AXES = ("y", "h", "c", "l", "x")
CTX = ("y", "h", "c")
CH = ("l", "x")
F32 = jnp.float32
BF16 = jnp.bfloat16
HALO = 16
SWAP = [(0, 1), (1, 0)]
SUB = 8


def shifted(array, axis, step):
    n = lax.axis_size(axis)
    return lax.ppermute(array, axis, [(i, (i + step) % n) for i in range(n)])


def in_order(mine_first, mine, theirs, axis):
    first, second = jnp.where(mine_first, mine, theirs), jnp.where(mine_first, theirs, mine)
    return jnp.concatenate([first, second], axis)


def both_ways(piece, axis):
    return shifted(piece, axis, 1), shifted(piece, axis, -1)


def relay_kernel(moves, count, *refs):
    sources, targets, sem = refs[:count], refs[count:-1], refs[-1]
    copies = []
    for number, (source, first, n, target, at) in enumerate(moves):
        copies.append(
            pltpu.make_async_copy(
                sources[source].at[pl.ds(first, n), :],
                targets[target].at[pl.ds(at, n), :],
                sem.at[number],
            )
        )
        copies[-1].start()
    for copy in copies:
        copy.wait()


def relayed(sources, moves, name):
    heights = [max(at + n for _, _, n, target, at in moves if target == t) for t in range(1 + max(m[3] for m in moves))]
    anywhere = pl.BlockSpec(memory_space=pl.ANY)
    return pl.pallas_call(
        functools.partial(relay_kernel, moves, len(sources)),
        out_shape=[jax.ShapeDtypeStruct((h, sources[0].shape[1]), sources[0].dtype) for h in heights],
        in_specs=[anywhere] * len(sources),
        out_specs=[anywhere] * len(heights),
        scratch_shapes=[pltpu.SemaphoreType.DMA((len(moves),))],
        cost_estimate=pl.CostEstimate(flops=0, bytes_accessed=2_000_000, transcendentals=0),
        compiler_params=pltpu.CompilerParams(vmem_limit_bytes=2**20),
        name=name,
    )(*sources)


def token_copies(sizes, pos, near, swapped, runs, tokv, sem):
    rows, depth, width, modes, seq = sizes
    k = depth // 16
    lines = rows + 2 * HALO
    copies, at = [], 0

    def add(source, target):
        copies.append(pltpu.make_async_copy(source, target, sem.at[len(copies)]))
        return copies[-1]

    for dy, dh, skip, n in runs:
        ys, hs = lax.rem(pos[1] - dy + 4, 4), lax.rem(pos[2] - dh + 4, 4)
        ch = 2 * ys + lax.div(hs, 2)
        lanes = pl.ds(pl.multiple_of(lax.rem(hs, 2) * k + skip, 128), n)
        x = lax.rem(ch, 4)
        other = lax.rem(lax.div(ch, 4) + pos[4], 2)
        to = pl.ds(at, n)
        line = pl.multiple_of(x * lines + HALO * other, HALO)
        add(swapped.at[pl.ds(line, HALO), lanes], tokv.at[pl.ds(0, HALO), to]).start()
        for core in range(2):
            target = tokv.at[pl.ds(HALO + core * rows, rows), to]
            line = pl.multiple_of((4 * core + x) * rows, rows)
            copy = add(near.at[pl.ds(line, rows), lanes], target)
            pl.when(other == 0)(copy.start)
            line = pl.multiple_of((4 * core + x) * lines + 2 * HALO, HALO)
            source = swapped.at[pl.ds(line, rows), lanes]
            copy = pltpu.make_async_copy(source, target, sem.at[len(copies) - 1])
            pl.when(other == 1)(copy.start)
        at += n
    return copies


def project_kernel(sizes, early, late, *refs):
    rows, depth, width, modes, seq = sizes
    pos, near, swapped, *pieces = refs[:-7]
    sums, late_tok, tokv, wv, tok_sem, late_sem, w_sem = refs[-7:]
    copies, at = [], 0
    for number, piece in enumerate(pieces):
        n = piece.shape[0]
        copies.append(pltpu.make_async_copy(piece, wv.at[pl.ds(at, n), :], w_sem.at[number]))
        copies[-1].start()
        at += n
    copies += token_copies(sizes, pos, near, swapped, early, tokv, tok_sem)
    late_copies = token_copies(sizes, pos, near, swapped, late, late_tok, late_sem)
    for copy in copies:
        copy.wait()

    @pl.loop(0, 3)
    def _(j):
        cols = pl.ds(pl.multiple_of(j * width, width), width)
        part = jnp.dot(tokv[...], wv[:, cols], preferred_element_type=F32)
        for lh in range(width // 128):
            sums[j * (width // 128) + lh] = part[:, lh * 128 : lh * 128 + 128]

    for copy in late_copies:
        copy.wait()


def late_products(sizes, signals, late_tok, pieces, sums, acc):
    rows, depth, width, modes, seq = sizes
    k = depth // 16
    first, last = signals
    halves = width // 128

    @pl.loop(first, last)
    def _(j):
        cols = pl.ds(pl.multiple_of(j * width, width), width)
        part = sum(
            jnp.dot(late_tok[:, i * k : i * k + k], piece[:, cols], preferred_element_type=F32)
            for i, piece in enumerate(pieces)
        )
        for lh in range(halves):
            new = part[:, lh * 128 : lh * 128 + 128]
            acc[(j - first) * halves + lh] = (sums[j * halves + lh] + new).astype(BF16).astype(F32)


def filtered(sizes, signals, lh, acc, taps, mine):
    rows, depth, width, modes, seq = sizes
    steps = 2 * rows // SUB
    halves = width // 128
    count = signals[1] - signals[0]
    weights = [[taps[lag, j : j + 1, mine] for j in range(*signals)] for lag in range(3)]

    def read(start):
        return [acc[j * halves + lh, pl.ds(start, SUB, stride=steps), :] for j in range(count)]

    def features(now, last, before):
        return [
            weights[0][j] * now[j] + weights[1][j] * last[j] + weights[2][j] * before[j]
            for j in range(count)
        ]

    return read, features


def state_kernel(sizes, *refs):
    rows, depth, width, modes, seq = sizes
    pos, late_tok, *pieces = refs[:-7]
    sums, taps, decay, product, gated, state, acc = refs[-7:]
    c = pos[3]
    late_products(sizes, (0, 1), late_tok, pieces, sums, gated)
    late_products(sizes, (1, 3), late_tok, pieces, sums, acc)
    steps = 2 * rows // SUB
    for lh in range(width // 128):
        mine = pl.ds(pl.multiple_of(c * width + lh * 128, 128), 128)
        lanes = pl.ds(lh * 128, 128)
        read, features = filtered(sizes, (1, 3), lh, acc, taps, mine)
        rates = [jnp.broadcast_to(decay[m : m + 1, mine] / seq, (SUB, 128)) for m in range(modes)]
        factors = [jnp.exp(-rate) for rate in rates]

        def step(t, carry):
            before, last, states = carry
            now = read(HALO + t)
            f = features(now, last, before)
            p = f[0] * f[1]
            product[t, :, lanes] = p
            return last, now, [a * s + p for a, s in zip(factors, states)]

        zero = jnp.zeros((SUB, 128), F32)
        carry = (read(HALO - 2), read(HALO - 1), [zero] * modes)
        states = lax.fori_loop(0, steps, step, carry, unroll=8)[2]
        line = lax.broadcasted_iota(jnp.int32, (SUB, 128), 0).astype(F32)
        left = (SUB - 1.0 - line) * float(steps)
        for m in range(modes):
            total = jnp.sum(jnp.exp(-rates[m] * left) * states[m], axis=0, keepdims=True)
            state[m : m + 1, lanes] = total


def local_kernel(sizes, pos, gated, taps, product, gain, decay, skip, gate, local, inside):
    rows, depth, width, modes, seq = sizes
    c = pos[3]
    steps = 2 * rows // SUB
    for lh in range(width // 128):
        mine = pl.ds(pl.multiple_of(c * width + lh * 128, 128), 128)
        lanes = pl.ds(lh * 128, 128)
        read, features = filtered(sizes, (0, 1), lh, gated, taps, mine)
        rates = [jnp.broadcast_to(decay[m : m + 1, mine] / seq, (SUB, 128)) for m in range(modes)]
        factors = [jnp.exp(-rate) for rate in rates]
        heights = [gain[m : m + 1, mine] * jnp.sqrt(2.0 * rates[m]) for m in range(modes)]
        direct = jnp.broadcast_to(skip[:, mine], (SUB, 128))

        def gates(t, carry):
            before, last = carry
            now = read(HALO + t)
            gate[t, :, lanes] = features(now, last, before)[0]
            return last, now

        lax.fori_loop(0, steps, gates, (read(HALO - 2), read(HALO - 1)), unroll=8)

        def step(t, states):
            p = product[t, :, lanes]
            states = [a * s + p for a, s in zip(factors, states)]
            parts = [w * s for w, s in zip(heights, states)]
            while len(parts) > 1:
                parts = [a + b for a, b in zip(parts[::2], parts[1::2])]
            local[t, :, lanes] = parts[0] + direct * p
            return states

        states = lax.fori_loop(0, steps, step, [jnp.zeros((SUB, 128), F32)] * modes, unroll=4)
        line = lax.broadcasted_iota(jnp.int32, (SUB, 128), 0)

        def later(value, by):
            return jnp.where(line >= by, pltpu.roll(value, by, 0), 0.0)

        for m in range(modes):
            s = states[m]
            for by in (1, 2, 4):
                s = s + jnp.exp(-float(steps * by) * rates[m]) * later(s, by)
            inside[m, :, lanes] = later(s, 1)


def combine_kernel(sizes, pos, *refs):
    rows, depth, width, modes, seq = sizes
    *states, decay, inner, total = refs
    h, c = pos[2], pos[3]
    rate = decay[:, pl.ds(pl.multiple_of(c * width, width), width)] / seq * float(2 * rows)
    entering = jnp.zeros((modes, width), F32)
    left = jnp.zeros((modes, width), F32)
    for d, state in enumerate(states):
        after = (3 - lax.rem(h - d + 4, 4)).astype(F32)
        left += jnp.exp(-rate * after) * state[...]
        if d > 0:
            entering += jnp.where(d <= h, jnp.exp(-rate * float(d - 1)) * state[...], 0.0)
    inner[...] = entering
    total[...] = left


def finish_kernel(sizes, pos, gate, local, inside, inner, *refs):
    rows, depth, width, modes, seq = sizes
    *totals, gain, decay, mine_out, their_out, start, whole = refs
    h, c = pos[2], pos[3]
    steps = 2 * rows // SUB
    length = 2 * rows
    for lh in range(width // 128):
        mine = pl.ds(pl.multiple_of(c * width + lh * 128, 128), 128)
        lanes = pl.ds(lh * 128, 128)
        over = decay[:, mine] / seq * float(length)
        outer = jnp.zeros((modes, 128), F32)
        for d, total in enumerate(totals):
            outer += jnp.exp(-over * float(4 * d)) * total[:, lanes]
        entering = inner[:, lanes] + jnp.exp(-over * h.astype(F32)) * outer
        start[:, lanes] = entering
        line = lax.broadcasted_iota(jnp.int32, (SUB, 128), 0).astype(F32) * float(steps)
        factors, waves = [], []
        for m in range(modes):
            rate = jnp.broadcast_to(decay[m : m + 1, mine] / seq, (SUB, 128))
            factors.append(jnp.exp(-rate))
            height = gain[m : m + 1, mine] * jnp.sqrt(2.0 * rate)
            waves.append(height * (inside[m, :, lanes] + jnp.exp(-rate * line) * start[m : m + 1, lanes]))

        def step(t, waves):
            waves = [a * z for a, z in zip(factors, waves)]
            parts = waves
            while len(parts) > 1:
                parts = [a + b for a, b in zip(parts[::2], parts[1::2])]
            whole[lh, pl.ds(t, SUB, stride=steps), :] = gate[t, :, lanes] * (local[t, :, lanes] + parts[0])
            return waves

        lax.fori_loop(0, steps, step, waves, unroll=4)
        for out, core in ((mine_out, c), (their_out, 1 - c)):
            line = pl.ds(pl.multiple_of(core * rows, rows), rows)
            out[:, lanes] = whole[lh, line, :].astype(BF16)


def body(tokens, w_in, taps, modes_gain, decay, skip):
    rows = tokens.shape[0]
    group = w_in.shape[2]
    width = group // 2
    k = w_in.shape[0]
    modes = decay.shape[0]
    depth = tokens.shape[1] * 8
    seq = rows * 32
    sizes = (rows, depth, width, modes, seq)
    y, h, c = (lax.axis_index(a) for a in CTX)
    pos = jnp.stack([y * 4 + h, y, h, c, lax.axis_index("l")]).astype(jnp.int32)

    tie = lax.optimization_barrier
    with jax.named_scope("weight_gather"):
        halves = w_in.reshape(k, 3, 2, width).transpose(2, 0, 1, 3).reshape(2, k, 3 * width)
        mine = lax.dynamic_index_in_dim(halves, c, 0, keepdims=False)
        theirs = lax.ppermute(lax.dynamic_index_in_dim(halves, 1 - c, 0, keepdims=False), "c", SWAP)
        own = in_order(c == 0, mine, theirs, 0)
    with jax.named_scope("token_swap"):
        other = lax.ppermute(tokens, "l", SWAP)
    with jax.named_scope("weight_rings"):
        farther = shifted(own, "y", 2)
        far = both_ways(own, "y")
        beside = both_ways(own, "h")
        other, far = tie((other, far))
        tails = jnp.concatenate([tokens[rows - HALO :], other[rows - HALO :]], 0)
        halos = lax.ppermute(tails, CTX, [(i, i + 1) for i in range(1, 31, 2)])
    first = (halos, other, farther, far, beside)
    halos, other, farther, far, beside = tie(first)
    with jax.named_scope("token_gather"):
        near = lax.all_gather(tokens, ("c", "x"), axis=0, tiled=True)
        wide = jnp.concatenate([halos, other], 0)
        swapped = lax.all_gather(wide, ("c", "x"), axis=0, tiled=True)
    with jax.named_scope("weight_rings"):
        two, half = 2 * k, k
        moves = [(0, 0, two, 0, 0), (1, 0, two, 0, two), (0, 0, half, 1, 0), (1, half, half, 2, 0)]
        pair, low, high = relayed(beside, moves, "relay_pair")
        far_pair = both_ways(pair, "y")
        opposite = shifted(low, "h", 1), shifted(high, "h", -1)
        far_pair, opposite = tie((far_pair, opposite))
        moves = [(0, 0, two, 0, 0), (1, two, two, 1, 0)]
        moves += [(side, 0, half, 2, side * half) for side in range(2)]
        moves += [(side, two + half, half, 3, side * half) for side in range(2)]
        moves += [(2 + side, 0, half, 4, side * half) for side in range(2)]
        behind, ahead, firsts, seconds, opposite = relayed([*far_pair, *opposite], moves, "relay_far")
        last = shifted(opposite, "y", 2)
        farther_pair = shifted(behind, "y", 1), shifted(ahead, "y", -1)
        far_opposite = shifted(firsts, "h", 1), shifted(seconds, "h", -1)

    early = [own, pair, opposite]
    early_runs = [(0, dh, 0, two) for dh in (0, 1, -1, 2)]
    for side, dy in enumerate((1, -1)):
        early += [far[side], far_pair[side]]
        early_runs += [(dy, dh, 0, two) for dh in (0, 1, -1)]
    early += [farther]
    early_runs += [(2, 0, 0, two)]
    late = [*farther_pair, *far_opposite, last]
    late_runs = [(2, 1, 0, two), (2, -1, 0, two)]
    late_runs += [(dy, 2, skip, half) for skip in (0, half) for dy in (1, -1)]
    late_runs += [(2, 2, 0, two)]

    vmem = pl.BlockSpec(memory_space=pltpu.VMEM)
    smem = pl.BlockSpec(memory_space=pltpu.SMEM)
    hbm = pl.BlockSpec(memory_space=pltpu.HBM)
    block = (2 * rows // SUB, SUB, width)
    full = jax.ShapeDtypeStruct(block, F32)
    lines = 2 * rows + HALO
    chunks = (3 * width // 128, lines, 128)

    def dma(n):
        return pltpu.SemaphoreType.DMA((n,))

    sums, late_tok = pl.pallas_call(
        functools.partial(project_kernel, sizes, early_runs, late_runs),
        out_shape=(
            jax.ShapeDtypeStruct(chunks, F32),
            jax.ShapeDtypeStruct((lines, 5 * two), BF16),
        ),
        in_specs=[smem] + [hbm] * (2 + len(early)),
        out_specs=(vmem, vmem),
        scratch_shapes=[
            pltpu.VMEM((lines, 11 * two), BF16),
            pltpu.VMEM((11 * two, 3 * width), BF16),
            dma(3 * len(early_runs)),
            dma(3 * len(late_runs)),
            dma(len(early)),
        ],
        compiler_params=pltpu.CompilerParams(vmem_limit_bytes=14 * 2**20),
        cost_estimate=pl.CostEstimate(
            flops=2 * lines * 11 * two * 3 * width, bytes_accessed=9_000_000, transcendentals=0
        ),
        name="project",
    )(pos, near, swapped, *early)
    params = pltpu.CompilerParams(vmem_limit_bytes=8 * 2**20)
    product, gated, state = pl.pallas_call(
        functools.partial(state_kernel, sizes),
        out_shape=(
            full,
            jax.ShapeDtypeStruct((width // 128, lines, 128), F32),
            jax.ShapeDtypeStruct((modes, width), F32),
        ),
        in_specs=[smem] + [vmem] * (4 + len(late)),
        out_specs=(vmem,) * 3,
        scratch_shapes=[pltpu.VMEM((2 * width // 128, lines, 128), F32)],
        compiler_params=params,
        name="states",
    )(pos, late_tok, *late, sums, taps, decay)

    with jax.named_scope("state_exchange"):
        states = [state, *(shifted(state, "h", d) for d in (1, 2, 3))]
        inner, total = pl.pallas_call(
            functools.partial(combine_kernel, sizes),
            out_shape=(jax.ShapeDtypeStruct((modes, width), F32),) * 2,
            in_specs=[smem] + [vmem] * 5,
            out_specs=(vmem, vmem),
            compiler_params=params,
            name="combine",
        )(pos, *states, decay)
        totals = [
            lax.ppermute(total, "y", [(i, i + d) for i in range(4 - d)]) for d in (1, 2, 3)
        ]
    gate, local, inside = pl.pallas_call(
        functools.partial(local_kernel, sizes),
        out_shape=(full, full, jax.ShapeDtypeStruct((modes, SUB, width), F32)),
        in_specs=[smem] + [vmem] * 6,
        out_specs=(vmem,) * 3,
        compiler_params=params,
        cost_estimate=pl.CostEstimate(
            flops=30_000_000, bytes_accessed=2_000_000, transcendentals=0
        ),
        name="local",
    )(pos, gated, taps, product, modes_gain, decay, skip.reshape(1, group))
    mine, theirs = pl.pallas_call(
        functools.partial(finish_kernel, sizes),
        out_shape=(jax.ShapeDtypeStruct((rows, width), BF16),) * 2,
        in_specs=[smem] + [vmem] * 9,
        out_specs=(vmem, vmem),
        scratch_shapes=[pltpu.VMEM((modes, width), F32), pltpu.VMEM((width // 128, 2 * rows, 128), F32)],
        compiler_params=params,
        name="finish",
    )(pos, gate, local, inside, inner, *totals, modes_gain, decay)
    with jax.named_scope("result_swap"):
        return in_order(c == 0, mine, lax.ppermute(theirs, "c", SWAP), 1)


def solution(mesh):
    split = Mesh(mesh.devices.reshape(4, 4, 2, 2, 4), AXES)
    return jax.shard_map(
        body,
        mesh=split,
        in_specs=(
            P(CTX, CH),
            P(CTX, None, CH),
            P(None, None, CH),
            P(None, CH),
            P(None, CH),
            P(CH),
        ),
        out_specs=P(CTX, CH),
        check_vma=False,
    )
```

```python
import functools

import jax
import jax.numpy as jnp
from jax import lax
from jax.experimental import pallas as pl
from jax.experimental.pallas import tpu as pltpu
from jax.sharding import Mesh
from jax.sharding import PartitionSpec as P

AXES = ("y", "h", "c", "l", "x")
CTX = ("y", "h", "c")
CH = ("l", "x")
F32 = jnp.float32
BF16 = jnp.bfloat16
HALO = 16
SWAP = [(0, 1), (1, 0)]
SUB = 8


def shifted(array, axis, step):
    n = lax.axis_size(axis)
    return lax.ppermute(array, axis, [(i, (i + step) % n) for i in range(n)])


def in_order(mine_first, mine, theirs, axis):
    first, second = jnp.where(mine_first, mine, theirs), jnp.where(mine_first, theirs, mine)
    return jnp.concatenate([first, second], axis)


def both_ways(piece, axis):
    return shifted(piece, axis, 1), shifted(piece, axis, -1)


def relay_kernel(moves, count, *refs):
    sources, targets, sem = refs[:count], refs[count:-1], refs[-1]
    copies = []
    for number, (source, first, n, target, at) in enumerate(moves):
        copies.append(
            pltpu.make_async_copy(
                sources[source].at[pl.ds(first, n), :],
                targets[target].at[pl.ds(at, n), :],
                sem.at[number],
            )
        )
        copies[-1].start()
    for copy in copies:
        copy.wait()


def relayed(sources, moves, name):
    heights = [max(at + n for _, _, n, target, at in moves if target == t) for t in range(1 + max(m[3] for m in moves))]
    anywhere = pl.BlockSpec(memory_space=pl.ANY)
    return pl.pallas_call(
        functools.partial(relay_kernel, moves, len(sources)),
        out_shape=[jax.ShapeDtypeStruct((h, sources[0].shape[1]), sources[0].dtype) for h in heights],
        in_specs=[anywhere] * len(sources),
        out_specs=[anywhere] * len(heights),
        scratch_shapes=[pltpu.SemaphoreType.DMA((len(moves),))],
        cost_estimate=pl.CostEstimate(flops=0, bytes_accessed=2_000_000, transcendentals=0),
        compiler_params=pltpu.CompilerParams(vmem_limit_bytes=2**20),
        name=name,
    )(*sources)


def token_copies(sizes, pos, near, swapped, runs, tokv, sem):
    rows, depth, width, modes, seq = sizes
    k = depth // 16
    lines = rows + 2 * HALO
    copies, at = [], 0

    def add(source, target):
        copies.append(pltpu.make_async_copy(source, target, sem.at[len(copies)]))
        return copies[-1]

    for dy, dh, skip, n in runs:
        ys, hs = lax.rem(pos[1] - dy + 4, 4), lax.rem(pos[2] - dh + 4, 4)
        ch = 2 * ys + lax.div(hs, 2)
        lanes = pl.ds(pl.multiple_of(lax.rem(hs, 2) * k + skip, 128), n)
        x = lax.rem(ch, 4)
        other = lax.rem(lax.div(ch, 4) + pos[4], 2)
        to = pl.ds(at, n)
        line = pl.multiple_of(x * lines + HALO * other, HALO)
        add(swapped.at[pl.ds(line, HALO), lanes], tokv.at[pl.ds(0, HALO), to]).start()
        for core in range(2):
            target = tokv.at[pl.ds(HALO + core * rows, rows), to]
            line = pl.multiple_of((4 * core + x) * rows, rows)
            copy = add(near.at[pl.ds(line, rows), lanes], target)
            pl.when(other == 0)(copy.start)
            line = pl.multiple_of((4 * core + x) * lines + 2 * HALO, HALO)
            source = swapped.at[pl.ds(line, rows), lanes]
            copy = pltpu.make_async_copy(source, target, sem.at[len(copies) - 1])
            pl.when(other == 1)(copy.start)
        at += n
    return copies


def project_kernel(sizes, early, late, *refs):
    rows, depth, width, modes, seq = sizes
    pos, near, swapped, *pieces = refs[:-7]
    sums, late_tok, tokv, wv, tok_sem, late_sem, w_sem = refs[-7:]
    copies, at = [], 0
    for number, piece in enumerate(pieces):
        n = piece.shape[0]
        copies.append(pltpu.make_async_copy(piece, wv.at[pl.ds(at, n), :], w_sem.at[number]))
        copies[-1].start()
        at += n
    copies += token_copies(sizes, pos, near, swapped, early, tokv, tok_sem)
    late_copies = token_copies(sizes, pos, near, swapped, late, late_tok, late_sem)
    for copy in copies:
        copy.wait()

    @pl.loop(0, 3)
    def _(j):
        cols = pl.ds(pl.multiple_of(j * width, width), width)
        part = jnp.dot(tokv[...], wv[:, cols], preferred_element_type=F32)
        for lh in range(width // 128):
            sums[j * (width // 128) + lh] = part[:, lh * 128 : lh * 128 + 128]

    for copy in late_copies:
        copy.wait()


def late_products(sizes, signals, late_tok, pieces, sums, acc):
    rows, depth, width, modes, seq = sizes
    k = depth // 16
    first, last = signals
    halves = width // 128

    @pl.loop(first, last)
    def _(j):
        cols = pl.ds(pl.multiple_of(j * width, width), width)
        part = sum(
            jnp.dot(late_tok[:, i * k : i * k + k], piece[:, cols], preferred_element_type=F32)
            for i, piece in enumerate(pieces)
        )
        for lh in range(halves):
            new = part[:, lh * 128 : lh * 128 + 128]
            acc[(j - first) * halves + lh] = (sums[j * halves + lh] + new).astype(BF16).astype(F32)


def filtered(sizes, signals, lh, acc, taps, mine):
    rows, depth, width, modes, seq = sizes
    steps = 2 * rows // SUB
    halves = width // 128
    count = signals[1] - signals[0]
    weights = [[taps[lag, j : j + 1, mine] for j in range(*signals)] for lag in range(3)]

    def read(start):
        return [acc[j * halves + lh, pl.ds(start, SUB, stride=steps), :] for j in range(count)]

    def features(now, last, before):
        return [
            weights[0][j] * now[j] + weights[1][j] * last[j] + weights[2][j] * before[j]
            for j in range(count)
        ]

    return read, features


def state_kernel(sizes, *refs):
    rows, depth, width, modes, seq = sizes
    pos, late_tok, *pieces = refs[:-8]
    sums, taps, decay, product, gated, states_out, acc, state = refs[-8:]
    c = pos[3]
    late_products(sizes, (0, 1), late_tok, pieces, sums, gated)
    late_products(sizes, (1, 3), late_tok, pieces, sums, acc)
    steps = 2 * rows // SUB
    for lh in range(width // 128):
        mine = pl.ds(pl.multiple_of(c * width + lh * 128, 128), 128)
        lanes = pl.ds(lh * 128, 128)
        read, features = filtered(sizes, (1, 3), lh, acc, taps, mine)
        rates = [jnp.broadcast_to(decay[m : m + 1, mine] / seq, (SUB, 128)) for m in range(modes)]
        factors = [jnp.exp(-rate) for rate in rates]

        def step(t, carry):
            before, last, states = carry
            now = read(HALO + t)
            f = features(now, last, before)
            p = f[0] * f[1]
            product[t, :, lanes] = p
            return last, now, [a * s + p for a, s in zip(factors, states)]

        zero = jnp.zeros((SUB, 128), F32)
        carry = (read(HALO - 2), read(HALO - 1), [zero] * modes)
        states = lax.fori_loop(0, steps, step, carry, unroll=8)[2]
        line = lax.broadcasted_iota(jnp.int32, (SUB, 128), 0).astype(F32)
        left = (SUB - 1.0 - line) * float(steps)
        for m in range(modes):
            total = jnp.sum(jnp.exp(-rates[m] * left) * states[m], axis=0, keepdims=True)
            state[m : m + 1, lanes] = total
    for r in range(16):
        states_out[r] = state[...]


def local_kernel(sizes, pos, gated, taps, product, gain, decay, skip, gate, local, inside):
    rows, depth, width, modes, seq = sizes
    c = pos[3]
    steps = 2 * rows // SUB
    for lh in range(width // 128):
        mine = pl.ds(pl.multiple_of(c * width + lh * 128, 128), 128)
        lanes = pl.ds(lh * 128, 128)
        read, features = filtered(sizes, (0, 1), lh, gated, taps, mine)
        rates = [jnp.broadcast_to(decay[m : m + 1, mine] / seq, (SUB, 128)) for m in range(modes)]
        factors = [jnp.exp(-rate) for rate in rates]
        heights = [gain[m : m + 1, mine] * jnp.sqrt(2.0 * rates[m]) for m in range(modes)]
        direct = jnp.broadcast_to(skip[:, mine], (SUB, 128))

        def gates(t, carry):
            before, last = carry
            now = read(HALO + t)
            gate[t, :, lanes] = features(now, last, before)[0]
            return last, now

        lax.fori_loop(0, steps, gates, (read(HALO - 2), read(HALO - 1)), unroll=8)

        def step(t, states):
            p = product[t, :, lanes]
            states = [a * s + p for a, s in zip(factors, states)]
            parts = [w * s for w, s in zip(heights, states)]
            while len(parts) > 1:
                parts = [a + b for a, b in zip(parts[::2], parts[1::2])]
            local[t, :, lanes] = parts[0] + direct * p
            return states

        states = lax.fori_loop(0, steps, step, [jnp.zeros((SUB, 128), F32)] * modes, unroll=4)
        line = lax.broadcasted_iota(jnp.int32, (SUB, 128), 0)

        def later(value, by):
            return jnp.where(line >= by, pltpu.roll(value, by, 0), 0.0)

        for m in range(modes):
            s = states[m]
            for by in (1, 2, 4):
                s = s + jnp.exp(-float(steps * by) * rates[m]) * later(s, by)
            inside[m, :, lanes] = later(s, 1)


def finish_kernel(sizes, pos, gate, local, inside, states, gain, decay, mine_out, their_out, start, whole):
    rows, depth, width, modes, seq = sizes
    rank, c = pos[0], pos[3]
    steps = 2 * rows // SUB
    length = 2 * rows
    for lh in range(width // 128):
        mine = pl.ds(pl.multiple_of(c * width + lh * 128, 128), 128)
        lanes = pl.ds(lh * 128, 128)
        over = jnp.exp(-float(length) * (decay[:, mine] / seq))
        entering = jnp.zeros((modes, 128), F32)
        for r in range(16):
            entering = jnp.where(r < rank, over * entering + states[r, :, lanes], entering)
        start[:, lanes] = entering
        line = lax.broadcasted_iota(jnp.int32, (SUB, 128), 0).astype(F32) * float(steps)
        factors, waves = [], []
        for m in range(modes):
            rate = jnp.broadcast_to(decay[m : m + 1, mine] / seq, (SUB, 128))
            factors.append(jnp.exp(-rate))
            height = gain[m : m + 1, mine] * jnp.sqrt(2.0 * rate)
            waves.append(height * (inside[m, :, lanes] + jnp.exp(-rate * line) * start[m : m + 1, lanes]))

        def step(t, waves):
            waves = [a * z for a, z in zip(factors, waves)]
            parts = waves
            while len(parts) > 1:
                parts = [a + b for a, b in zip(parts[::2], parts[1::2])]
            whole[lh, pl.ds(t, SUB, stride=steps), :] = gate[t, :, lanes] * (local[t, :, lanes] + parts[0])
            return waves

        lax.fori_loop(0, steps, step, waves, unroll=4)
        for out, core in ((mine_out, c), (their_out, 1 - c)):
            line = pl.ds(pl.multiple_of(core * rows, rows), rows)
            out[:, lanes] = whole[lh, line, :].astype(BF16)


def body(tokens, w_in, taps, modes_gain, decay, skip):
    rows = tokens.shape[0]
    group = w_in.shape[2]
    width = group // 2
    k = w_in.shape[0]
    modes = decay.shape[0]
    depth = tokens.shape[1] * 8
    seq = rows * 32
    sizes = (rows, depth, width, modes, seq)
    y, h, c = (lax.axis_index(a) for a in CTX)
    pos = jnp.stack([y * 4 + h, y, h, c, lax.axis_index("l")]).astype(jnp.int32)

    tie = lax.optimization_barrier
    with jax.named_scope("weight_gather"):
        halves = w_in.reshape(k, 3, 2, width).transpose(2, 0, 1, 3).reshape(2, k, 3 * width)
        mine = lax.dynamic_index_in_dim(halves, c, 0, keepdims=False)
        theirs = lax.ppermute(lax.dynamic_index_in_dim(halves, 1 - c, 0, keepdims=False), "c", SWAP)
        own = in_order(c == 0, mine, theirs, 0)
    with jax.named_scope("token_halo"):
        route = [(i, i + 1) for i in range(1, 31, 2)]
        halo = lax.ppermute(tokens[rows - HALO :], CTX, route)
    with jax.named_scope("weight_rings"):
        farther = shifted(own, "y", 2)
        far = both_ways(own, "y")
        beside = both_ways(own, "h")
        halo, far = tie((halo, far))
    with jax.named_scope("token_swap"):
        other = lax.ppermute(jnp.concatenate([halo, tokens], 0), "l", SWAP)
    first = (halo, other, farther, far, beside)
    halo, other, farther, far, beside = tie(first)
    with jax.named_scope("token_gather"):
        near = lax.all_gather(tokens, ("c", "x"), axis=0, tiled=True)
        wide = jnp.concatenate([halo, other], 0)
        swapped = lax.all_gather(wide, ("c", "x"), axis=0, tiled=True)
    with jax.named_scope("weight_rings"):
        two, half = 2 * k, k
        moves = [(0, 0, two, 0, 0), (1, 0, two, 0, two), (0, 0, half, 1, 0), (1, half, half, 2, 0)]
        pair, low, high = relayed(beside, moves, "relay_pair")
        far_pair = both_ways(pair, "y")
        opposite = shifted(low, "h", 1), shifted(high, "h", -1)
        far_pair, opposite = tie((far_pair, opposite))
        moves = [(0, 0, two, 0, 0), (1, two, two, 1, 0)]
        moves += [(side, 0, half, 2, side * half) for side in range(2)]
        moves += [(side, two + half, half, 3, side * half) for side in range(2)]
        moves += [(2 + side, 0, half, 4, side * half) for side in range(2)]
        behind, ahead, firsts, seconds, opposite = relayed([*far_pair, *opposite], moves, "relay_far")
        last = shifted(opposite, "y", 2)
        farther_pair = shifted(behind, "y", 1), shifted(ahead, "y", -1)
        far_opposite = shifted(firsts, "h", 1), shifted(seconds, "h", -1)

    early = [own, pair, opposite]
    early_runs = [(0, dh, 0, two) for dh in (0, 1, -1, 2)]
    for side, dy in enumerate((1, -1)):
        early += [far[side], far_pair[side]]
        early_runs += [(dy, dh, 0, two) for dh in (0, 1, -1)]
    early += [farther]
    early_runs += [(2, 0, 0, two)]
    late = [*farther_pair, *far_opposite, last]
    late_runs = [(2, 1, 0, two), (2, -1, 0, two)]
    late_runs += [(dy, 2, skip, half) for skip in (0, half) for dy in (1, -1)]
    late_runs += [(2, 2, 0, two)]

    vmem = pl.BlockSpec(memory_space=pltpu.VMEM)
    smem = pl.BlockSpec(memory_space=pltpu.SMEM)
    hbm = pl.BlockSpec(memory_space=pltpu.HBM)
    block = (2 * rows // SUB, SUB, width)
    full = jax.ShapeDtypeStruct(block, F32)
    lines = 2 * rows + HALO
    chunks = (3 * width // 128, lines, 128)

    def dma(n):
        return pltpu.SemaphoreType.DMA((n,))

    sums, late_tok = pl.pallas_call(
        functools.partial(project_kernel, sizes, early_runs, late_runs),
        out_shape=(
            jax.ShapeDtypeStruct(chunks, F32),
            jax.ShapeDtypeStruct((lines, 5 * two), BF16),
        ),
        in_specs=[smem] + [hbm] * (2 + len(early)),
        out_specs=(vmem, vmem),
        scratch_shapes=[
            pltpu.VMEM((lines, 11 * two), BF16),
            pltpu.VMEM((11 * two, 3 * width), BF16),
            dma(3 * len(early_runs)),
            dma(3 * len(late_runs)),
            dma(len(early)),
        ],
        compiler_params=pltpu.CompilerParams(vmem_limit_bytes=14 * 2**20),
        cost_estimate=pl.CostEstimate(
            flops=2 * lines * 11 * two * 3 * width, bytes_accessed=9_000_000, transcendentals=0
        ),
        name="project",
    )(pos, near, swapped, *early)
    params = pltpu.CompilerParams(vmem_limit_bytes=8 * 2**20)
    product, gated, state = pl.pallas_call(
        functools.partial(state_kernel, sizes),
        out_shape=(
            full,
            jax.ShapeDtypeStruct((width // 128, lines, 128), F32),
            jax.ShapeDtypeStruct((16, modes, width), F32),
        ),
        in_specs=[smem] + [vmem] * (4 + len(late)),
        out_specs=(vmem,) * 3,
        scratch_shapes=[
            pltpu.VMEM((2 * width // 128, lines, 128), F32),
            pltpu.VMEM((modes, width), F32),
        ],
        compiler_params=params,
        name="states",
    )(pos, late_tok, *late, sums, taps, decay)

    with jax.named_scope("state_exchange"):
        states = lax.all_to_all(state, ("y", "h"), 0, 0, tiled=True)
    gate, local, inside = pl.pallas_call(
        functools.partial(local_kernel, sizes),
        out_shape=(full, full, jax.ShapeDtypeStruct((modes, SUB, width), F32)),
        in_specs=[smem] + [vmem] * 6,
        out_specs=(vmem,) * 3,
        compiler_params=params,
        cost_estimate=pl.CostEstimate(
            flops=30_000_000, bytes_accessed=2_000_000, transcendentals=0
        ),
        name="local",
    )(pos, gated, taps, product, modes_gain, decay, skip.reshape(1, group))
    mine, theirs = pl.pallas_call(
        functools.partial(finish_kernel, sizes),
        out_shape=(jax.ShapeDtypeStruct((rows, width), BF16),) * 2,
        in_specs=[smem] + [vmem] * 6,
        out_specs=(vmem, vmem),
        scratch_shapes=[pltpu.VMEM((modes, width), F32), pltpu.VMEM((width // 128, 2 * rows, 128), F32)],
        compiler_params=params,
        name="finish",
    )(pos, gate, local, inside, states, modes_gain, decay)
    with jax.named_scope("result_swap"):
        return in_order(c == 0, mine, lax.ppermute(theirs, "c", SWAP), 1)


def solution(mesh):
    split = Mesh(mesh.devices.reshape(4, 4, 2, 2, 4), AXES)
    return jax.shard_map(
        body,
        mesh=split,
        in_specs=(
            P(CTX, CH),
            P(CTX, None, CH),
            P(None, None, CH),
            P(None, CH),
            P(None, CH),
            P(CH),
        ),
        out_specs=P(CTX, CH),
        check_vma=False,
    )
```

```python
import functools

import jax
import jax.numpy as jnp
from jax import lax
from jax.experimental import pallas as pl
from jax.experimental.pallas import tpu as pltpu
from jax.sharding import Mesh
from jax.sharding import PartitionSpec as P

AXES = ("y", "h", "c", "l", "x")
CTX = ("y", "h", "c")
CH = ("l", "x")
F32 = jnp.float32
BF16 = jnp.bfloat16
HALO = 16
SWAP = [(0, 1), (1, 0)]
SUB = 8


def shifted(array, axis, step):
    n = lax.axis_size(axis)
    return lax.ppermute(array, axis, [(i, (i + step) % n) for i in range(n)])


def in_order(mine_first, mine, theirs, axis):
    first, second = jnp.where(mine_first, mine, theirs), jnp.where(mine_first, theirs, mine)
    return jnp.concatenate([first, second], axis)


def both_ways(piece, axis):
    return shifted(piece, axis, 1), shifted(piece, axis, -1)


def relay_kernel(moves, count, *refs):
    sources, targets, sem = refs[:count], refs[count:-1], refs[-1]
    copies = []
    for number, (source, first, n, target, at) in enumerate(moves):
        copies.append(
            pltpu.make_async_copy(
                sources[source].at[pl.ds(first, n), :],
                targets[target].at[pl.ds(at, n), :],
                sem.at[number],
            )
        )
        copies[-1].start()
    for copy in copies:
        copy.wait()


def relayed(sources, moves, name):
    heights = [max(at + n for _, _, n, target, at in moves if target == t) for t in range(1 + max(m[3] for m in moves))]
    anywhere = pl.BlockSpec(memory_space=pl.ANY)
    return pl.pallas_call(
        functools.partial(relay_kernel, moves, len(sources)),
        out_shape=[jax.ShapeDtypeStruct((h, sources[0].shape[1]), sources[0].dtype) for h in heights],
        in_specs=[anywhere] * len(sources),
        out_specs=[anywhere] * len(heights),
        scratch_shapes=[pltpu.SemaphoreType.DMA((len(moves),))],
        cost_estimate=pl.CostEstimate(flops=0, bytes_accessed=2_000_000, transcendentals=0),
        compiler_params=pltpu.CompilerParams(vmem_limit_bytes=2**20),
        name=name,
    )(*sources)


def token_copies(sizes, pos, near, swapped, runs, tokv, sem):
    rows, depth, width, modes, seq = sizes
    k = depth // 16
    lines = rows + 2 * HALO
    copies, at = [], 0

    def add(source, target):
        copies.append(pltpu.make_async_copy(source, target, sem.at[len(copies)]))
        return copies[-1]

    for dy, dh, skip, n in runs:
        ys, hs = lax.rem(pos[1] - dy + 4, 4), lax.rem(pos[2] - dh + 4, 4)
        ch = 2 * ys + lax.div(hs, 2)
        lanes = pl.ds(pl.multiple_of(lax.rem(hs, 2) * k + skip, 128), n)
        x = lax.rem(ch, 4)
        other = lax.rem(lax.div(ch, 4) + pos[4], 2)
        to = pl.ds(at, n)
        line = pl.multiple_of(x * lines + HALO * other, HALO)
        add(swapped.at[pl.ds(line, HALO), lanes], tokv.at[pl.ds(0, HALO), to]).start()
        for core in range(2):
            target = tokv.at[pl.ds(HALO + core * rows, rows), to]
            line = pl.multiple_of((4 * core + x) * rows, rows)
            copy = add(near.at[pl.ds(line, rows), lanes], target)
            pl.when(other == 0)(copy.start)
            line = pl.multiple_of((4 * core + x) * lines + 2 * HALO, HALO)
            source = swapped.at[pl.ds(line, rows), lanes]
            copy = pltpu.make_async_copy(source, target, sem.at[len(copies) - 1])
            pl.when(other == 1)(copy.start)
        at += n
    return copies


def project_kernel(sizes, early, late, *refs):
    rows, depth, width, modes, seq = sizes
    pos, near, swapped, *pieces = refs[:-7]
    sums, late_tok, tokv, wv, tok_sem, late_sem, w_sem = refs[-7:]
    copies, at = [], 0
    for number, piece in enumerate(pieces):
        n = piece.shape[0]
        copies.append(pltpu.make_async_copy(piece, wv.at[pl.ds(at, n), :], w_sem.at[number]))
        copies[-1].start()
        at += n
    copies += token_copies(sizes, pos, near, swapped, early, tokv, tok_sem)
    late_copies = token_copies(sizes, pos, near, swapped, late, late_tok, late_sem)
    for copy in copies:
        copy.wait()

    @pl.loop(0, 3)
    def _(j):
        cols = pl.ds(pl.multiple_of(j * width, width), width)
        part = jnp.dot(tokv[...], wv[:, cols], preferred_element_type=F32)
        for lh in range(width // 128):
            sums[j * (width // 128) + lh] = part[:, lh * 128 : lh * 128 + 128]

    for copy in late_copies:
        copy.wait()


def late_products(sizes, signals, late_tok, pieces, sums, acc):
    rows, depth, width, modes, seq = sizes
    k = depth // 16
    first, last = signals
    halves = width // 128

    @pl.loop(first, last)
    def _(j):
        cols = pl.ds(pl.multiple_of(j * width, width), width)
        part = sum(
            jnp.dot(late_tok[:, i * k : i * k + k], piece[:, cols], preferred_element_type=F32)
            for i, piece in enumerate(pieces)
        )
        for lh in range(halves):
            new = part[:, lh * 128 : lh * 128 + 128]
            acc[(j - first) * halves + lh] = (sums[j * halves + lh] + new).astype(BF16).astype(F32)


def filtered(sizes, signals, lh, acc, taps, mine):
    rows, depth, width, modes, seq = sizes
    steps = 2 * rows // SUB
    halves = width // 128
    count = signals[1] - signals[0]
    weights = [[taps[lag, j : j + 1, mine] for j in range(*signals)] for lag in range(3)]

    def read(start):
        return [acc[j * halves + lh, pl.ds(start, SUB, stride=steps), :] for j in range(count)]

    def features(now, last, before):
        return [
            weights[0][j] * now[j] + weights[1][j] * last[j] + weights[2][j] * before[j]
            for j in range(count)
        ]

    return read, features


def state_kernel(sizes, *refs):
    rows, depth, width, modes, seq = sizes
    pos, late_tok, *pieces = refs[:-8]
    sums, taps, decay, product, gated, states_out, acc, state = refs[-8:]
    c = pos[3]
    late_products(sizes, (0, 1), late_tok, pieces, sums, gated)
    late_products(sizes, (1, 3), late_tok, pieces, sums, acc)
    steps = 2 * rows // SUB
    for lh in range(width // 128):
        mine = pl.ds(pl.multiple_of(c * width + lh * 128, 128), 128)
        lanes = pl.ds(lh * 128, 128)
        read, features = filtered(sizes, (1, 3), lh, acc, taps, mine)
        rates = [jnp.broadcast_to(decay[m : m + 1, mine] / seq, (SUB, 128)) for m in range(modes)]
        factors = [jnp.exp(-rate) for rate in rates]

        def step(t, carry):
            before, last, states = carry
            now = read(HALO + t)
            f = features(now, last, before)
            p = f[0] * f[1]
            product[t, :, lanes] = p
            return last, now, [a * s + p for a, s in zip(factors, states)]

        zero = jnp.zeros((SUB, 128), F32)
        carry = (read(HALO - 2), read(HALO - 1), [zero] * modes)
        states = lax.fori_loop(0, steps, step, carry, unroll=8)[2]
        line = lax.broadcasted_iota(jnp.int32, (SUB, 128), 0).astype(F32)
        left = (SUB - 1.0 - line) * float(steps)
        for m in range(modes):
            total = jnp.sum(jnp.exp(-rates[m] * left) * states[m], axis=0, keepdims=True)
            state[m : m + 1, lanes] = total
    for r in range(16):
        states_out[r] = state[...]


def local_kernel(sizes, pos, gated, taps, product, gain, decay, skip, gate, local, inside):
    rows, depth, width, modes, seq = sizes
    c = pos[3]
    steps = 2 * rows // SUB
    for lh in range(width // 128):
        mine = pl.ds(pl.multiple_of(c * width + lh * 128, 128), 128)
        lanes = pl.ds(lh * 128, 128)
        read, features = filtered(sizes, (0, 1), lh, gated, taps, mine)
        rates = [jnp.broadcast_to(decay[m : m + 1, mine] / seq, (SUB, 128)) for m in range(modes)]
        factors = [jnp.exp(-rate) for rate in rates]
        heights = [gain[m : m + 1, mine] * jnp.sqrt(2.0 * rates[m]) for m in range(modes)]
        direct = jnp.broadcast_to(skip[:, mine], (SUB, 128))

        def gates(t, carry):
            before, last = carry
            now = read(HALO + t)
            gate[t, :, lanes] = features(now, last, before)[0]
            return last, now

        lax.fori_loop(0, steps, gates, (read(HALO - 2), read(HALO - 1)), unroll=8)

        def step(t, states):
            p = product[t, :, lanes]
            states = [a * s + p for a, s in zip(factors, states)]
            parts = [w * s for w, s in zip(heights, states)]
            while len(parts) > 1:
                parts = [a + b for a, b in zip(parts[::2], parts[1::2])]
            local[t, :, lanes] = parts[0] + direct * p
            return states

        states = lax.fori_loop(0, steps, step, [jnp.zeros((SUB, 128), F32)] * modes, unroll=4)
        line = lax.broadcasted_iota(jnp.int32, (SUB, 128), 0)

        def later(value, by):
            return jnp.where(line >= by, pltpu.roll(value, by, 0), 0.0)

        for m in range(modes):
            s = states[m]
            for by in (1, 2, 4):
                s = s + jnp.exp(-float(steps * by) * rates[m]) * later(s, by)
            inside[m, :, lanes] = later(s, 1)


def finish_kernel(sizes, pos, gate, local, inside, states, gain, decay, mine_out, their_out, start, whole):
    rows, depth, width, modes, seq = sizes
    rank, c = pos[0], pos[3]
    steps = 2 * rows // SUB
    length = 2 * rows
    for lh in range(width // 128):
        mine = pl.ds(pl.multiple_of(c * width + lh * 128, 128), 128)
        lanes = pl.ds(lh * 128, 128)
        over = jnp.exp(-float(length) * (decay[:, mine] / seq))
        entering = jnp.zeros((modes, 128), F32)
        for r in range(16):
            entering = jnp.where(r < rank, over * entering + states[r, :, lanes], entering)
        start[:, lanes] = entering
        line = lax.broadcasted_iota(jnp.int32, (SUB, 128), 0).astype(F32) * float(steps)
        factors, waves = [], []
        for m in range(modes):
            rate = jnp.broadcast_to(decay[m : m + 1, mine] / seq, (SUB, 128))
            factors.append(jnp.exp(-rate))
            height = gain[m : m + 1, mine] * jnp.sqrt(2.0 * rate)
            waves.append(height * (inside[m, :, lanes] + jnp.exp(-rate * line) * start[m : m + 1, lanes]))

        def step(t, waves):
            waves = [a * z for a, z in zip(factors, waves)]
            parts = waves
            while len(parts) > 1:
                parts = [a + b for a, b in zip(parts[::2], parts[1::2])]
            whole[lh, pl.ds(t, SUB, stride=steps), :] = gate[t, :, lanes] * (local[t, :, lanes] + parts[0])
            return waves

        lax.fori_loop(0, steps, step, waves, unroll=4)
        for out, core in ((mine_out, c), (their_out, 1 - c)):
            line = pl.ds(pl.multiple_of(core * rows, rows), rows)
            out[:, lanes] = whole[lh, line, :].astype(BF16)


def body(tokens, w_in, taps, modes_gain, decay, skip):
    rows = tokens.shape[0]
    group = w_in.shape[2]
    width = group // 2
    k = w_in.shape[0]
    modes = decay.shape[0]
    depth = tokens.shape[1] * 8
    seq = rows * 32
    sizes = (rows, depth, width, modes, seq)
    y, h, c = (lax.axis_index(a) for a in CTX)
    pos = jnp.stack([y * 4 + h, y, h, c, lax.axis_index("l")]).astype(jnp.int32)

    tie = lax.optimization_barrier
    with jax.named_scope("weight_gather"):
        halves = w_in.reshape(k, 3, 2, width).transpose(2, 0, 1, 3).reshape(2, k, 3 * width)
        mine = lax.dynamic_index_in_dim(halves, c, 0, keepdims=False)
        theirs = lax.ppermute(lax.dynamic_index_in_dim(halves, 1 - c, 0, keepdims=False), "c", SWAP)
        own = in_order(c == 0, mine, theirs, 0)
    with jax.named_scope("token_swap"):
        both = lax.all_to_all(jnp.broadcast_to(tokens, (2, rows, group)), "l", 0, 0)
        other = lax.dynamic_index_in_dim(both, 1 - lax.axis_index("l"), 0, keepdims=False)
    with jax.named_scope("weight_rings"):
        farther = shifted(own, "y", 2)
        far = both_ways(own, "y")
        beside = both_ways(own, "h")
        other, far = tie((other, far))
        tails = jnp.concatenate([tokens[rows - HALO :], other[rows - HALO :]], 0)
        halos = lax.ppermute(tails, CTX, [(i, i + 1) for i in range(1, 31, 2)])
    first = (halos, other, farther, far, beside)
    halos, other, farther, far, beside = tie(first)
    with jax.named_scope("token_gather"):
        near = lax.all_gather(tokens, ("c", "x"), axis=0, tiled=True)
        wide = jnp.concatenate([halos, other], 0)
        swapped = lax.all_gather(wide, ("c", "x"), axis=0, tiled=True)
    with jax.named_scope("weight_rings"):
        two, half = 2 * k, k
        moves = [(0, 0, two, 0, 0), (1, 0, two, 0, two), (0, 0, half, 1, 0), (1, half, half, 2, 0)]
        pair, low, high = relayed(beside, moves, "relay_pair")
        far_pair = both_ways(pair, "y")
        opposite = shifted(low, "h", 1), shifted(high, "h", -1)
        far_pair, opposite = tie((far_pair, opposite))
        moves = [(0, 0, two, 0, 0), (1, two, two, 1, 0)]
        moves += [(side, 0, half, 2, side * half) for side in range(2)]
        moves += [(side, two + half, half, 3, side * half) for side in range(2)]
        moves += [(2 + side, 0, half, 4, side * half) for side in range(2)]
        behind, ahead, firsts, seconds, opposite = relayed([*far_pair, *opposite], moves, "relay_far")
        last = shifted(opposite, "y", 2)
        farther_pair = shifted(behind, "y", 1), shifted(ahead, "y", -1)
        far_opposite = shifted(firsts, "h", 1), shifted(seconds, "h", -1)

    early = [own, pair, opposite]
    early_runs = [(0, dh, 0, two) for dh in (0, 1, -1, 2)]
    for side, dy in enumerate((1, -1)):
        early += [far[side], far_pair[side]]
        early_runs += [(dy, dh, 0, two) for dh in (0, 1, -1)]
    early += [farther]
    early_runs += [(2, 0, 0, two)]
    late = [*farther_pair, *far_opposite, last]
    late_runs = [(2, 1, 0, two), (2, -1, 0, two)]
    late_runs += [(dy, 2, skip, half) for skip in (0, half) for dy in (1, -1)]
    late_runs += [(2, 2, 0, two)]

    vmem = pl.BlockSpec(memory_space=pltpu.VMEM)
    smem = pl.BlockSpec(memory_space=pltpu.SMEM)
    hbm = pl.BlockSpec(memory_space=pltpu.HBM)
    block = (2 * rows // SUB, SUB, width)
    full = jax.ShapeDtypeStruct(block, F32)
    lines = 2 * rows + HALO
    chunks = (3 * width // 128, lines, 128)

    def dma(n):
        return pltpu.SemaphoreType.DMA((n,))

    sums, late_tok = pl.pallas_call(
        functools.partial(project_kernel, sizes, early_runs, late_runs),
        out_shape=(
            jax.ShapeDtypeStruct(chunks, F32),
            jax.ShapeDtypeStruct((lines, 5 * two), BF16),
        ),
        in_specs=[smem] + [hbm] * (2 + len(early)),
        out_specs=(vmem, vmem),
        scratch_shapes=[
            pltpu.VMEM((lines, 11 * two), BF16),
            pltpu.VMEM((11 * two, 3 * width), BF16),
            dma(3 * len(early_runs)),
            dma(3 * len(late_runs)),
            dma(len(early)),
        ],
        compiler_params=pltpu.CompilerParams(vmem_limit_bytes=14 * 2**20),
        cost_estimate=pl.CostEstimate(
            flops=2 * lines * 11 * two * 3 * width, bytes_accessed=9_000_000, transcendentals=0
        ),
        name="project",
    )(pos, near, swapped, *early)
    params = pltpu.CompilerParams(vmem_limit_bytes=8 * 2**20)
    product, gated, state = pl.pallas_call(
        functools.partial(state_kernel, sizes),
        out_shape=(
            full,
            jax.ShapeDtypeStruct((width // 128, lines, 128), F32),
            jax.ShapeDtypeStruct((16, modes, width), F32),
        ),
        in_specs=[smem] + [vmem] * (4 + len(late)),
        out_specs=(vmem,) * 3,
        scratch_shapes=[
            pltpu.VMEM((2 * width // 128, lines, 128), F32),
            pltpu.VMEM((modes, width), F32),
        ],
        compiler_params=params,
        name="states",
    )(pos, late_tok, *late, sums, taps, decay)

    with jax.named_scope("state_exchange"):
        states = lax.all_to_all(state, ("y", "h"), 0, 0, tiled=True)
    gate, local, inside = pl.pallas_call(
        functools.partial(local_kernel, sizes),
        out_shape=(full, full, jax.ShapeDtypeStruct((modes, SUB, width), F32)),
        in_specs=[smem] + [vmem] * 6,
        out_specs=(vmem,) * 3,
        compiler_params=params,
        cost_estimate=pl.CostEstimate(
            flops=30_000_000, bytes_accessed=2_000_000, transcendentals=0
        ),
        name="local",
    )(pos, gated, taps, product, modes_gain, decay, skip.reshape(1, group))
    mine, theirs = pl.pallas_call(
        functools.partial(finish_kernel, sizes),
        out_shape=(jax.ShapeDtypeStruct((rows, width), BF16),) * 2,
        in_specs=[smem] + [vmem] * 6,
        out_specs=(vmem, vmem),
        scratch_shapes=[pltpu.VMEM((modes, width), F32), pltpu.VMEM((width // 128, 2 * rows, 128), F32)],
        compiler_params=params,
        name="finish",
    )(pos, gate, local, inside, states, modes_gain, decay)
    with jax.named_scope("result_swap"):
        return in_order(c == 0, mine, lax.ppermute(theirs, "c", SWAP), 1)


def solution(mesh):
    split = Mesh(mesh.devices.reshape(4, 4, 2, 2, 4), AXES)
    return jax.shard_map(
        body,
        mesh=split,
        in_specs=(
            P(CTX, CH),
            P(CTX, None, CH),
            P(None, None, CH),
            P(None, CH),
            P(None, CH),
            P(CH),
        ),
        out_specs=P(CTX, CH),
        check_vma=False,
    )
```

```python
import functools

import jax
import jax.numpy as jnp
from jax import lax
from jax.experimental import pallas as pl
from jax.experimental.pallas import tpu as pltpu
from jax.sharding import Mesh
from jax.sharding import PartitionSpec as P

AXES = ("y", "h", "c", "l", "x")
CTX = ("y", "h", "c")
CH = ("l", "x")
F32 = jnp.float32
BF16 = jnp.bfloat16
HALO = 16
SWAP = [(0, 1), (1, 0)]
SUB = 8


def shifted(array, axis, step):
    n = lax.axis_size(axis)
    return lax.ppermute(array, axis, [(i, (i + step) % n) for i in range(n)])


def in_order(mine_first, mine, theirs, axis):
    first, second = jnp.where(mine_first, mine, theirs), jnp.where(mine_first, theirs, mine)
    return jnp.concatenate([first, second], axis)


def both_ways(piece, axis):
    return shifted(piece, axis, 1), shifted(piece, axis, -1)


def relay_kernel(moves, count, *refs):
    sources, targets, sem = refs[:count], refs[count:-1], refs[-1]
    copies = []
    for number, (source, first, n, target, at) in enumerate(moves):
        copies.append(
            pltpu.make_async_copy(
                sources[source].at[pl.ds(first, n), :],
                targets[target].at[pl.ds(at, n), :],
                sem.at[number],
            )
        )
        copies[-1].start()
    for copy in copies:
        copy.wait()


def relayed(sources, moves, name):
    heights = [max(at + n for _, _, n, target, at in moves if target == t) for t in range(1 + max(m[3] for m in moves))]
    anywhere = pl.BlockSpec(memory_space=pl.ANY)
    return pl.pallas_call(
        functools.partial(relay_kernel, moves, len(sources)),
        out_shape=[jax.ShapeDtypeStruct((h, sources[0].shape[1]), sources[0].dtype) for h in heights],
        in_specs=[anywhere] * len(sources),
        out_specs=[anywhere] * len(heights),
        scratch_shapes=[pltpu.SemaphoreType.DMA((len(moves),))],
        cost_estimate=pl.CostEstimate(flops=0, bytes_accessed=2_000_000, transcendentals=0),
        compiler_params=pltpu.CompilerParams(vmem_limit_bytes=2**20),
        name=name,
    )(*sources)


def token_copies(sizes, pos, near, swapped, runs, tokv, sem):
    rows, depth, width, modes, seq = sizes
    k = depth // 16
    lines = rows + 2 * HALO
    copies, at = [], 0

    def add(source, target):
        copies.append(pltpu.make_async_copy(source, target, sem.at[len(copies)]))
        return copies[-1]

    for dy, dh, skip, n in runs:
        ys, hs = lax.rem(pos[1] - dy + 4, 4), lax.rem(pos[2] - dh + 4, 4)
        ch = 2 * ys + lax.div(hs, 2)
        lanes = pl.ds(pl.multiple_of(lax.rem(hs, 2) * k + skip, 128), n)
        x = lax.rem(ch, 4)
        other = lax.rem(lax.div(ch, 4) + pos[4], 2)
        to = pl.ds(at, n)
        line = pl.multiple_of(x * lines + HALO * other, HALO)
        add(swapped.at[pl.ds(line, HALO), lanes], tokv.at[pl.ds(0, HALO), to]).start()
        for core in range(2):
            target = tokv.at[pl.ds(HALO + core * rows, rows), to]
            line = pl.multiple_of((4 * core + x) * rows, rows)
            copy = add(near.at[pl.ds(line, rows), lanes], target)
            pl.when(other == 0)(copy.start)
            line = pl.multiple_of((4 * core + x) * lines + 2 * HALO, HALO)
            source = swapped.at[pl.ds(line, rows), lanes]
            copy = pltpu.make_async_copy(source, target, sem.at[len(copies) - 1])
            pl.when(other == 1)(copy.start)
        at += n
    return copies


def project_kernel(sizes, early, late, *refs):
    rows, depth, width, modes, seq = sizes
    pos, near, swapped, *pieces = refs[:-7]
    sums, late_tok, tokv, wv, tok_sem, late_sem, w_sem = refs[-7:]
    copies, at = [], 0
    for number, piece in enumerate(pieces):
        n = piece.shape[0]
        copies.append(pltpu.make_async_copy(piece, wv.at[pl.ds(at, n), :], w_sem.at[number]))
        copies[-1].start()
        at += n
    copies += token_copies(sizes, pos, near, swapped, early, tokv, tok_sem)
    late_copies = token_copies(sizes, pos, near, swapped, late, late_tok, late_sem)
    for copy in copies:
        copy.wait()

    @pl.loop(0, 3)
    def _(j):
        cols = pl.ds(pl.multiple_of(j * width, width), width)
        part = jnp.dot(tokv[...], wv[:, cols], preferred_element_type=F32)
        for lh in range(width // 128):
            sums[j * (width // 128) + lh] = part[:, lh * 128 : lh * 128 + 128]

    for copy in late_copies:
        copy.wait()


def late_products(sizes, signals, late_tok, pieces, sums, acc):
    rows, depth, width, modes, seq = sizes
    first, last = signals
    halves = width // 128

    @pl.loop(first, last)
    def _(j):
        cols = pl.ds(pl.multiple_of(j * width, width), width)
        part, at = 0.0, 0
        for piece in pieces:
            n = piece.shape[0]
            part += jnp.dot(late_tok[:, at : at + n], piece[:, cols], preferred_element_type=F32)
            at += n
        for lh in range(halves):
            new = part[:, lh * 128 : lh * 128 + 128]
            acc[(j - first) * halves + lh] = (sums[j * halves + lh] + new).astype(BF16).astype(F32)


def filtered(sizes, signals, lh, acc, taps, mine):
    rows, depth, width, modes, seq = sizes
    steps = 2 * rows // SUB
    halves = width // 128
    count = signals[1] - signals[0]
    weights = [[taps[lag, j : j + 1, mine] for j in range(*signals)] for lag in range(3)]

    def read(start):
        return [acc[j * halves + lh, pl.ds(start, SUB, stride=steps), :] for j in range(count)]

    def features(now, last, before):
        return [
            weights[0][j] * now[j] + weights[1][j] * last[j] + weights[2][j] * before[j]
            for j in range(count)
        ]

    return read, features


def state_kernel(sizes, *refs):
    rows, depth, width, modes, seq = sizes
    pos, late_tok, *pieces = refs[:-8]
    sums, taps, decay, product, gated, states_out, acc, state = refs[-8:]
    c = pos[3]
    late_products(sizes, (0, 1), late_tok, pieces, sums, gated)
    late_products(sizes, (1, 3), late_tok, pieces, sums, acc)
    steps = 2 * rows // SUB
    for lh in range(width // 128):
        mine = pl.ds(pl.multiple_of(c * width + lh * 128, 128), 128)
        lanes = pl.ds(lh * 128, 128)
        read, features = filtered(sizes, (1, 3), lh, acc, taps, mine)
        rates = [jnp.broadcast_to(decay[m : m + 1, mine] / seq, (SUB, 128)) for m in range(modes)]
        factors = [jnp.exp(-rate) for rate in rates]

        def step(t, carry):
            before, last, states = carry
            now = read(HALO + t)
            f = features(now, last, before)
            p = f[0] * f[1]
            product[t, :, lanes] = p
            return last, now, [a * s + p for a, s in zip(factors, states)]

        zero = jnp.zeros((SUB, 128), F32)
        carry = (read(HALO - 2), read(HALO - 1), [zero] * modes)
        states = lax.fori_loop(0, steps, step, carry, unroll=8)[2]
        line = lax.broadcasted_iota(jnp.int32, (SUB, 128), 0).astype(F32)
        left = (SUB - 1.0 - line) * float(steps)
        for m in range(modes):
            total = jnp.sum(jnp.exp(-rates[m] * left) * states[m], axis=0, keepdims=True)
            state[m : m + 1, lanes] = total
    for r in range(16):
        states_out[r] = state[...]


def local_kernel(sizes, pos, gated, taps, product, gain, decay, skip, gate, local, inside):
    rows, depth, width, modes, seq = sizes
    c = pos[3]
    steps = 2 * rows // SUB
    for lh in range(width // 128):
        mine = pl.ds(pl.multiple_of(c * width + lh * 128, 128), 128)
        lanes = pl.ds(lh * 128, 128)
        read, features = filtered(sizes, (0, 1), lh, gated, taps, mine)
        rates = [jnp.broadcast_to(decay[m : m + 1, mine] / seq, (SUB, 128)) for m in range(modes)]
        factors = [jnp.exp(-rate) for rate in rates]
        heights = [gain[m : m + 1, mine] * jnp.sqrt(2.0 * rates[m]) for m in range(modes)]
        direct = jnp.broadcast_to(skip[:, mine], (SUB, 128))

        def gates(t, carry):
            before, last = carry
            now = read(HALO + t)
            gate[t, :, lanes] = features(now, last, before)[0]
            return last, now

        lax.fori_loop(0, steps, gates, (read(HALO - 2), read(HALO - 1)), unroll=8)

        def step(t, states):
            p = product[t, :, lanes]
            states = [a * s + p for a, s in zip(factors, states)]
            parts = [w * s for w, s in zip(heights, states)]
            while len(parts) > 1:
                parts = [a + b for a, b in zip(parts[::2], parts[1::2])]
            local[t, :, lanes] = parts[0] + direct * p
            return states

        states = lax.fori_loop(0, steps, step, [jnp.zeros((SUB, 128), F32)] * modes, unroll=4)
        line = lax.broadcasted_iota(jnp.int32, (SUB, 128), 0)

        def later(value, by):
            return jnp.where(line >= by, pltpu.roll(value, by, 0), 0.0)

        for m in range(modes):
            s = states[m]
            for by in (1, 2, 4):
                s = s + jnp.exp(-float(steps * by) * rates[m]) * later(s, by)
            inside[m, :, lanes] = later(s, 1)


def finish_kernel(sizes, pos, gate, local, inside, states, gain, decay, mine_out, their_out, start, whole):
    rows, depth, width, modes, seq = sizes
    rank, c = pos[0], pos[3]
    steps = 2 * rows // SUB
    length = 2 * rows
    for lh in range(width // 128):
        mine = pl.ds(pl.multiple_of(c * width + lh * 128, 128), 128)
        lanes = pl.ds(lh * 128, 128)
        over = jnp.exp(-float(length) * (decay[:, mine] / seq))
        entering = jnp.zeros((modes, 128), F32)
        for r in range(16):
            entering = jnp.where(r < rank, over * entering + states[r, :, lanes], entering)
        start[:, lanes] = entering
        line = lax.broadcasted_iota(jnp.int32, (SUB, 128), 0).astype(F32) * float(steps)
        factors, waves = [], []
        for m in range(modes):
            rate = jnp.broadcast_to(decay[m : m + 1, mine] / seq, (SUB, 128))
            factors.append(jnp.exp(-rate))
            height = gain[m : m + 1, mine] * jnp.sqrt(2.0 * rate)
            waves.append(height * (inside[m, :, lanes] + jnp.exp(-rate * line) * start[m : m + 1, lanes]))

        def step(t, waves):
            waves = [a * z for a, z in zip(factors, waves)]
            parts = waves
            while len(parts) > 1:
                parts = [a + b for a, b in zip(parts[::2], parts[1::2])]
            whole[lh, pl.ds(t, SUB, stride=steps), :] = gate[t, :, lanes] * (local[t, :, lanes] + parts[0])
            return waves

        lax.fori_loop(0, steps, step, waves, unroll=4)
        for out, core in ((mine_out, c), (their_out, 1 - c)):
            line = pl.ds(pl.multiple_of(core * rows, rows), rows)
            out[:, lanes] = whole[lh, line, :].astype(BF16)


def body(tokens, w_in, taps, modes_gain, decay, skip):
    rows = tokens.shape[0]
    group = w_in.shape[2]
    width = group // 2
    k = w_in.shape[0]
    modes = decay.shape[0]
    depth = tokens.shape[1] * 8
    seq = rows * 32
    sizes = (rows, depth, width, modes, seq)
    y, h, c = (lax.axis_index(a) for a in CTX)
    pos = jnp.stack([y * 4 + h, y, h, c, lax.axis_index("l")]).astype(jnp.int32)

    tie = lax.optimization_barrier
    with jax.named_scope("weight_gather"):
        halves = w_in.reshape(k, 3, 2, width).transpose(2, 0, 1, 3).reshape(2, k, 3 * width)
        mine = lax.dynamic_index_in_dim(halves, c, 0, keepdims=False)
        theirs = lax.ppermute(lax.dynamic_index_in_dim(halves, 1 - c, 0, keepdims=False), "c", SWAP)
        own = in_order(c == 0, mine, theirs, 0)
    with jax.named_scope("token_swap"):
        other = lax.ppermute(tokens, "l", SWAP)
    with jax.named_scope("weight_rings"):
        far = both_ways(own, "y")
        beside = both_ways(own, "h")
        other, far = tie((other, far))
        tails = jnp.concatenate([tokens[rows - HALO :], other[rows - HALO :]], 0)
        halos = lax.ppermute(tails, CTX, [(i, i + 1) for i in range(1, 31, 2)])
    first = (halos, other, far, beside)
    halos, other, far, beside = tie(first)
    with jax.named_scope("token_gather"):
        near = lax.all_gather(tokens, ("c", "x"), axis=0, tiled=True)
        wide = jnp.concatenate([halos, other], 0)
        swapped = lax.all_gather(wide, ("c", "x"), axis=0, tiled=True)
    with jax.named_scope("weight_rings"):
        two, half = 2 * k, k
        moves = [(0, 0, two, 0, 0), (1, 0, two, 0, two), (0, 0, half, 1, 0), (1, half, half, 2, 0)]
        pair, low, high = relayed(beside, moves, "relay_pair")
        far_pair = both_ways(pair, "y")
        opposite = shifted(low, "h", 1), shifted(high, "h", -1)
        far_pair, opposite = tie((far_pair, opposite))
        moves = [(0, 0, two, 0, 0), (1, two, two, 1, 0)]
        moves += [(side, 0, half, 2, side * half) for side in range(2)]
        moves += [(side, two + half, half, 3, side * half) for side in range(2)]
        moves += [(2 + side, 0, half, 4, side * half) for side in range(2)]
        moves += [(4 + side, side * half, half, side, two) for side in range(2)]
        behind, ahead, firsts, seconds, opposite = relayed(
            [*far_pair, *opposite, *far], moves, "relay_far"
        )
        last = shifted(opposite, "y", 2)
        farther_pair = shifted(behind, "y", 1), shifted(ahead, "y", -1)
        far_opposite = shifted(firsts, "h", 1), shifted(seconds, "h", -1)

    early = [own, pair, opposite]
    early_runs = [(0, dh, 0, two) for dh in (0, 1, -1, 2)]
    for side, dy in enumerate((1, -1)):
        early += [far[side], far_pair[side]]
        early_runs += [(dy, dh, 0, two) for dh in (0, 1, -1)]
    late = [*farther_pair, *far_opposite, last]
    late_runs = [(2, 1, 0, two), (2, 0, 0, half), (2, -1, 0, two), (2, 0, half, half)]
    late_runs += [(dy, 2, skip, half) for skip in (0, half) for dy in (1, -1)]
    late_runs += [(2, 2, 0, two)]

    vmem = pl.BlockSpec(memory_space=pltpu.VMEM)
    smem = pl.BlockSpec(memory_space=pltpu.SMEM)
    hbm = pl.BlockSpec(memory_space=pltpu.HBM)
    block = (2 * rows // SUB, SUB, width)
    full = jax.ShapeDtypeStruct(block, F32)
    lines = 2 * rows + HALO
    chunks = (3 * width // 128, lines, 128)

    def dma(n):
        return pltpu.SemaphoreType.DMA((n,))

    sums, late_tok = pl.pallas_call(
        functools.partial(project_kernel, sizes, early_runs, late_runs),
        out_shape=(
            jax.ShapeDtypeStruct(chunks, F32),
            jax.ShapeDtypeStruct((lines, 6 * two), BF16),
        ),
        in_specs=[smem] + [hbm] * (2 + len(early)),
        out_specs=(vmem, vmem),
        scratch_shapes=[
            pltpu.VMEM((lines, 10 * two), BF16),
            pltpu.VMEM((10 * two, 3 * width), BF16),
            dma(3 * len(early_runs)),
            dma(3 * len(late_runs)),
            dma(len(early)),
        ],
        compiler_params=pltpu.CompilerParams(vmem_limit_bytes=14 * 2**20),
        cost_estimate=pl.CostEstimate(
            flops=2 * lines * 10 * two * 3 * width, bytes_accessed=9_000_000, transcendentals=0
        ),
        name="project",
    )(pos, near, swapped, *early)
    params = pltpu.CompilerParams(vmem_limit_bytes=8 * 2**20)
    product, gated, state = pl.pallas_call(
        functools.partial(state_kernel, sizes),
        out_shape=(
            full,
            jax.ShapeDtypeStruct((width // 128, lines, 128), F32),
            jax.ShapeDtypeStruct((16, modes, width), F32),
        ),
        in_specs=[smem] + [vmem] * (4 + len(late)),
        out_specs=(vmem,) * 3,
        scratch_shapes=[
            pltpu.VMEM((2 * width // 128, lines, 128), F32),
            pltpu.VMEM((modes, width), F32),
        ],
        compiler_params=params,
        name="states",
    )(pos, late_tok, *late, sums, taps, decay)

    with jax.named_scope("state_exchange"):
        states = lax.all_to_all(state, ("y", "h"), 0, 0, tiled=True)
    gate, local, inside = pl.pallas_call(
        functools.partial(local_kernel, sizes),
        out_shape=(full, full, jax.ShapeDtypeStruct((modes, SUB, width), F32)),
        in_specs=[smem] + [vmem] * 6,
        out_specs=(vmem,) * 3,
        compiler_params=params,
        cost_estimate=pl.CostEstimate(
            flops=30_000_000, bytes_accessed=2_000_000, transcendentals=0
        ),
        name="local",
    )(pos, gated, taps, product, modes_gain, decay, skip.reshape(1, group))
    mine, theirs = pl.pallas_call(
        functools.partial(finish_kernel, sizes),
        out_shape=(jax.ShapeDtypeStruct((rows, width), BF16),) * 2,
        in_specs=[smem] + [vmem] * 6,
        out_specs=(vmem, vmem),
        scratch_shapes=[pltpu.VMEM((modes, width), F32), pltpu.VMEM((width // 128, 2 * rows, 128), F32)],
        compiler_params=params,
        name="finish",
    )(pos, gate, local, inside, states, modes_gain, decay)
    with jax.named_scope("result_swap"):
        return in_order(c == 0, mine, lax.ppermute(theirs, "c", SWAP), 1)


def solution(mesh):
    split = Mesh(mesh.devices.reshape(4, 4, 2, 2, 4), AXES)
    return jax.shard_map(
        body,
        mesh=split,
        in_specs=(
            P(CTX, CH),
            P(CTX, None, CH),
            P(None, None, CH),
            P(None, CH),
            P(None, CH),
            P(CH),
        ),
        out_specs=P(CTX, CH),
        check_vma=False,
    )
```

```python
import functools

import jax
import jax.numpy as jnp
from jax import lax
from jax.experimental import pallas as pl
from jax.experimental.pallas import tpu as pltpu
from jax.sharding import Mesh
from jax.sharding import PartitionSpec as P

AXES = ("y", "h", "c", "l", "x")
CTX = ("y", "h", "c")
CH = ("l", "x")
F32 = jnp.float32
BF16 = jnp.bfloat16
HALO = 16
SWAP = [(0, 1), (1, 0)]
SUB = 8


def shifted(array, axis, step):
    n = lax.axis_size(axis)
    return lax.ppermute(array, axis, [(i, (i + step) % n) for i in range(n)])


def in_order(mine_first, mine, theirs, axis):
    first, second = jnp.where(mine_first, mine, theirs), jnp.where(mine_first, theirs, mine)
    return jnp.concatenate([first, second], axis)


def both_ways(piece, axis):
    return shifted(piece, axis, 1), shifted(piece, axis, -1)


def relay_kernel(moves, count, *refs):
    sources, targets, sem = refs[:count], refs[count:-1], refs[-1]
    copies = []
    for number, (source, first, n, target, at) in enumerate(moves):
        copies.append(
            pltpu.make_async_copy(
                sources[source].at[pl.ds(first, n), :],
                targets[target].at[pl.ds(at, n), :],
                sem.at[number],
            )
        )
        copies[-1].start()
    for copy in copies:
        copy.wait()


def relayed(sources, moves, name):
    heights = [max(at + n for _, _, n, target, at in moves if target == t) for t in range(1 + max(m[3] for m in moves))]
    anywhere = pl.BlockSpec(memory_space=pl.ANY)
    return pl.pallas_call(
        functools.partial(relay_kernel, moves, len(sources)),
        out_shape=[jax.ShapeDtypeStruct((h, sources[0].shape[1]), sources[0].dtype) for h in heights],
        in_specs=[anywhere] * len(sources),
        out_specs=[anywhere] * len(heights),
        scratch_shapes=[pltpu.SemaphoreType.DMA((len(moves),))],
        cost_estimate=pl.CostEstimate(flops=0, bytes_accessed=2_000_000, transcendentals=0),
        compiler_params=pltpu.CompilerParams(vmem_limit_bytes=2**20),
        name=name,
    )(*sources)


def token_copies(sizes, pos, near, swapped, runs, tokv, sem):
    rows, depth, width, modes, seq = sizes
    k = depth // 16
    lines = rows + 2 * HALO
    copies, at = [], 0

    def add(source, target):
        copies.append(pltpu.make_async_copy(source, target, sem.at[len(copies)]))
        return copies[-1]

    for dy, dh, skip, n in runs:
        ys, hs = lax.rem(pos[1] - dy + 4, 4), lax.rem(pos[2] - dh + 4, 4)
        ch = 2 * ys + lax.div(hs, 2)
        lanes = pl.ds(pl.multiple_of(lax.rem(hs, 2) * k + skip, 128), n)
        x = lax.rem(ch, 4)
        other = lax.rem(lax.div(ch, 4) + pos[4], 2)
        to = pl.ds(at, n)
        line = pl.multiple_of(x * lines + HALO * other, HALO)
        add(swapped.at[pl.ds(line, HALO), lanes], tokv.at[pl.ds(0, HALO), to]).start()
        for core in range(2):
            target = tokv.at[pl.ds(HALO + core * rows, rows), to]
            line = pl.multiple_of((4 * core + x) * rows, rows)
            copy = add(near.at[pl.ds(line, rows), lanes], target)
            pl.when(other == 0)(copy.start)
            line = pl.multiple_of((4 * core + x) * lines + 2 * HALO, HALO)
            source = swapped.at[pl.ds(line, rows), lanes]
            copy = pltpu.make_async_copy(source, target, sem.at[len(copies) - 1])
            pl.when(other == 1)(copy.start)
        at += n
    return copies


def project_kernel(sizes, early, late, *refs):
    rows, depth, width, modes, seq = sizes
    pos, near, swapped, *pieces = refs[:-7]
    sums, late_tok, tokv, wv, tok_sem, late_sem, w_sem = refs[-7:]
    copies, at = [], 0
    for number, piece in enumerate(pieces):
        n = piece.shape[0]
        copies.append(pltpu.make_async_copy(piece, wv.at[pl.ds(at, n), :], w_sem.at[number]))
        copies[-1].start()
        at += n
    copies += token_copies(sizes, pos, near, swapped, early, tokv, tok_sem)
    late_copies = token_copies(sizes, pos, near, swapped, late, late_tok, late_sem)
    for copy in copies:
        copy.wait()

    @pl.loop(0, 3)
    def _(j):
        cols = pl.ds(pl.multiple_of(j * width, width), width)
        part = jnp.dot(tokv[...], wv[:, cols], preferred_element_type=F32)
        for lh in range(width // 128):
            sums[j * (width // 128) + lh] = part[:, lh * 128 : lh * 128 + 128]

    for copy in late_copies:
        copy.wait()


def late_products(sizes, signals, late_tok, pieces, sums, acc):
    rows, depth, width, modes, seq = sizes
    k = depth // 16
    first, last = signals
    halves = width // 128

    @pl.loop(first, last)
    def _(j):
        cols = pl.ds(pl.multiple_of(j * width, width), width)
        part = sum(
            jnp.dot(late_tok[:, i * k : i * k + k], piece[:, cols], preferred_element_type=F32)
            for i, piece in enumerate(pieces)
        )
        for lh in range(halves):
            new = part[:, lh * 128 : lh * 128 + 128]
            acc[(j - first) * halves + lh] = (sums[j * halves + lh] + new).astype(BF16).astype(F32)


def filtered(sizes, signals, lh, acc, taps, mine):
    rows, depth, width, modes, seq = sizes
    steps = 2 * rows // SUB
    halves = width // 128
    count = signals[1] - signals[0]
    weights = [[taps[lag, j : j + 1, mine] for j in range(*signals)] for lag in range(3)]

    def read(start):
        return [acc[j * halves + lh, pl.ds(start, SUB, stride=steps), :] for j in range(count)]

    def features(now, last, before):
        return [
            weights[0][j] * now[j] + weights[1][j] * last[j] + weights[2][j] * before[j]
            for j in range(count)
        ]

    return read, features


def state_kernel(sizes, *refs):
    rows, depth, width, modes, seq = sizes
    pos, late_tok, *pieces = refs[:-8]
    sums, taps, decay, product, gated, states_out, acc, state = refs[-8:]
    c = pos[3]
    late_products(sizes, (0, 1), late_tok, pieces, sums, gated)
    late_products(sizes, (1, 3), late_tok, pieces, sums, acc)
    steps = 2 * rows // SUB
    for lh in range(width // 128):
        mine = pl.ds(pl.multiple_of(c * width + lh * 128, 128), 128)
        lanes = pl.ds(lh * 128, 128)
        read, features = filtered(sizes, (1, 3), lh, acc, taps, mine)
        rates = [jnp.broadcast_to(decay[m : m + 1, mine] / seq, (SUB, 128)) for m in range(modes)]
        factors = [jnp.exp(-rate) for rate in rates]

        def step(t, carry):
            before, last, states = carry
            now = read(HALO + t)
            f = features(now, last, before)
            p = f[0] * f[1]
            product[t, :, lanes] = p
            return last, now, [a * s + p for a, s in zip(factors, states)]

        zero = jnp.zeros((SUB, 128), F32)
        carry = (read(HALO - 2), read(HALO - 1), [zero] * modes)
        states = lax.fori_loop(0, steps, step, carry, unroll=8)[2]
        line = lax.broadcasted_iota(jnp.int32, (SUB, 128), 0).astype(F32)
        left = (SUB - 1.0 - line) * float(steps)
        for m in range(modes):
            total = jnp.sum(jnp.exp(-rates[m] * left) * states[m], axis=0, keepdims=True)
            state[m : m + 1, lanes] = total
    sent = state[...].astype(BF16)
    for r in range(16):
        states_out[r] = sent


def local_kernel(sizes, pos, gated, taps, product, gain, decay, skip, gate, local, inside):
    rows, depth, width, modes, seq = sizes
    c = pos[3]
    steps = 2 * rows // SUB
    for lh in range(width // 128):
        mine = pl.ds(pl.multiple_of(c * width + lh * 128, 128), 128)
        lanes = pl.ds(lh * 128, 128)
        read, features = filtered(sizes, (0, 1), lh, gated, taps, mine)
        rates = [jnp.broadcast_to(decay[m : m + 1, mine] / seq, (SUB, 128)) for m in range(modes)]
        factors = [jnp.exp(-rate) for rate in rates]
        heights = [gain[m : m + 1, mine] * jnp.sqrt(2.0 * rates[m]) for m in range(modes)]
        direct = jnp.broadcast_to(skip[:, mine], (SUB, 128))

        def gates(t, carry):
            before, last = carry
            now = read(HALO + t)
            gate[t, :, lanes] = features(now, last, before)[0]
            return last, now

        lax.fori_loop(0, steps, gates, (read(HALO - 2), read(HALO - 1)), unroll=8)

        def step(t, states):
            p = product[t, :, lanes]
            states = [a * s + p for a, s in zip(factors, states)]
            parts = [w * s for w, s in zip(heights, states)]
            while len(parts) > 1:
                parts = [a + b for a, b in zip(parts[::2], parts[1::2])]
            local[t, :, lanes] = parts[0] + direct * p
            return states

        states = lax.fori_loop(0, steps, step, [jnp.zeros((SUB, 128), F32)] * modes, unroll=4)
        line = lax.broadcasted_iota(jnp.int32, (SUB, 128), 0)

        def later(value, by):
            return jnp.where(line >= by, pltpu.roll(value, by, 0), 0.0)

        for m in range(modes):
            s = states[m]
            for by in (1, 2, 4):
                s = s + jnp.exp(-float(steps * by) * rates[m]) * later(s, by)
            inside[m, :, lanes] = later(s, 1)


def finish_kernel(sizes, pos, gate, local, inside, states, gain, decay, mine_out, their_out, start, whole):
    rows, depth, width, modes, seq = sizes
    rank, c = pos[0], pos[3]
    steps = 2 * rows // SUB
    length = 2 * rows
    for lh in range(width // 128):
        mine = pl.ds(pl.multiple_of(c * width + lh * 128, 128), 128)
        lanes = pl.ds(lh * 128, 128)
        over = jnp.exp(-float(length) * (decay[:, mine] / seq))
        entering = jnp.zeros((modes, 128), F32)
        for r in range(16):
            entering = jnp.where(r < rank, over * entering + states[r, :, lanes].astype(F32), entering)
        start[:, lanes] = entering
        line = lax.broadcasted_iota(jnp.int32, (SUB, 128), 0).astype(F32) * float(steps)
        factors, waves = [], []
        for m in range(modes):
            rate = jnp.broadcast_to(decay[m : m + 1, mine] / seq, (SUB, 128))
            factors.append(jnp.exp(-rate))
            height = gain[m : m + 1, mine] * jnp.sqrt(2.0 * rate)
            waves.append(height * (inside[m, :, lanes] + jnp.exp(-rate * line) * start[m : m + 1, lanes]))

        def step(t, waves):
            waves = [a * z for a, z in zip(factors, waves)]
            parts = waves
            while len(parts) > 1:
                parts = [a + b for a, b in zip(parts[::2], parts[1::2])]
            whole[lh, pl.ds(t, SUB, stride=steps), :] = gate[t, :, lanes] * (local[t, :, lanes] + parts[0])
            return waves

        lax.fori_loop(0, steps, step, waves, unroll=4)
        for out, core in ((mine_out, c), (their_out, 1 - c)):
            line = pl.ds(pl.multiple_of(core * rows, rows), rows)
            out[:, lanes] = whole[lh, line, :].astype(BF16)


def body(tokens, w_in, taps, modes_gain, decay, skip):
    rows = tokens.shape[0]
    group = w_in.shape[2]
    width = group // 2
    k = w_in.shape[0]
    modes = decay.shape[0]
    depth = tokens.shape[1] * 8
    seq = rows * 32
    sizes = (rows, depth, width, modes, seq)
    y, h, c = (lax.axis_index(a) for a in CTX)
    pos = jnp.stack([y * 4 + h, y, h, c, lax.axis_index("l")]).astype(jnp.int32)

    tie = lax.optimization_barrier
    with jax.named_scope("weight_gather"):
        halves = w_in.reshape(k, 3, 2, width).transpose(2, 0, 1, 3).reshape(2, k, 3 * width)
        mine = lax.dynamic_index_in_dim(halves, c, 0, keepdims=False)
        theirs = lax.ppermute(lax.dynamic_index_in_dim(halves, 1 - c, 0, keepdims=False), "c", SWAP)
        own = in_order(c == 0, mine, theirs, 0)
    with jax.named_scope("token_swap"):
        other = lax.ppermute(tokens, "l", SWAP)
    with jax.named_scope("weight_rings"):
        farther = shifted(own, "y", 2)
        far = both_ways(own, "y")
        beside = both_ways(own, "h")
        other, far = tie((other, far))
        tails = jnp.concatenate([tokens[rows - HALO :], other[rows - HALO :]], 0)
        halos = lax.ppermute(tails, CTX, [(i, i + 1) for i in range(1, 31, 2)])
    first = (halos, other, farther, far, beside)
    halos, other, farther, far, beside = tie(first)
    with jax.named_scope("token_gather"):
        near = lax.all_gather(tokens, ("c", "x"), axis=0, tiled=True)
        wide = jnp.concatenate([halos, other], 0)
        swapped = lax.all_gather(wide, ("c", "x"), axis=0, tiled=True)
    with jax.named_scope("weight_rings"):
        two, half = 2 * k, k
        moves = [(0, 0, two, 0, 0), (1, 0, two, 0, two), (0, 0, half, 1, 0), (1, half, half, 2, 0)]
        pair, low, high = relayed(beside, moves, "relay_pair")
        far_pair = both_ways(pair, "y")
        opposite = shifted(low, "h", 1), shifted(high, "h", -1)
        far_pair, opposite = tie((far_pair, opposite))
        moves = [(0, 0, two, 0, 0), (1, two, two, 1, 0)]
        moves += [(side, 0, half, 2, side * half) for side in range(2)]
        moves += [(side, two + half, half, 3, side * half) for side in range(2)]
        moves += [(2 + side, 0, half, 4, side * half) for side in range(2)]
        behind, ahead, firsts, seconds, opposite = relayed([*far_pair, *opposite], moves, "relay_far")
        last = shifted(opposite, "y", 2)
        farther_pair = shifted(behind, "y", 1), shifted(ahead, "y", -1)
        far_opposite = shifted(firsts, "h", 1), shifted(seconds, "h", -1)

    early = [own, pair, opposite]
    early_runs = [(0, dh, 0, two) for dh in (0, 1, -1, 2)]
    for side, dy in enumerate((1, -1)):
        early += [far[side], far_pair[side]]
        early_runs += [(dy, dh, 0, two) for dh in (0, 1, -1)]
    early += [farther]
    early_runs += [(2, 0, 0, two)]
    late = [*farther_pair, *far_opposite, last]
    late_runs = [(2, 1, 0, two), (2, -1, 0, two)]
    late_runs += [(dy, 2, skip, half) for skip in (0, half) for dy in (1, -1)]
    late_runs += [(2, 2, 0, two)]

    vmem = pl.BlockSpec(memory_space=pltpu.VMEM)
    smem = pl.BlockSpec(memory_space=pltpu.SMEM)
    hbm = pl.BlockSpec(memory_space=pltpu.HBM)
    block = (2 * rows // SUB, SUB, width)
    full = jax.ShapeDtypeStruct(block, F32)
    lines = 2 * rows + HALO
    chunks = (3 * width // 128, lines, 128)

    def dma(n):
        return pltpu.SemaphoreType.DMA((n,))

    sums, late_tok = pl.pallas_call(
        functools.partial(project_kernel, sizes, early_runs, late_runs),
        out_shape=(
            jax.ShapeDtypeStruct(chunks, F32),
            jax.ShapeDtypeStruct((lines, 5 * two), BF16),
        ),
        in_specs=[smem] + [hbm] * (2 + len(early)),
        out_specs=(vmem, vmem),
        scratch_shapes=[
            pltpu.VMEM((lines, 11 * two), BF16),
            pltpu.VMEM((11 * two, 3 * width), BF16),
            dma(3 * len(early_runs)),
            dma(3 * len(late_runs)),
            dma(len(early)),
        ],
        compiler_params=pltpu.CompilerParams(vmem_limit_bytes=14 * 2**20),
        cost_estimate=pl.CostEstimate(
            flops=2 * lines * 11 * two * 3 * width, bytes_accessed=9_000_000, transcendentals=0
        ),
        name="project",
    )(pos, near, swapped, *early)
    params = pltpu.CompilerParams(vmem_limit_bytes=8 * 2**20)
    product, gated, state = pl.pallas_call(
        functools.partial(state_kernel, sizes),
        out_shape=(
            full,
            jax.ShapeDtypeStruct((width // 128, lines, 128), F32),
            jax.ShapeDtypeStruct((16, modes, width), BF16),
        ),
        in_specs=[smem] + [vmem] * (4 + len(late)),
        out_specs=(vmem,) * 3,
        scratch_shapes=[
            pltpu.VMEM((2 * width // 128, lines, 128), F32),
            pltpu.VMEM((modes, width), F32),
        ],
        compiler_params=params,
        name="states",
    )(pos, late_tok, *late, sums, taps, decay)

    with jax.named_scope("state_exchange"):
        states = lax.all_to_all(state, ("y", "h"), 0, 0, tiled=True)
    gate, local, inside = pl.pallas_call(
        functools.partial(local_kernel, sizes),
        out_shape=(full, full, jax.ShapeDtypeStruct((modes, SUB, width), F32)),
        in_specs=[smem] + [vmem] * 6,
        out_specs=(vmem,) * 3,
        compiler_params=params,
        cost_estimate=pl.CostEstimate(
            flops=30_000_000, bytes_accessed=2_000_000, transcendentals=0
        ),
        name="local",
    )(pos, gated, taps, product, modes_gain, decay, skip.reshape(1, group))
    mine, theirs = pl.pallas_call(
        functools.partial(finish_kernel, sizes),
        out_shape=(jax.ShapeDtypeStruct((rows, width), BF16),) * 2,
        in_specs=[smem] + [vmem] * 6,
        out_specs=(vmem, vmem),
        scratch_shapes=[pltpu.VMEM((modes, width), F32), pltpu.VMEM((width // 128, 2 * rows, 128), F32)],
        compiler_params=params,
        name="finish",
    )(pos, gate, local, inside, states, modes_gain, decay)
    with jax.named_scope("result_swap"):
        return in_order(c == 0, mine, lax.ppermute(theirs, "c", SWAP), 1)


def solution(mesh):
    split = Mesh(mesh.devices.reshape(4, 4, 2, 2, 4), AXES)
    return jax.shard_map(
        body,
        mesh=split,
        in_specs=(
            P(CTX, CH),
            P(CTX, None, CH),
            P(None, None, CH),
            P(None, CH),
            P(None, CH),
            P(CH),
        ),
        out_specs=P(CTX, CH),
        check_vma=False,
    )
```

```python
import functools

import jax
import jax.numpy as jnp
from jax import lax
from jax.experimental import pallas as pl
from jax.experimental.pallas import tpu as pltpu
from jax.sharding import Mesh
from jax.sharding import PartitionSpec as P

AXES = ("y", "h", "c", "l", "x")
CTX = ("y", "h", "c")
CH = ("l", "x")
F32 = jnp.float32
BF16 = jnp.bfloat16
HALO = 16
SWAP = [(0, 1), (1, 0)]
SUB = 8


def shifted(array, axis, step):
    n = lax.axis_size(axis)
    return lax.ppermute(array, axis, [(i, (i + step) % n) for i in range(n)])


def in_order(mine_first, mine, theirs, axis):
    first, second = jnp.where(mine_first, mine, theirs), jnp.where(mine_first, theirs, mine)
    return jnp.concatenate([first, second], axis)


def both_ways(piece, axis):
    return shifted(piece, axis, 1), shifted(piece, axis, -1)


def relay_kernel(moves, count, *refs):
    sources, targets, sem = refs[:count], refs[count:-1], refs[-1]
    copies = []
    for number, (source, first, n, target, at) in enumerate(moves):
        copies.append(
            pltpu.make_async_copy(
                sources[source].at[pl.ds(first, n), :],
                targets[target].at[pl.ds(at, n), :],
                sem.at[number],
            )
        )
        copies[-1].start()
    for copy in copies:
        copy.wait()


def relayed(sources, moves, name):
    heights = [max(at + n for _, _, n, target, at in moves if target == t) for t in range(1 + max(m[3] for m in moves))]
    anywhere = pl.BlockSpec(memory_space=pl.ANY)
    return pl.pallas_call(
        functools.partial(relay_kernel, moves, len(sources)),
        out_shape=[jax.ShapeDtypeStruct((h, sources[0].shape[1]), sources[0].dtype) for h in heights],
        in_specs=[anywhere] * len(sources),
        out_specs=[anywhere] * len(heights),
        scratch_shapes=[pltpu.SemaphoreType.DMA((len(moves),))],
        cost_estimate=pl.CostEstimate(flops=0, bytes_accessed=2_000_000, transcendentals=0),
        compiler_params=pltpu.CompilerParams(vmem_limit_bytes=2**20),
        name=name,
    )(*sources)


def token_copies(sizes, pos, near, swapped, runs, tokv, sem):
    rows, depth, width, modes, seq = sizes
    k = depth // 16
    lines = rows + 2 * HALO
    copies, at = [], 0

    def add(source, target):
        copies.append(pltpu.make_async_copy(source, target, sem.at[len(copies)]))
        return copies[-1]

    for dy, dh, skip, n in runs:
        ys, hs = lax.rem(pos[1] - dy + 4, 4), lax.rem(pos[2] - dh + 4, 4)
        ch = 2 * ys + lax.div(hs, 2)
        lanes = pl.ds(pl.multiple_of(lax.rem(hs, 2) * k + skip, 128), n)
        x = lax.rem(ch, 4)
        other = lax.rem(lax.div(ch, 4) + pos[4], 2)
        to = pl.ds(at, n)
        line = pl.multiple_of(x * lines + HALO * other, HALO)
        add(swapped.at[pl.ds(line, HALO), lanes], tokv.at[pl.ds(0, HALO), to]).start()
        for core in range(2):
            target = tokv.at[pl.ds(HALO + core * rows, rows), to]
            line = pl.multiple_of((4 * core + x) * rows, rows)
            copy = add(near.at[pl.ds(line, rows), lanes], target)
            pl.when(other == 0)(copy.start)
            line = pl.multiple_of((4 * core + x) * lines + 2 * HALO, HALO)
            source = swapped.at[pl.ds(line, rows), lanes]
            copy = pltpu.make_async_copy(source, target, sem.at[len(copies) - 1])
            pl.when(other == 1)(copy.start)
        at += n
    return copies


def project_kernel(sizes, early, late, *refs):
    rows, depth, width, modes, seq = sizes
    pos, near, swapped, *pieces = refs[:-7]
    sums, late_tok, tokv, wv, tok_sem, late_sem, w_sem = refs[-7:]
    copies, at = [], 0
    for number, piece in enumerate(pieces):
        n = piece.shape[0]
        copies.append(pltpu.make_async_copy(piece, wv.at[pl.ds(at, n), :], w_sem.at[number]))
        copies[-1].start()
        at += n
    copies += token_copies(sizes, pos, near, swapped, early, tokv, tok_sem)
    late_copies = token_copies(sizes, pos, near, swapped, late, late_tok, late_sem)
    for copy in copies:
        copy.wait()

    @pl.loop(0, 3)
    def _(j):
        cols = pl.ds(pl.multiple_of(j * width, width), width)
        part = jnp.dot(tokv[...], wv[:, cols], preferred_element_type=F32)
        for lh in range(width // 128):
            sums[j * (width // 128) + lh] = part[:, lh * 128 : lh * 128 + 128]

    for copy in late_copies:
        copy.wait()


def late_products(sizes, signals, late_tok, pieces, sums, acc):
    rows, depth, width, modes, seq = sizes
    k = depth // 16
    first, last = signals
    halves = width // 128

    @pl.loop(first, last)
    def _(j):
        cols = pl.ds(pl.multiple_of(j * width, width), width)
        part = sum(
            jnp.dot(late_tok[:, i * k : i * k + k], piece[:, cols], preferred_element_type=F32)
            for i, piece in enumerate(pieces)
        )
        for lh in range(halves):
            new = part[:, lh * 128 : lh * 128 + 128]
            acc[(j - first) * halves + lh] = (sums[j * halves + lh] + new).astype(BF16).astype(F32)


def filtered(sizes, signals, lh, acc, taps, mine):
    rows, depth, width, modes, seq = sizes
    steps = 2 * rows // SUB
    halves = width // 128
    count = signals[1] - signals[0]
    weights = [[taps[lag, j : j + 1, mine] for j in range(*signals)] for lag in range(3)]

    def read(start):
        return [acc[j * halves + lh, pl.ds(start, SUB, stride=steps), :] for j in range(count)]

    def features(now, last, before):
        return [
            weights[0][j] * now[j] + weights[1][j] * last[j] + weights[2][j] * before[j]
            for j in range(count)
        ]

    return read, features


def state_kernel(sizes, *refs):
    rows, depth, width, modes, seq = sizes
    pos, late_tok, *pieces = refs[:-8]
    sums, taps, decay, product, gated, states_out, acc, state = refs[-8:]
    c = pos[3]
    late_products(sizes, (0, 1), late_tok, pieces, sums, gated)
    late_products(sizes, (1, 3), late_tok, pieces, sums, acc)
    steps = 2 * rows // SUB
    for lh in range(width // 128):
        mine = pl.ds(pl.multiple_of(c * width + lh * 128, 128), 128)
        lanes = pl.ds(lh * 128, 128)
        read, features = filtered(sizes, (1, 3), lh, acc, taps, mine)
        rates = [jnp.broadcast_to(decay[m : m + 1, mine] / seq, (SUB, 128)) for m in range(modes)]
        factors = [jnp.exp(-rate) for rate in rates]

        def step(t, carry):
            before, last, states = carry
            now = read(HALO + t)
            f = features(now, last, before)
            p = f[0] * f[1]
            product[t, :, lanes] = p
            return last, now, [a * s + p for a, s in zip(factors, states)]

        zero = jnp.zeros((SUB, 128), F32)
        carry = (read(HALO - 2), read(HALO - 1), [zero] * modes)
        states = lax.fori_loop(0, steps, step, carry, unroll=8)[2]
        line = lax.broadcasted_iota(jnp.int32, (SUB, 128), 0).astype(F32)
        left = (SUB - 1.0 - line) * float(steps)
        for m in range(modes):
            total = jnp.sum(jnp.exp(-rates[m] * left) * states[m], axis=0, keepdims=True)
            state[m : m + 1, lanes] = total
    sent = state[...].astype(BF16)
    for r in range(16):
        states_out[r] = sent


def local_kernel(sizes, pos, gated, taps, product, gain, decay, skip, gate, local, inside):
    rows, depth, width, modes, seq = sizes
    c = pos[3]
    steps = 2 * rows // SUB
    for lh in range(width // 128):
        mine = pl.ds(pl.multiple_of(c * width + lh * 128, 128), 128)
        lanes = pl.ds(lh * 128, 128)
        read, features = filtered(sizes, (0, 1), lh, gated, taps, mine)
        rates = [jnp.broadcast_to(decay[m : m + 1, mine] / seq, (SUB, 128)) for m in range(modes)]
        factors = [jnp.exp(-rate) for rate in rates]
        heights = [gain[m : m + 1, mine] * jnp.sqrt(2.0 * rates[m]) for m in range(modes)]
        direct = jnp.broadcast_to(skip[:, mine], (SUB, 128))

        def gates(t, carry):
            before, last = carry
            now = read(HALO + t)
            gate[t, :, lanes] = features(now, last, before)[0]
            return last, now

        lax.fori_loop(0, steps, gates, (read(HALO - 2), read(HALO - 1)), unroll=8)

        def step(t, states):
            p = product[t, :, lanes]
            states = [a * s + p for a, s in zip(factors, states)]
            parts = [w * s for w, s in zip(heights, states)]
            while len(parts) > 1:
                parts = [a + b for a, b in zip(parts[::2], parts[1::2])]
            local[t, :, lanes] = parts[0] + direct * p
            return states

        states = lax.fori_loop(0, steps, step, [jnp.zeros((SUB, 128), F32)] * modes, unroll=4)
        line = lax.broadcasted_iota(jnp.int32, (SUB, 128), 0)

        def later(value, by):
            return jnp.where(line >= by, pltpu.roll(value, by, 0), 0.0)

        for m in range(modes):
            s = states[m]
            for by in (1, 2, 4):
                s = s + jnp.exp(-float(steps * by) * rates[m]) * later(s, by)
            inside[m, :, lanes] = later(s, 1)


def finish_kernel(sizes, pos, gate, local, inside, states, gain, decay, mine_out, their_out, start, whole):
    rows, depth, width, modes, seq = sizes
    rank, c = pos[0], pos[3]
    steps = 2 * rows // SUB
    length = 2 * rows
    for lh in range(width // 128):
        mine = pl.ds(pl.multiple_of(c * width + lh * 128, 128), 128)
        lanes = pl.ds(lh * 128, 128)
        over = jnp.exp(-float(length) * (decay[:, mine] / seq))
        entering = jnp.zeros((modes, 128), F32)
        for r in range(16):
            entering = jnp.where(r < rank, over * entering + states[r, :, lanes].astype(F32), entering)
        start[:, lanes] = entering
        line = lax.broadcasted_iota(jnp.int32, (SUB, 128), 0).astype(F32) * float(steps)
        factors, waves = [], []
        for m in range(modes):
            rate = jnp.broadcast_to(decay[m : m + 1, mine] / seq, (SUB, 128))
            factors.append(jnp.exp(-rate))
            height = gain[m : m + 1, mine] * jnp.sqrt(2.0 * rate)
            waves.append(height * (inside[m, :, lanes] + jnp.exp(-rate * line) * start[m : m + 1, lanes]))

        def step(t, waves):
            waves = [a * z for a, z in zip(factors, waves)]
            parts = waves
            while len(parts) > 1:
                parts = [a + b for a, b in zip(parts[::2], parts[1::2])]
            whole[lh, pl.ds(t, SUB, stride=steps), :] = gate[t, :, lanes] * (local[t, :, lanes] + parts[0])
            return waves

        lax.fori_loop(0, steps, step, waves, unroll=4)
        for out, core in ((mine_out, c), (their_out, 1 - c)):
            line = pl.ds(pl.multiple_of(core * rows, rows), rows)
            out[:, lanes] = whole[lh, line, :].astype(BF16)


def body(tokens, w_in, taps, modes_gain, decay, skip):
    rows = tokens.shape[0]
    group = w_in.shape[2]
    width = group // 2
    k = w_in.shape[0]
    modes = decay.shape[0]
    depth = tokens.shape[1] * 8
    seq = rows * 32
    sizes = (rows, depth, width, modes, seq)
    y, h, c = (lax.axis_index(a) for a in CTX)
    pos = jnp.stack([y * 4 + h, y, h, c, lax.axis_index("l")]).astype(jnp.int32)

    tie = lax.optimization_barrier
    with jax.named_scope("weight_gather"):
        halves = w_in.reshape(k, 3, 2, width).transpose(2, 0, 1, 3).reshape(2, k, 3 * width)
        mine = lax.dynamic_index_in_dim(halves, c, 0, keepdims=False)
        theirs = lax.ppermute(lax.dynamic_index_in_dim(halves, 1 - c, 0, keepdims=False), "c", SWAP)
        own = in_order(c == 0, mine, theirs, 0)
    with jax.named_scope("token_swap"):
        other = lax.ppermute(tokens, "l", SWAP)
    with jax.named_scope("weight_rings"):
        farther = shifted(own, "y", 2)
        far = both_ways(own, "y")
        beside = both_ways(own, "h")
        other, far = tie((other, far))
        tails = jnp.concatenate([tokens[rows - HALO :], other[rows - HALO :]], 0)
        halos = lax.ppermute(tails, CTX, [(i, i + 1) for i in range(1, 31, 2)])
    first = (halos, other, farther, far, beside)
    halos, other, farther, far, beside = tie(first)
    with jax.named_scope("token_gather"):
        near = lax.all_gather(tokens, ("c", "x"), axis=0, tiled=True)
        wide = jnp.concatenate([halos, other], 0)
        swapped = lax.all_gather(wide, ("c", "x"), axis=0, tiled=True)
    with jax.named_scope("weight_rings"):
        two, half = 2 * k, k
        moves = [(0, 0, two, 0, 0), (1, 0, two, 0, two), (0, 0, half, 1, 0), (1, half, half, 2, 0)]
        pair, low, high = relayed(beside, moves, "relay_pair")
        far_pair = both_ways(pair, "y")
        opposite = shifted(low, "h", 1), shifted(high, "h", -1)
        far_pair, opposite = tie((far_pair, opposite))
        moves = [(0, 0, two, 0, 0), (1, two, two, 1, 0)]
        moves += [(side, 0, half, 2, side * half) for side in range(2)]
        moves += [(side, two + half, half, 3, side * half) for side in range(2)]
        moves += [(2 + side, 0, half, 4, side * half) for side in range(2)]
        behind, ahead, firsts, seconds, opposite = relayed([*far_pair, *opposite], moves, "relay_far")
        last = shifted(opposite, "y", 2)
        farther_pair = shifted(behind, "y", 1), shifted(ahead, "y", -1)
        far_opposite = shifted(firsts, "h", 1), shifted(seconds, "h", -1)

    early = [own, pair, opposite]
    early_runs = [(0, dh, 0, two) for dh in (0, 1, -1, 2)]
    for side, dy in enumerate((1, -1)):
        early += [far[side], far_pair[side]]
        early_runs += [(dy, dh, 0, two) for dh in (0, 1, -1)]
    early += [farther]
    early_runs += [(2, 0, 0, two)]
    late = [*farther_pair, last, *far_opposite]
    late_runs = [(2, 1, 0, two), (2, -1, 0, two), (2, 2, 0, two)]
    late_runs += [(dy, 2, skip, half) for skip in (0, half) for dy in (1, -1)]

    vmem = pl.BlockSpec(memory_space=pltpu.VMEM)
    smem = pl.BlockSpec(memory_space=pltpu.SMEM)
    hbm = pl.BlockSpec(memory_space=pltpu.HBM)
    block = (2 * rows // SUB, SUB, width)
    full = jax.ShapeDtypeStruct(block, F32)
    lines = 2 * rows + HALO
    chunks = (3 * width // 128, lines, 128)

    def dma(n):
        return pltpu.SemaphoreType.DMA((n,))

    sums, late_tok = pl.pallas_call(
        functools.partial(project_kernel, sizes, early_runs, late_runs),
        out_shape=(
            jax.ShapeDtypeStruct(chunks, F32),
            jax.ShapeDtypeStruct((lines, 5 * two), BF16),
        ),
        in_specs=[smem] + [hbm] * (2 + len(early)),
        out_specs=(vmem, vmem),
        scratch_shapes=[
            pltpu.VMEM((lines, 11 * two), BF16),
            pltpu.VMEM((11 * two, 3 * width), BF16),
            dma(3 * len(early_runs)),
            dma(3 * len(late_runs)),
            dma(len(early)),
        ],
        compiler_params=pltpu.CompilerParams(vmem_limit_bytes=14 * 2**20),
        cost_estimate=pl.CostEstimate(
            flops=2 * lines * 11 * two * 3 * width, bytes_accessed=9_000_000, transcendentals=0
        ),
        name="project",
    )(pos, near, swapped, *early)
    params = pltpu.CompilerParams(vmem_limit_bytes=8 * 2**20)
    product, gated, state = pl.pallas_call(
        functools.partial(state_kernel, sizes),
        out_shape=(
            full,
            jax.ShapeDtypeStruct((width // 128, lines, 128), F32),
            jax.ShapeDtypeStruct((16, modes, width), BF16),
        ),
        in_specs=[smem] + [vmem] * (4 + len(late)),
        out_specs=(vmem,) * 3,
        scratch_shapes=[
            pltpu.VMEM((2 * width // 128, lines, 128), F32),
            pltpu.VMEM((modes, width), F32),
        ],
        compiler_params=params,
        name="states",
    )(pos, late_tok, *late, sums, taps, decay)

    with jax.named_scope("state_exchange"):
        states = lax.all_to_all(state, ("y", "h"), 0, 0, tiled=True)
    gate, local, inside = pl.pallas_call(
        functools.partial(local_kernel, sizes),
        out_shape=(full, full, jax.ShapeDtypeStruct((modes, SUB, width), F32)),
        in_specs=[smem] + [vmem] * 6,
        out_specs=(vmem,) * 3,
        compiler_params=params,
        cost_estimate=pl.CostEstimate(
            flops=30_000_000, bytes_accessed=2_000_000, transcendentals=0
        ),
        name="local",
    )(pos, gated, taps, product, modes_gain, decay, skip.reshape(1, group))
    mine, theirs = pl.pallas_call(
        functools.partial(finish_kernel, sizes),
        out_shape=(jax.ShapeDtypeStruct((rows, width), BF16),) * 2,
        in_specs=[smem] + [vmem] * 6,
        out_specs=(vmem, vmem),
        scratch_shapes=[pltpu.VMEM((modes, width), F32), pltpu.VMEM((width // 128, 2 * rows, 128), F32)],
        compiler_params=params,
        name="finish",
    )(pos, gate, local, inside, states, modes_gain, decay)
    with jax.named_scope("result_swap"):
        return in_order(c == 0, mine, lax.ppermute(theirs, "c", SWAP), 1)


def solution(mesh):
    split = Mesh(mesh.devices.reshape(4, 4, 2, 2, 4), AXES)
    return jax.shard_map(
        body,
        mesh=split,
        in_specs=(
            P(CTX, CH),
            P(CTX, None, CH),
            P(None, None, CH),
            P(None, CH),
            P(None, CH),
            P(CH),
        ),
        out_specs=P(CTX, CH),
        check_vma=False,
    )
```

```python
import functools

import jax
import jax.numpy as jnp
from jax import lax
from jax.experimental import pallas as pl
from jax.experimental.pallas import tpu as pltpu
from jax.sharding import Mesh
from jax.sharding import PartitionSpec as P

AXES = ("y", "h", "c", "l", "x")
CTX = ("y", "h", "c")
CH = ("l", "x")
F32 = jnp.float32
BF16 = jnp.bfloat16
HALO = 16
SWAP = [(0, 1), (1, 0)]
SUB = 8


def shifted(array, axis, step):
    n = lax.axis_size(axis)
    return lax.ppermute(array, axis, [(i, (i + step) % n) for i in range(n)])


def in_order(mine_first, mine, theirs, axis):
    first, second = jnp.where(mine_first, mine, theirs), jnp.where(mine_first, theirs, mine)
    return jnp.concatenate([first, second], axis)


def both_ways(piece, axis):
    return shifted(piece, axis, 1), shifted(piece, axis, -1)


def relay_kernel(moves, count, *refs):
    sources, targets, sem = refs[:count], refs[count:-1], refs[-1]
    copies = []
    for number, (source, first, n, target, at) in enumerate(moves):
        copies.append(
            pltpu.make_async_copy(
                sources[source].at[pl.ds(first, n), :],
                targets[target].at[pl.ds(at, n), :],
                sem.at[number],
            )
        )
        copies[-1].start()
    for copy in copies:
        copy.wait()


def relayed(sources, moves, name):
    heights = [max(at + n for _, _, n, target, at in moves if target == t) for t in range(1 + max(m[3] for m in moves))]
    anywhere = pl.BlockSpec(memory_space=pl.ANY)
    return pl.pallas_call(
        functools.partial(relay_kernel, moves, len(sources)),
        out_shape=[jax.ShapeDtypeStruct((h, sources[0].shape[1]), sources[0].dtype) for h in heights],
        in_specs=[anywhere] * len(sources),
        out_specs=[anywhere] * len(heights),
        scratch_shapes=[pltpu.SemaphoreType.DMA((len(moves),))],
        cost_estimate=pl.CostEstimate(flops=0, bytes_accessed=2_000_000, transcendentals=0),
        compiler_params=pltpu.CompilerParams(vmem_limit_bytes=2**20),
        name=name,
    )(*sources)


def token_copies(sizes, pos, near, swapped, runs, tokv, sem):
    rows, depth, width, modes, seq = sizes
    k = depth // 16
    lines = rows + 2 * HALO
    copies, at = [], 0

    def add(source, target):
        copies.append(pltpu.make_async_copy(source, target, sem.at[len(copies)]))
        return copies[-1]

    for dy, dh, skip, n in runs:
        ys, hs = lax.rem(pos[1] - dy + 4, 4), lax.rem(pos[2] - dh + 4, 4)
        ch = 2 * ys + lax.div(hs, 2)
        lanes = pl.ds(pl.multiple_of(lax.rem(hs, 2) * k + skip, 128), n)
        x = lax.rem(ch, 4)
        other = lax.rem(lax.div(ch, 4) + pos[4], 2)
        to = pl.ds(at, n)
        line = pl.multiple_of(x * lines + HALO * other, HALO)
        add(swapped.at[pl.ds(line, HALO), lanes], tokv.at[pl.ds(0, HALO), to]).start()
        for core in range(2):
            target = tokv.at[pl.ds(HALO + core * rows, rows), to]
            line = pl.multiple_of((4 * core + x) * rows, rows)
            copy = add(near.at[pl.ds(line, rows), lanes], target)
            pl.when(other == 0)(copy.start)
            line = pl.multiple_of((4 * core + x) * lines + 2 * HALO, HALO)
            source = swapped.at[pl.ds(line, rows), lanes]
            copy = pltpu.make_async_copy(source, target, sem.at[len(copies) - 1])
            pl.when(other == 1)(copy.start)
        at += n
    return copies


def project_kernel(sizes, early, late, *refs):
    rows, depth, width, modes, seq = sizes
    pos, near, swapped, *pieces = refs[:-7]
    sums, late_tok, tokv, wv, tok_sem, late_sem, w_sem = refs[-7:]
    copies, at = [], 0
    for number, piece in enumerate(pieces):
        n = piece.shape[0]
        copies.append(pltpu.make_async_copy(piece, wv.at[pl.ds(at, n), :], w_sem.at[number]))
        copies[-1].start()
        at += n
    copies += token_copies(sizes, pos, near, swapped, early, tokv, tok_sem)
    late_copies = token_copies(sizes, pos, near, swapped, late, late_tok, late_sem)
    for copy in copies:
        copy.wait()

    @pl.loop(0, 3)
    def _(j):
        cols = pl.ds(pl.multiple_of(j * width, width), width)
        part = jnp.dot(tokv[...], wv[:, cols], preferred_element_type=F32)
        for lh in range(width // 128):
            sums[j * (width // 128) + lh] = part[:, lh * 128 : lh * 128 + 128]

    for copy in late_copies:
        copy.wait()


def late_products(sizes, signals, late_tok, pieces, sums, acc):
    rows, depth, width, modes, seq = sizes
    k = depth // 16
    first, last = signals
    halves = width // 128

    @pl.loop(first, last)
    def _(j):
        cols = pl.ds(pl.multiple_of(j * width, width), width)
        part = sum(
            jnp.dot(late_tok[:, i * k : i * k + k], piece[:, cols], preferred_element_type=F32)
            for i, piece in enumerate(pieces)
        )
        for lh in range(halves):
            new = part[:, lh * 128 : lh * 128 + 128]
            acc[(j - first) * halves + lh] = (sums[j * halves + lh] + new).astype(BF16).astype(F32)


def filtered(sizes, signals, lh, acc, taps, mine):
    rows, depth, width, modes, seq = sizes
    steps = 2 * rows // SUB
    halves = width // 128
    count = signals[1] - signals[0]
    weights = [[taps[lag, j : j + 1, mine] for j in range(*signals)] for lag in range(3)]

    def read(start):
        return [acc[j * halves + lh, pl.ds(start, SUB, stride=steps), :] for j in range(count)]

    def features(now, last, before):
        return [
            weights[0][j] * now[j] + weights[1][j] * last[j] + weights[2][j] * before[j]
            for j in range(count)
        ]

    return read, features


def state_kernel(sizes, *refs):
    rows, depth, width, modes, seq = sizes
    pos, late_tok, *pieces = refs[:-8]
    sums, taps, decay, product, gated, states_out, acc, state = refs[-8:]
    c = pos[3]
    late_products(sizes, (0, 1), late_tok, pieces, sums, gated)
    late_products(sizes, (1, 3), late_tok, pieces, sums, acc)
    steps = 2 * rows // SUB
    for lh in range(width // 128):
        mine = pl.ds(pl.multiple_of(c * width + lh * 128, 128), 128)
        lanes = pl.ds(lh * 128, 128)
        read, features = filtered(sizes, (1, 3), lh, acc, taps, mine)
        rates = [jnp.broadcast_to(decay[m : m + 1, mine] / seq, (SUB, 128)) for m in range(modes)]
        factors = [jnp.exp(-rate) for rate in rates]

        def step(t, carry):
            before, last, states = carry
            now = read(HALO + t)
            f = features(now, last, before)
            p = f[0] * f[1]
            product[t, :, lanes] = p
            return last, now, [a * s + p for a, s in zip(factors, states)]

        zero = jnp.zeros((SUB, 128), F32)
        carry = (read(HALO - 2), read(HALO - 1), [zero] * modes)
        states = lax.fori_loop(0, steps, step, carry, unroll=8)[2]
        line = lax.broadcasted_iota(jnp.int32, (SUB, 128), 0).astype(F32)
        left = (SUB - 1.0 - line) * float(steps)
        for m in range(modes):
            total = jnp.sum(jnp.exp(-rates[m] * left) * states[m], axis=0, keepdims=True)
            state[m : m + 1, lanes] = total
    sent = state[...].astype(BF16)
    for r in range(16):
        states_out[r] = sent


def local_kernel(sizes, pos, gated, taps, product, gain, decay, skip, gate, local, inside):
    rows, depth, width, modes, seq = sizes
    c = pos[3]
    steps = 2 * rows // SUB
    for lh in range(width // 128):
        mine = pl.ds(pl.multiple_of(c * width + lh * 128, 128), 128)
        lanes = pl.ds(lh * 128, 128)
        read, features = filtered(sizes, (0, 1), lh, gated, taps, mine)
        rates = [jnp.broadcast_to(decay[m : m + 1, mine] / seq, (SUB, 128)) for m in range(modes)]
        factors = [jnp.exp(-rate) for rate in rates]
        heights = [gain[m : m + 1, mine] * jnp.sqrt(2.0 * rates[m]) for m in range(modes)]
        direct = jnp.broadcast_to(skip[:, mine], (SUB, 128))

        def gates(t, carry):
            before, last = carry
            now = read(HALO + t)
            gate[t, :, lanes] = features(now, last, before)[0]
            return last, now

        lax.fori_loop(0, steps, gates, (read(HALO - 2), read(HALO - 1)), unroll=8)

        def step(t, states):
            p = product[t, :, lanes]
            states = [a * s + p for a, s in zip(factors, states)]
            parts = [w * s for w, s in zip(heights, states)]
            while len(parts) > 1:
                parts = [a + b for a, b in zip(parts[::2], parts[1::2])]
            local[t, :, lanes] = parts[0] + direct * p
            return states

        states = lax.fori_loop(0, steps, step, [jnp.zeros((SUB, 128), F32)] * modes, unroll=4)
        line = lax.broadcasted_iota(jnp.int32, (SUB, 128), 0)

        def later(value, by):
            return jnp.where(line >= by, pltpu.roll(value, by, 0), 0.0)

        for m in range(modes):
            s = states[m]
            for by in (1, 2, 4):
                s = s + jnp.exp(-float(steps * by) * rates[m]) * later(s, by)
            inside[m, :, lanes] = later(s, 1)


def finish_kernel(sizes, pos, gate, local, inside, states, gain, decay, mine_out, their_out, start, whole):
    rows, depth, width, modes, seq = sizes
    rank, c = pos[0], pos[3]
    steps = 2 * rows // SUB
    length = 2 * rows
    for lh in range(width // 128):
        mine = pl.ds(pl.multiple_of(c * width + lh * 128, 128), 128)
        lanes = pl.ds(lh * 128, 128)
        over = jnp.exp(-float(length) * (decay[:, mine] / seq))
        entering = jnp.zeros((modes, 128), F32)
        for r in range(16):
            entering = jnp.where(r < rank, over * entering + states[r, :, lanes].astype(F32), entering)
        start[:, lanes] = entering
        line = lax.broadcasted_iota(jnp.int32, (SUB, 128), 0).astype(F32) * float(steps)
        factors, waves = [], []
        for m in range(modes):
            rate = jnp.broadcast_to(decay[m : m + 1, mine] / seq, (SUB, 128))
            factors.append(jnp.exp(-rate))
            height = gain[m : m + 1, mine] * jnp.sqrt(2.0 * rate)
            waves.append(height * (inside[m, :, lanes] + jnp.exp(-rate * line) * start[m : m + 1, lanes]))

        def step(t, waves):
            waves = [a * z for a, z in zip(factors, waves)]
            parts = waves
            while len(parts) > 1:
                parts = [a + b for a, b in zip(parts[::2], parts[1::2])]
            whole[lh, pl.ds(t, SUB, stride=steps), :] = gate[t, :, lanes] * (local[t, :, lanes] + parts[0])
            return waves

        lax.fori_loop(0, steps, step, waves, unroll=4)
        for out, core in ((mine_out, c), (their_out, 1 - c)):
            line = pl.ds(pl.multiple_of(core * rows, rows), rows)
            out[:, lanes] = whole[lh, line, :].astype(BF16)


def body(tokens, w_in, taps, modes_gain, decay, skip):
    rows = tokens.shape[0]
    group = w_in.shape[2]
    width = group // 2
    k = w_in.shape[0]
    modes = decay.shape[0]
    depth = tokens.shape[1] * 8
    seq = rows * 32
    sizes = (rows, depth, width, modes, seq)
    y, h, c = (lax.axis_index(a) for a in CTX)
    pos = jnp.stack([y * 4 + h, y, h, c, lax.axis_index("l")]).astype(jnp.int32)

    tie = lax.optimization_barrier
    with jax.named_scope("weight_gather"):
        halves = w_in.reshape(k, 3, 2, width).transpose(2, 0, 1, 3).reshape(2, k, 3 * width)
        mine = lax.dynamic_index_in_dim(halves, c, 0, keepdims=False)
        theirs = lax.ppermute(lax.dynamic_index_in_dim(halves, 1 - c, 0, keepdims=False), "c", SWAP)
        own = in_order(c == 0, mine, theirs, 0)
    with jax.named_scope("token_swap"):
        other = lax.ppermute(tokens, "l", SWAP)
    with jax.named_scope("weight_rings"):
        farther = shifted(own, "y", 2)
        far = both_ways(own, "y")
        beside = both_ways(own, "h")
        other, farther = tie((other, farther))
        tails = jnp.concatenate([tokens[rows - HALO :], other[rows - HALO :]], 0)
        halos = lax.ppermute(tails, CTX, [(i, i + 1) for i in range(1, 31, 2)])
    first = (halos, other, farther, far, beside)
    halos, other, farther, far, beside = tie(first)
    with jax.named_scope("token_gather"):
        near = lax.all_gather(tokens, ("c", "x"), axis=0, tiled=True)
        wide = jnp.concatenate([halos, other], 0)
        swapped = lax.all_gather(wide, ("c", "x"), axis=0, tiled=True)
    with jax.named_scope("weight_rings"):
        two, half = 2 * k, k
        moves = [(0, 0, two, 0, 0), (1, 0, two, 0, two), (0, 0, half, 1, 0), (1, half, half, 2, 0)]
        pair, low, high = relayed(beside, moves, "relay_pair")
        far_pair = both_ways(pair, "y")
        opposite = shifted(low, "h", 1), shifted(high, "h", -1)
        far_pair, opposite = tie((far_pair, opposite))
        moves = [(0, 0, two, 0, 0), (1, two, two, 1, 0)]
        moves += [(side, 0, half, 2, side * half) for side in range(2)]
        moves += [(side, two + half, half, 3, side * half) for side in range(2)]
        moves += [(2 + side, 0, half, 4, side * half) for side in range(2)]
        behind, ahead, firsts, seconds, opposite = relayed([*far_pair, *opposite], moves, "relay_far")
        last = shifted(opposite, "y", 2)
        farther_pair = shifted(behind, "y", 1), shifted(ahead, "y", -1)
        far_opposite = shifted(firsts, "h", 1), shifted(seconds, "h", -1)

    early = [own, pair, opposite]
    early_runs = [(0, dh, 0, two) for dh in (0, 1, -1, 2)]
    for side, dy in enumerate((1, -1)):
        early += [far[side], far_pair[side]]
        early_runs += [(dy, dh, 0, two) for dh in (0, 1, -1)]
    early += [farther]
    early_runs += [(2, 0, 0, two)]
    late = [*farther_pair, *far_opposite, last]
    late_runs = [(2, 1, 0, two), (2, -1, 0, two)]
    late_runs += [(dy, 2, skip, half) for skip in (0, half) for dy in (1, -1)]
    late_runs += [(2, 2, 0, two)]

    vmem = pl.BlockSpec(memory_space=pltpu.VMEM)
    smem = pl.BlockSpec(memory_space=pltpu.SMEM)
    hbm = pl.BlockSpec(memory_space=pltpu.HBM)
    block = (2 * rows // SUB, SUB, width)
    full = jax.ShapeDtypeStruct(block, F32)
    lines = 2 * rows + HALO
    chunks = (3 * width // 128, lines, 128)

    def dma(n):
        return pltpu.SemaphoreType.DMA((n,))

    sums, late_tok = pl.pallas_call(
        functools.partial(project_kernel, sizes, early_runs, late_runs),
        out_shape=(
            jax.ShapeDtypeStruct(chunks, F32),
            jax.ShapeDtypeStruct((lines, 5 * two), BF16),
        ),
        in_specs=[smem] + [hbm] * (2 + len(early)),
        out_specs=(vmem, vmem),
        scratch_shapes=[
            pltpu.VMEM((lines, 11 * two), BF16),
            pltpu.VMEM((11 * two, 3 * width), BF16),
            dma(3 * len(early_runs)),
            dma(3 * len(late_runs)),
            dma(len(early)),
        ],
        compiler_params=pltpu.CompilerParams(vmem_limit_bytes=14 * 2**20),
        cost_estimate=pl.CostEstimate(
            flops=2 * lines * 11 * two * 3 * width, bytes_accessed=9_000_000, transcendentals=0
        ),
        name="project",
    )(pos, near, swapped, *early)
    params = pltpu.CompilerParams(vmem_limit_bytes=8 * 2**20)
    product, gated, state = pl.pallas_call(
        functools.partial(state_kernel, sizes),
        out_shape=(
            full,
            jax.ShapeDtypeStruct((width // 128, lines, 128), F32),
            jax.ShapeDtypeStruct((16, modes, width), BF16),
        ),
        in_specs=[smem] + [vmem] * (4 + len(late)),
        out_specs=(vmem,) * 3,
        scratch_shapes=[
            pltpu.VMEM((2 * width // 128, lines, 128), F32),
            pltpu.VMEM((modes, width), F32),
        ],
        compiler_params=params,
        name="states",
    )(pos, late_tok, *late, sums, taps, decay)

    with jax.named_scope("state_exchange"):
        states = lax.all_to_all(state, ("y", "h"), 0, 0, tiled=True)
    gate, local, inside = pl.pallas_call(
        functools.partial(local_kernel, sizes),
        out_shape=(full, full, jax.ShapeDtypeStruct((modes, SUB, width), F32)),
        in_specs=[smem] + [vmem] * 6,
        out_specs=(vmem,) * 3,
        compiler_params=params,
        cost_estimate=pl.CostEstimate(
            flops=30_000_000, bytes_accessed=2_000_000, transcendentals=0
        ),
        name="local",
    )(pos, gated, taps, product, modes_gain, decay, skip.reshape(1, group))
    mine, theirs = pl.pallas_call(
        functools.partial(finish_kernel, sizes),
        out_shape=(jax.ShapeDtypeStruct((rows, width), BF16),) * 2,
        in_specs=[smem] + [vmem] * 6,
        out_specs=(vmem, vmem),
        scratch_shapes=[pltpu.VMEM((modes, width), F32), pltpu.VMEM((width // 128, 2 * rows, 128), F32)],
        compiler_params=params,
        name="finish",
    )(pos, gate, local, inside, states, modes_gain, decay)
    with jax.named_scope("result_swap"):
        return in_order(c == 0, mine, lax.ppermute(theirs, "c", SWAP), 1)


def solution(mesh):
    split = Mesh(mesh.devices.reshape(4, 4, 2, 2, 4), AXES)
    return jax.shard_map(
        body,
        mesh=split,
        in_specs=(
            P(CTX, CH),
            P(CTX, None, CH),
            P(None, None, CH),
            P(None, CH),
            P(None, CH),
            P(CH),
        ),
        out_specs=P(CTX, CH),
        check_vma=False,
    )
```
